1024 devices in a mesh: gx: 8 (over y), gy: 4 (over x), gz: 32 (over z, core).
Axes of the slice: x: 4, y: 8, z: 16, core: 2. Of those that a mesh axis runs over, the one named last changes fastest.
Arguments:
- relative: float32 [19, 128, 32, 1024], P(None, 'gz', 'gy', 'gx'), may hold values from 0.7 to 1.3
- fluid: int32 [128, 32, 1024], P('gz', 'gy', 'gx'), may hold values from 0 to 1, as said below
- block_fluid: int32 [64, 4, 8], P('gz', 'gy', 'gx'), may hold values from 0 to 2048, as said below
- new_owner: int32 [64, 4, 8], P('gz', 'gy', 'gx'), may hold values from 0 to 31, as said below
Outputs:
- relative_out: float32 [19, 128, 32, 1024], P(None, 'gz', 'gy', 'gx')
- block_density: float32 [64, 4, 8], P('gz', 'gy', 'gx')
The draws below stay inside these ranges and needn't reach their ends.
Inputs may be any that keep to these rules, and one draw needn't show every extreme that they name: 1 marks fluid, 0 solid. `block_fluid`: the number of voxels of the block where fluid is 1. `new_owner`: a block only trades places across a boundary between gz neighbours: the last slot of one device with the first slot of the device above it, both entries of that pair naming the other device; every other entry names its own device.
All inputs are finite; a program needn't handle non-finite values.
Results may differ from the reference program's by a relative error of at most 0.00015.
Values sent between devices are 32-bit elements; how exact they have to be, the bound alone decides.
No kernel may reach another device: no remote copies, remote signals or barrier semaphores. Data moves between devices by JAX's collectives and lax.ppermute only.
A program may use at most 32 MiB of HBM per device.

```python
import jax
import jax.numpy as jnp

BZ = 2
BY = 8
BX = 128
BLK = 2
STEPS = 4
NBZ = 64
NBY = 4
NBX = 8
NZ = 128
NY = 32
NX = 1024


def rock_voxels(key):
    cell_draw = jax.random.randint(jax.random.fold_in(key, 11), (NZ, NY, NX), 0, 4)
    block_draw = jax.random.randint(jax.random.fold_in(key, 12), (NBZ, NBY, NBX), 0, 6)
    total_blocks = NBZ * NBY * NBX
    flat_kind = block_draw.reshape(-1)
    full_pick = jax.random.randint(jax.random.fold_in(key, 13), (), 0, total_blocks)
    solid_pick = (full_pick + 1 + jax.random.randint(jax.random.fold_in(key, 14), (), 0, total_blocks - 1)) % total_blocks
    flat_kind = flat_kind.at[full_pick].set(5).at[solid_pick].set(0)
    block_kind = flat_kind.reshape(NBZ, NBY, NBX)
    kind_cells = jnp.repeat(jnp.repeat(jnp.repeat(block_kind, BZ, axis=0), BY, axis=1), BX, axis=2)
    return (((cell_draw != 0) | (kind_cells == 5)) & (kind_cells != 0)).astype(jnp.int32)


def draw_fluid(key, part):
    return rock_voxels(key)


def draw_block_fluid(key, part):
    fluid_cells = rock_voxels(key)
    return fluid_cells.reshape(NBZ, BZ, NBY, BY, NBX, BX).sum(axis=(1, 3, 5)).astype(jnp.int32)


def draw_new_owner(key, part):
    key = jax.random.fold_in(key, 3)
    devices_z = NBZ // BLK
    swap_bits = jax.random.randint(key, (devices_z, NBY, NBX), 0, 2)
    boundary = jnp.arange(devices_z, dtype=jnp.int32)[:, None, None]
    swap_bits = jnp.where(boundary < devices_z - 1, swap_bits, 0)
    swap_below = jnp.concatenate([jnp.zeros_like(swap_bits[:1]), swap_bits[:-1]], axis=0)
    places = jnp.arange(NBZ, dtype=jnp.int32)
    owner_index = places // BLK
    slot_index = places % BLK
    going_up = jnp.where((slot_index == BLK - 1)[:, None, None], swap_bits[owner_index], 0)
    going_down = jnp.where((slot_index == 0)[:, None, None], swap_below[owner_index], 0)
    return (owner_index[:, None, None] + going_up - going_down).astype(jnp.int32)


def setup_inputs(seed: int = 0) -> dict:
    keys = jax.random.split(jax.random.key(seed), 5)
    return {
        "relative": jnp.clip(1.0 + 0.06 * jax.random.normal(keys[0], (19, NZ, NY, NX), jnp.float32), 0.7, 1.3),
        "fluid": draw_fluid(jax.random.fold_in(keys[4], 71), 0),
        "block_fluid": draw_block_fluid(jax.random.fold_in(keys[4], 71), 0),
        "new_owner": draw_new_owner(jax.random.fold_in(keys[4], 71), 0),
    }


VELOCITIES = [(0, 0, 0), (1, 0, 0), (-1, 0, 0), (0, 1, 0), (0, -1, 0), (0, 0, 1), (0, 0, -1),
              (1, 1, 0), (-1, -1, 0), (1, -1, 0), (-1, 1, 0), (1, 0, 1), (-1, 0, -1),
              (1, 0, -1), (-1, 0, 1), (0, 1, 1), (0, -1, -1), (0, 1, -1), (0, -1, 1)]
OPPOSITE = [0, 2, 1, 4, 3, 6, 5, 8, 7, 10, 9, 12, 11, 14, 13, 16, 15, 18, 17]
WEIGHTS = [1.0 / 3.0] + [1.0 / 18.0] * 6 + [1.0 / 36.0] * 12
OMEGA = 1.5


def collide(populations, fluid_flag):
    wet = fluid_flag[0] > 0.5
    density = jnp.sum(populations, axis=0)
    safe_density = jnp.where(wet, density, 1.0)
    speeds = []
    for axis_pick in range(3):
        moment = sum(VELOCITIES[index][axis_pick] * populations[index] for index in range(1, 19) if VELOCITIES[index][axis_pick] != 0)
        speeds.append(jnp.where(wet, moment / safe_density, 0.0))
    square = speeds[0] * speeds[0] + speeds[1] * speeds[1] + speeds[2] * speeds[2]
    relaxed = []
    for index in range(19):
        along = VELOCITIES[index][0] * speeds[0] + VELOCITIES[index][1] * speeds[1] + VELOCITIES[index][2] * speeds[2]
        balance = WEIGHTS[index] * density * (1.0 + 3.0 * along + 4.5 * along * along - 1.5 * square)
        relaxed.append(fluid_flag[0] * (populations[index] + OMEGA * (balance - populations[index])))
    return jnp.stack(relaxed)


def stream(relaxed_pad, fluid_pad):
    size_z = relaxed_pad.shape[1] - 2
    size_y = relaxed_pad.shape[2] - 2
    size_x = relaxed_pad.shape[3] - 2
    centre = fluid_pad[0, 1:1 + size_z, 1:1 + size_y, 1:1 + size_x]
    read = []
    for index in range(19):
        step_z, step_y, step_x = VELOCITIES[index]
        source = relaxed_pad[index, 1 - step_z:1 - step_z + size_z, 1 - step_y:1 - step_y + size_y, 1 - step_x:1 - step_x + size_x]
        open_side = fluid_pad[0, 1 - step_z:1 - step_z + size_z, 1 - step_y:1 - step_y + size_y, 1 - step_x:1 - step_x + size_x]
        bounce = relaxed_pad[OPPOSITE[index], 1:1 + size_z, 1:1 + size_y, 1:1 + size_x]
        read.append(centre * jnp.where(open_side > 0.5, source, bounce))
    return jnp.stack(read)


def spread_flag(flag):
    return jnp.repeat(jnp.repeat(flag, BY, axis=1), BX, axis=2)[None, :, None]


def reference(relative, fluid, block_fluid, new_owner):
    blocks = relative.reshape(19, NBZ, BZ, NY, NX)
    places = jnp.arange(NBZ, dtype=jnp.int32)
    owner_index = places // BLK
    slot_index = places % BLK
    take_low = (slot_index == 0)[:, None, None] & (new_owner == (owner_index - 1)[:, None, None])
    take_high = (slot_index == BLK - 1)[:, None, None] & (new_owner == (owner_index + 1)[:, None, None])
    from_lower = jnp.concatenate([jnp.zeros_like(blocks[:, :1]), blocks[:, :-1]], axis=1)
    from_upper = jnp.concatenate([blocks[:, 1:], jnp.zeros_like(blocks[:, :1])], axis=1)
    home = jnp.where(spread_flag(take_low), from_lower, jnp.where(spread_flag(take_high), from_upper, blocks))
    home = home.reshape(19, NZ, NY, NX)
    weights = jnp.array(WEIGHTS, jnp.float32).reshape(19, 1, 1, 1)
    fluid_flag = fluid.astype(jnp.float32)[None]
    populations = weights * home * fluid_flag
    fluid_pad = jnp.pad(fluid_flag, ((0, 0), (1, 1), (1, 1), (1, 1)))
    for sweep in range(STEPS):
        relaxed = collide(populations, fluid_flag)
        relaxed_pad = jnp.pad(relaxed, ((0, 0), (1, 1), (1, 1), (1, 1)))
        populations = stream(relaxed_pad, fluid_pad)
    relative_out = populations / weights
    density = jnp.sum(populations, axis=0)
    block_mass = density.reshape(NBZ, BZ, NBY, BY, NBX, BX).sum(axis=(1, 3, 5))
    block_density = block_mass / jnp.maximum(block_fluid, 1).astype(jnp.float32)
    return relative_out, block_density
```

```python
import functools

import jax
import jax.numpy as jnp
from jax import lax
from jax.experimental import pallas as pl
from jax.experimental.pallas import tpu as pltpu
from jax.sharding import PartitionSpec as P


VELOCITIES = [
    (0, 0, 0),
    (1, 0, 0),
    (-1, 0, 0),
    (0, 1, 0),
    (0, -1, 0),
    (0, 0, 1),
    (0, 0, -1),
    (1, 1, 0),
    (-1, -1, 0),
    (1, -1, 0),
    (-1, 1, 0),
    (1, 0, 1),
    (-1, 0, -1),
    (1, 0, -1),
    (-1, 0, 1),
    (0, 1, 1),
    (0, -1, -1),
    (0, 1, -1),
    (0, -1, 1),
]
OPPOSITE = [0, 2, 1, 4, 3, 6, 5, 8, 7, 10, 9, 12, 11, 14, 13, 16, 15, 18, 17]
Q = 19
UP_Y = [i for i in range(Q) if VELOCITIES[i][1] == 1]
DOWN_Y = [i for i in range(Q) if VELOCITIES[i][1] == -1]
SOLID = 3.0e38
F32 = jnp.float32
VMEM = pl.BlockSpec(memory_space=pltpu.VMEM)
SMEM = pl.BlockSpec(memory_space=pltpu.SMEM)
ANY = pl.BlockSpec(memory_space=pl.ANY)


def shape(*dims):
    return jax.ShapeDtypeStruct(dims, F32)


def lanes():
    return lax.broadcasted_iota(jnp.int32, (8, 128), 1)


def sublanes():
    return lax.broadcasted_iota(jnp.int32, (8, 128), 0)


def roll(value, sublane_shift, lane_shift):
    if sublane_shift % 8:
        value = pltpu.roll(value, sublane_shift % 8, 0)
    if lane_shift % 128:
        value = pltpu.roll(value, lane_shift % 128, 1)
    return value


def relax(g):
    sums = [g[k] + g[k + 1] for k in range(1, Q, 2)]
    diffs = [g[k] - g[k + 1] for k in range(1, Q, 2)]
    axis_sum = sums[0] + sums[1] + sums[2]
    edge_sum = (sums[3] + sums[4]) + (sums[5] + sums[6]) + (sums[7] + sums[8])
    density = 12.0 * g[0] + 2.0 * axis_sum + edge_sum
    moment_z = 2.0 * diffs[0] + ((diffs[3] + diffs[4]) + (diffs[5] + diffs[6]))
    moment_y = 2.0 * diffs[1] + ((diffs[3] - diffs[4]) + (diffs[7] + diffs[8]))
    moment_x = 2.0 * diffs[2] + ((diffs[5] - diffs[6]) + (diffs[7] - diffs[8]))
    inverse = 1.0 / density
    speed = [moment_z * inverse, moment_y * inverse, moment_x * inverse]
    square = speed[0] * speed[0] + speed[1] * speed[1] + speed[2] * speed[2]
    scaled = density * (1.5 / 36.0)
    base = scaled * (1.0 - 1.5 * square)
    linear = [(4.5 / 36.0) * m for m in (moment_z, moment_y, moment_x)]
    speed = [1.5 * s for s in speed]
    out = [base - 0.5 * g[0]]
    for pair in range(9):
        velocity = VELOCITIES[1 + 2 * pair]
        along = None
        twice = None
        for axis in range(3):
            if velocity[axis] == 0:
                continue
            if along is None:
                along, twice = linear[axis], speed[axis]
            elif velocity[axis] > 0:
                along, twice = along + linear[axis], twice + speed[axis]
            else:
                along, twice = along - linear[axis], twice - speed[axis]
        even = base + along * twice - 0.25 * sums[pair]
        odd = along - 0.25 * diffs[pair]
        out += [even + odd, even - odd]
    return out


def relax_wet(g, wet):
    return [jnp.where(wet, value, SOLID) for value in relax(g)]


def stream_row(ref, row, first):
    at = row - first
    out = [ref[0, at]]
    for i in range(1, Q):
        step_z, step_y, step_x = VELOCITIES[i]
        source = roll(ref[i, at - step_y], step_z, step_x)
        out.append(jnp.where(source == SOLID, ref[OPPOSITE[i], at], source))
    return out


def stream_patch(values):
    out = [values[0]]
    for i in range(1, Q):
        step_z, step_y, step_x = VELOCITIES[i]
        source = roll(values[i], step_z, 8 * step_y + step_x)
        out.append(jnp.where(source == SOLID, values[OPPOSITE[i]], source))
    return out


def over_rows(first, last, body):
    def step(row, carry):
        body(row)
        return carry

    lax.fori_loop(first, last, step, 0)


def gather_columns(values, rows):
    lane_row = lanes() // 8
    tile = jnp.full((8, 128), SOLID, F32)
    for row, value in zip(rows, values):
        tile = jnp.where(lane_row == row, roll(value, 0, 8 * row + 4), tile)
    return tile


def split_slabs(relative, fluid, low, high, sems):
    copies = [
        pltpu.make_async_copy(relative.at[:, 0:2], low.at[0:Q], sems.at[0]),
        pltpu.make_async_copy(relative.at[:, 2:4], high.at[0:Q], sems.at[1]),
    ]
    for copy in copies:
        copy.start()
    low[Q] = fluid[0:2].astype(F32)
    high[Q] = fluid[2:4].astype(F32)
    for copy in copies:
        copy.wait()


def first_relax(low, high, below, above, owner, own, y_low, y_high, turn):
    place = lax.axis_index("gz")
    swap_low = owner[0, 0, 0] == place - 1
    swap_high = owner[1, 0, 0] == place + 1
    kinds = [below[Q, 0], below[Q, 1], low[Q, 0], low[Q, 1], high[Q, 0], high[Q, 1], above[Q, 0], above[Q, 1]]
    for layer in range(8):
        turn[Q, 8 * layer : 8 * layer + 8] = kinds[layer]

    def home(i, carry):
        for k in range(2):
            mine, other = low[i, k], below[i, k]
            turn[i, 8 * k : 8 * k + 8] = jnp.where(swap_low, mine, other)
            turn[i, 8 * (k + 2) : 8 * (k + 3)] = jnp.where(swap_low, other, mine)
            mine, other = high[i, k], above[i, k]
            turn[i, 8 * (k + 4) : 8 * (k + 5)] = jnp.where(swap_high, other, mine)
            turn[i, 8 * (k + 6) : 8 * (k + 7)] = jnp.where(swap_high, mine, other)
        return carry

    lax.fori_loop(0, Q, home, 0)
    for row in range(8):
        wet = turn[Q, pl.ds(row, 8, stride=8)] > 0.5
        values = relax_wet([turn[i, pl.ds(row, 8, stride=8)] for i in range(Q)], wet)
        for i in range(Q):
            own[i, row] = values[i]
            if row < 3:
                y_low[3 * i + row] = values[i]
            if row > 4:
                y_high[3 * i + row - 5] = values[i]
        if row == 3:
            for k, i in enumerate(DOWN_Y):
                y_low[3 * Q + k] = values[i]
        if row == 4:
            for k, i in enumerate(UP_Y):
                y_high[3 * Q + k] = values[i]


def join_rows(own, below, above, main, edge):
    place = lax.axis_index("gy")
    at_low = place == 0
    at_high = place == lax.axis_size("gy") - 1
    for i in range(Q):
        rows = []
        if i in UP_Y:
            rows.append(jnp.where(at_low, SOLID, below[3 * Q + UP_Y.index(i)]))
        else:
            rows.append(jnp.full((8, 128), SOLID, F32))
        for k in range(3):
            rows.append(jnp.where(at_low, SOLID, below[3 * i + k]))
        for k in range(8):
            rows.append(own[i, k])
        for k in range(3):
            rows.append(jnp.where(at_high, SOLID, above[3 * i + k]))
        if i in DOWN_Y:
            rows.append(jnp.where(at_high, SOLID, above[3 * Q + DOWN_Y.index(i)]))
        else:
            rows.append(jnp.full((8, 128), SOLID, F32))
        for k in range(16):
            main[i, k] = rows[k]
        edge[i] = gather_columns(rows, range(16))


def two_steps(main, out, middle):
    def first(row):
        wet = main[0, row] != SOLID
        values = relax_wet(stream_row(main, row, 0), wet)
        for i in range(Q):
            middle[i, row - 1] = values[i]

    def second(row):
        wet = middle[0, row - 1] != SOLID
        values = relax_wet(stream_row(middle, row, 1), wet)
        for i in range(Q):
            out[i, row - 2] = values[i]

    over_rows(1, 15, first)
    over_rows(2, 14, second)


def patch_two_steps(inner, edge, left, right, main, below, above, halo):
    place = lax.axis_index("gx")
    at_low = place == 0
    at_high = place == lax.axis_size("gx") - 1
    low_side = lanes() % 8 < 4
    sides = []
    for side in range(2):
        values = []
        for i in range(Q):
            if side == 0:
                value = jnp.where(low_side, jnp.where(at_low, SOLID, left[i]), edge[i])
            else:
                value = jnp.where(low_side, edge[i], jnp.where(at_high, SOLID, right[i]))
            values.append(value)
        for step in range(2):
            wet = values[0] != SOLID
            values = relax_wet(stream_patch(values), wet)
        sides.append(values)
    lane = lanes()
    seam = (lane < 2) | (lane >= 126)
    sublane_pair = sublanes() // 2
    for i in range(Q):
        own_columns = jnp.where(low_side, sides[1][i], sides[0][i])
        halo[i] = jnp.where(low_side, sides[0][i], sides[1][i])
        for group in range(3):
            pack_low = None
            pack_high = None
            for k in range(4):
                row = 4 * group + k
                value = jnp.where(seam, roll(own_columns, 0, -(8 * (row + 2) + 4)), inner[i, row])
                main[i, row] = value
                to_low, to_high = roll(value, 2 * k - 2, 0), roll(value, 2 * k - 4, 0)
                if pack_low is None:
                    pack_low, pack_high = to_low, to_high
                else:
                    pack_low = jnp.where(sublane_pair == k, to_low, pack_low)
                    pack_high = jnp.where(sublane_pair == k, to_high, pack_high)
            below[3 * i + group] = pack_low
            above[3 * i + group] = pack_high
    for group in range(5):
        pack_low = None
        pack_high = None
        for k in range(4):
            value = halo[min(4 * group + k, Q - 1)]
            to_low, to_high = roll(value, 2 * k - 2, 0), roll(value, 2 * k - 4, 0)
            if pack_low is None:
                pack_low, pack_high = to_low, to_high
            else:
                pack_low = jnp.where(sublane_pair == k, to_low, pack_low)
                pack_high = jnp.where(sublane_pair == k, to_high, pack_high)
        below[3 * Q + group] = pack_low
        above[3 * Q + group] = pack_high


def last_two_steps(main, halo, below, above, block_fluid, out, block_density, joined, middle, turn):
    place = lax.axis_index("gz")
    at_low = place == 0
    at_high = place == lax.axis_size("gz") - 1
    sublane = sublanes()
    lane = lanes()
    low_side = lane % 8 < 4

    def with_layers(value, low, high, k):
        low = roll(jnp.where(at_low, SOLID, low), -2 * k, 0)
        high = roll(jnp.where(at_high, SOLID, high), 6 - 2 * k, 0)
        return jnp.where(sublane < 2, low, jnp.where(sublane >= 6, high, value))

    patches = [[], []]
    for i in range(Q):
        rows = []
        for group in range(3):
            low, high = below[3 * i + group], above[3 * i + group]
            for k in range(4):
                value = with_layers(main[i, 4 * group + k], low, high, k)
                joined[i, 4 * group + k] = value
                rows.append(value)
        edge = gather_columns(rows, range(2, 14))
        group, k = divmod(i, 4)
        side = with_layers(halo[i], below[3 * Q + group], above[3 * Q + group], k)
        patches[0].append(jnp.where(low_side, side, edge))
        patches[1].append(jnp.where(low_side, edge, side))

    def third(row):
        wet = joined[0, row - 2] != SOLID
        values = relax_wet(stream_row(joined, row, 2), wet)
        for i in range(Q):
            middle[i, row - 3] = values[i]

    over_rows(3, 13, third)
    for side in range(2):
        wet = patches[side][0] != SOLID
        values = relax_wet(stream_patch(patches[side]), wet)
        patches[side] = stream_patch(values)
    own_columns = [jnp.where(low_side, patches[1][i], patches[0][i]) for i in range(Q)]
    seam = (lane < 2) | (lane >= 126)
    for row in range(8):
        wet = middle[0, row + 1] != SOLID
        values = stream_row(middle, row + 4, 3)
        for i in range(Q):
            value = jnp.where(seam, roll(own_columns[i], 0, -(8 * (row + 4) + 4)), values[i])
            turn[i, 8 * row : 8 * row + 8] = jnp.where(wet, value, 0.0)
    for slot in range(2):
        mass = None
        for k in range(2):
            layer = 2 * slot + k
            values = [turn[i, pl.ds(layer + 2, 8, stride=8)] for i in range(Q)]
            for i in range(Q):
                out[i, layer] = values[i]
            axis_sum = functools.reduce(jnp.add, values[1:7])
            edge_sum = functools.reduce(jnp.add, values[7:])
            density = values[0] * (1.0 / 3.0) + axis_sum * (1.0 / 18.0) + edge_sum * (1.0 / 36.0)
            mass = density if mass is None else mass + density
        count = jnp.maximum(block_fluid[slot, 0, 0], 1).astype(F32)
        block_density[slot, 0, 0] = jnp.sum(mass) / count


def exchange(to_low, to_high, axis):
    count = lax.axis_size(axis)
    up = [(i, i + 1) for i in range(count - 1)]
    down = [(i + 1, i) for i in range(count - 1)]
    return lax.ppermute(to_high, axis, up), lax.ppermute(to_low, axis, down)


def call(kernel, outs, in_specs, out_specs=None, scratch=()):
    if out_specs is None:
        out_specs = [VMEM] * len(outs)
    return pl.pallas_call(
        kernel,
        out_shape=outs,
        in_specs=in_specs,
        out_specs=out_specs,
        scratch_shapes=list(scratch),
        compiler_params=pltpu.CompilerParams(vmem_limit_bytes=32 * 1024 * 1024),
    )


def on_device(relative, fluid, block_fluid, new_owner):
    low, high = call(
        split_slabs,
        [shape(Q + 1, 2, 8, 128)] * 2,
        [ANY, VMEM],
        scratch=[pltpu.SemaphoreType.DMA((2,))],
    )(relative, fluid)
    below, above = exchange(low, high, "gz")
    own, y_low, y_high = call(
        first_relax,
        [shape(Q, 8, 8, 128), shape(3 * Q + 5, 8, 128), shape(3 * Q + 5, 8, 128)],
        [VMEM] * 4 + [SMEM],
        scratch=[pltpu.VMEM((Q + 1, 64, 128), F32)],
    )(low, high, below, above, new_owner)
    below, above = exchange(y_low, y_high, "gy")
    main, edge = call(
        join_rows, [shape(Q, 16, 8, 128), shape(Q, 8, 128)], [VMEM] * 3
    )(own, below, above)
    left, right = exchange(edge, edge, "gx")
    inner = call(
        two_steps,
        [shape(Q, 12, 8, 128)],
        [VMEM],
        scratch=[pltpu.VMEM((Q, 14, 8, 128), F32)],
    )(main)[0]
    main, z_low, z_high, halo = call(
        patch_two_steps,
        [shape(Q, 12, 8, 128), shape(3 * Q + 5, 8, 128), shape(3 * Q + 5, 8, 128), shape(Q, 8, 128)],
        [VMEM] * 4,
    )(inner, edge, left, right)
    below, above = exchange(z_low, z_high, "gz")
    out, block_density = call(
        last_two_steps,
        [shape(Q, 4, 8, 128), shape(2, 1, 1)],
        [VMEM] * 4 + [SMEM],
        [VMEM, SMEM],
        scratch=[
            pltpu.VMEM((Q, 12, 8, 128), F32),
            pltpu.VMEM((Q, 10, 8, 128), F32),
            pltpu.VMEM((Q, 64, 128), F32),
        ],
    )(main, halo, below, above, block_fluid)
    return out, block_density


def solution(mesh):
    return jax.shard_map(
        on_device,
        mesh=mesh,
        in_specs=(
            P(None, "gz", "gy", "gx"),
            P("gz", "gy", "gx"),
            P("gz", "gy", "gx"),
            P("gz", "gy", "gx"),
        ),
        out_specs=(P(None, "gz", "gy", "gx"), P("gz", "gy", "gx")),
        check_vma=False,
    )
```

```python
import functools

import jax
import jax.numpy as jnp
from jax import lax
from jax.experimental import pallas as pl
from jax.experimental.pallas import tpu as pltpu
from jax.sharding import PartitionSpec as P


VELOCITIES = [
    (0, 0, 0),
    (1, 0, 0),
    (-1, 0, 0),
    (0, 1, 0),
    (0, -1, 0),
    (0, 0, 1),
    (0, 0, -1),
    (1, 1, 0),
    (-1, -1, 0),
    (1, -1, 0),
    (-1, 1, 0),
    (1, 0, 1),
    (-1, 0, -1),
    (1, 0, -1),
    (-1, 0, 1),
    (0, 1, 1),
    (0, -1, -1),
    (0, 1, -1),
    (0, -1, 1),
]
OPPOSITE = [0, 2, 1, 4, 3, 6, 5, 8, 7, 10, 9, 12, 11, 14, 13, 16, 15, 18, 17]
Q = 19
UP_Y = [i for i in range(Q) if VELOCITIES[i][1] == 1]
DOWN_Y = [i for i in range(Q) if VELOCITIES[i][1] == -1]
SOLID = 3.0e38
Z_ORDER = sorted(range(Q), key=lambda i: {1: 0, -1: 1, 0: 2}[VELOCITIES[i][0]])
SLOT = [Z_ORDER.index(i) for i in range(Q)]
PER_SLOT = 14
NEAR = 34
FAR = 9
FLAT_ROWS = 8 * 8 * NEAR
F32 = jnp.float32
UNROLL = 2
VMEM = pl.BlockSpec(memory_space=pltpu.VMEM)
SMEM = pl.BlockSpec(memory_space=pltpu.SMEM)
HBM = pl.BlockSpec(memory_space=pltpu.HBM)


def shape(*dims):
    return jax.ShapeDtypeStruct(dims, F32)


def lanes():
    return lax.broadcasted_iota(jnp.int32, (8, 128), 1)


def sublanes():
    return lax.broadcasted_iota(jnp.int32, (8, 128), 0)


def roll(value, sublane_shift, lane_shift):
    if sublane_shift % 8:
        value = pltpu.roll(value, sublane_shift % 8, 0)
    if lane_shift % 128:
        value = pltpu.roll(value, lane_shift % 128, 1)
    return value


def relax(g):
    sums = [g[k] + g[k + 1] for k in range(1, Q, 2)]
    diffs = [g[k] - g[k + 1] for k in range(1, Q, 2)]
    axis_sum = sums[0] + sums[1] + sums[2]
    edge_sum = (sums[3] + sums[4]) + (sums[5] + sums[6]) + (sums[7] + sums[8])
    density = 12.0 * g[0] + 2.0 * axis_sum + edge_sum
    moment_z = 2.0 * diffs[0] + ((diffs[3] + diffs[4]) + (diffs[5] + diffs[6]))
    moment_y = 2.0 * diffs[1] + ((diffs[3] - diffs[4]) + (diffs[7] + diffs[8]))
    moment_x = 2.0 * diffs[2] + ((diffs[5] - diffs[6]) + (diffs[7] - diffs[8]))
    inverse = 1.0 / density
    speed = [moment_z * inverse, moment_y * inverse, moment_x * inverse]
    square = speed[0] * speed[0] + speed[1] * speed[1] + speed[2] * speed[2]
    scaled = density * (1.5 / 36.0)
    base = scaled * (1.0 - 1.5 * square)
    linear = [(4.5 / 36.0) * m for m in (moment_z, moment_y, moment_x)]
    speed = [1.5 * s for s in speed]
    out = [base - 0.5 * g[0]]
    for pair in range(9):
        velocity = VELOCITIES[1 + 2 * pair]
        along = None
        twice = None
        for axis in range(3):
            if velocity[axis] == 0:
                continue
            if along is None:
                along, twice = linear[axis], speed[axis]
            elif velocity[axis] > 0:
                along, twice = along + linear[axis], twice + speed[axis]
            else:
                along, twice = along - linear[axis], twice - speed[axis]
        even = base + along * twice - 0.25 * sums[pair]
        odd = along - 0.25 * diffs[pair]
        out += [even + odd, even - odd]
    return out


def relax_wet(g, wet):
    return [jnp.where(wet, value, SOLID) for value in relax(g)]


def stream_row(tile, at):
    own = [tile(i, at) for i in range(Q)]
    out = [own[0]]
    for i in range(1, Q):
        step_z, step_y, step_x = VELOCITIES[i]
        source = own[i] if step_y == 0 else tile(i, at - step_y)
        source = roll(source, step_z, step_x)
        out.append(jnp.where(source == SOLID, own[OPPOSITE[i]], source))
    return out


def relax_row(tile, at):
    wet = tile(0, at) != SOLID
    return relax_wet(stream_row(tile, at), wet)


def stream_patch(values):
    out = [values[0]]
    for i in range(1, Q):
        step_z, step_y, step_x = VELOCITIES[i]
        source = roll(values[i], step_z, 8 * step_y + step_x)
        out.append(jnp.where(source == SOLID, values[OPPOSITE[i]], source))
    return out


def over_rows(first, last, body):
    def step(row, carry):
        body(row)
        return carry

    lax.fori_loop(first, last, step, 0, unroll=UNROLL)


def gather_columns(values, rows):
    lane_row = lanes() // 8
    tile = jnp.full((8, 128), SOLID, F32)
    for row, value in zip(rows, values):
        tile = jnp.where(lane_row == row, roll(value, 0, 8 * row + 4), tile)
    return tile


def split_slabs(relative, fluid, new_owner, low, high, moved, kinds, owner, sems):
    copies = [
        pltpu.make_async_copy(fluid, kinds, sems.at[0]),
        pltpu.make_async_copy(relative.at[:, 2:4], high.at[0:Q], sems.at[1]),
        pltpu.make_async_copy(relative.at[:, 0:2], low.at[0:Q], sems.at[2]),
        pltpu.make_async_copy(new_owner, owner, sems.at[3]),
    ]
    for copy in copies:
        copy.start()
    copies[3].wait()
    place = lax.axis_index("gz")
    moved[0] = jnp.full((8, 128), jnp.where((owner[0, 0] == place - 1) & (place > 0), 1.0, 0.0), F32)
    inside = place < lax.axis_size("gz") - 1
    moved[1] = jnp.full((8, 128), jnp.where((owner[0, 1] == place + 1) & inside, 1.0, 0.0), F32)
    copies[0].wait()
    low[Q] = kinds[0:2].astype(F32)
    high[Q] = kinds[2:4].astype(F32)
    copies[1].wait()
    copies[2].wait()


def first_relax(low, high, below, above, moved, own, y_low, y_high, turn):
    place = lax.axis_index("gz")
    at_low = place == 0
    at_high = place == lax.axis_size("gz") - 1
    swap_low = moved[0] > 0.5
    swap_high = moved[1] > 0.5
    for k in range(2):
        turn[Q, 8 * k : 8 * k + 8] = jnp.where(at_low, 0.0, below[Q, k])
        turn[Q, 8 * (k + 2) : 8 * (k + 3)] = low[Q, k]
        turn[Q, 8 * (k + 4) : 8 * (k + 5)] = high[Q, k]
        turn[Q, 8 * (k + 6) : 8 * (k + 7)] = jnp.where(at_high, 0.0, above[Q, k])
    for i in range(Q):
        for k in range(2):
            mine, other = low[i, k], below[i, k]
            turn[i, 8 * k : 8 * k + 8] = jnp.where(swap_low, mine, other)
            turn[i, 8 * (k + 2) : 8 * (k + 3)] = jnp.where(swap_low, other, mine)
            mine, other = high[i, k], above[i, k]
            turn[i, 8 * (k + 4) : 8 * (k + 5)] = jnp.where(swap_high, other, mine)
            turn[i, 8 * (k + 6) : 8 * (k + 7)] = jnp.where(swap_high, mine, other)
    for row in range(8):
        wet = turn[Q, pl.ds(row, 8, stride=8)] > 0.5
        values = relax_wet([turn[i, pl.ds(row, 8, stride=8)] for i in range(Q)], wet)
        for i in range(Q):
            own[i, row] = values[i]
            if row < 3:
                y_low[3 * i + row] = values[i]
            if row > 4:
                y_high[3 * i + row - 5] = values[i]
        if row == 3:
            for k, i in enumerate(DOWN_Y):
                y_low[3 * Q + k] = values[i]
        if row == 4:
            for k, i in enumerate(UP_Y):
                y_high[3 * Q + k] = values[i]


def join_rows(own, below, above, main, edge, x_low, x_high):
    place = lax.axis_index("gy")
    at_low = place == 0
    at_high = place == lax.axis_size("gy") - 1
    edges = []
    for i in range(Q):
        rows = []
        if i in UP_Y:
            rows.append(jnp.where(at_low, SOLID, below[3 * Q + UP_Y.index(i)]))
        else:
            rows.append(jnp.full((8, 128), SOLID, F32))
        for k in range(3):
            rows.append(jnp.where(at_low, SOLID, below[3 * i + k]))
        for k in range(8):
            rows.append(own[i, k])
        for k in range(3):
            rows.append(jnp.where(at_high, SOLID, above[3 * i + k]))
        if i in DOWN_Y:
            rows.append(jnp.where(at_high, SOLID, above[3 * Q + DOWN_Y.index(i)]))
        else:
            rows.append(jnp.full((8, 128), SOLID, F32))
        for k in range(16):
            main[i, k] = rows[k]
        edges.append(gather_columns(rows, range(16)))
        edge[i] = edges[i]
    low_side = lanes() % 8 < 4
    for i in range(10):
        if i + 10 < Q:
            x_low[i] = jnp.where(low_side, roll(edges[i + 10], 0, -4), edges[i])
            x_high[i] = jnp.where(low_side, edges[i], roll(edges[i + 10], 0, 4))
        else:
            x_low[i] = edges[i]
            x_high[i] = edges[i]


def two_steps(main, out, edge, middle):
    def first(row):
        values = relax_row(lambda i, at: main[i, at], row)
        for i in range(Q):
            middle[i, row - 1] = values[i]

    def second(row):
        values = relax_row(lambda i, at: middle[i, at], row - 1)
        for i in range(Q):
            out[i, row - 2] = values[i]

    over_rows(1, 15, first)
    over_rows(2, 14, second)
    for i in range(Q):
        edge[i] = gather_columns([out[i, k] for k in range(12)], range(2, 14))


def patch_two_steps(inner, inner_edge, edge, left, right, flat, below, above):
    place = lax.axis_index("gx")
    at_low = place == 0
    at_high = place == lax.axis_size("gx") - 1
    column = lanes() % 8
    low_side = column < 4
    sides = []
    for side in range(2):
        values = []
        for i in range(Q):
            message = (left, right)[side][i % 10]
            if i >= 10:
                message = roll(message, 0, (-4, 4)[side])
            message = jnp.where((at_low, at_high)[side], SOLID, message)
            if side == 0:
                values.append(jnp.where(low_side, message, edge[i]))
            else:
                values.append(jnp.where(low_side, edge[i], message))
        for step in range(2):
            wet = values[0] != SOLID
            values = relax_wet(stream_patch(values), wet)
        sides.append(values)
    lane = lanes()
    seam = (lane < 2) | (lane >= 126)
    for i in range(Q):
        own_columns = jnp.where(low_side, sides[1][i], sides[0][i])
        first = PER_SLOT * SLOT[i]
        for row in range(12):
            value = jnp.where(seam, roll(own_columns, 0, -(8 * (row + 2) + 4)), inner[i, row])
            flat[8 * (first + row) : 8 * (first + row) + 8] = value
        fresh = inner_edge[i]
        for side in range(2):
            stale = (column < 6) if side == 0 else (column >= 2)
            at = 8 * (first + 12 + side)
            flat[at : at + 8] = jnp.where(stale, sides[side][i], fresh)
    flat[8 * PER_SLOT * Q :] = jnp.full((FLAT_ROWS - 8 * PER_SLOT * Q, 128), SOLID, F32)
    for group in range(NEAR):
        above[group] = flat[pl.ds(64 * group + 5, 8, stride=8)]
        below[group] = flat[pl.ds(64 * group + 2, 8, stride=8)]
    for group in range(FAR):
        above[NEAR + group] = flat[pl.ds(64 * group + 4, 8, stride=8)]
        below[NEAR + group] = flat[pl.ds(8 * 5 * PER_SLOT + 64 * group + 3, 8, stride=8)]


def last_two_steps(
    flat_in, below, above, block_fluid, out, block_density, flat, middle, turn, final, wet_count, sems
):
    count_copy = pltpu.make_async_copy(block_fluid, wet_count, sems.at[2])
    count_copy.start()
    place = lax.axis_index("gz")
    at_low = place == 0
    at_high = place == lax.axis_size("gz") - 1
    lane = lanes()
    low_side = lane % 8 < 4
    for group in range(NEAR):
        flat[pl.ds(64 * group + 1, 8, stride=8)] = jnp.where(at_low, SOLID, below[group])
        flat[pl.ds(64 * group + 6, 8, stride=8)] = jnp.where(at_high, SOLID, above[group])
    for group in range(FAR):
        flat[pl.ds(64 * group, 8, stride=8)] = jnp.where(at_low, SOLID, below[NEAR + group])
        flat[pl.ds(8 * 5 * PER_SLOT + 64 * group + 7, 8, stride=8)] = jnp.where(
            at_high, SOLID, above[NEAR + group]
        )

    def joined(i, at):
        return flat[pl.ds(pl.multiple_of(8 * (PER_SLOT * SLOT[i] + at), 8), 8)]

    def third(row):
        values = relax_row(joined, row - 2)
        for i in range(Q):
            middle[i, row - 3] = values[i]

    over_rows(3, 13, third)
    patches = []
    for side in range(2):
        values = [joined(i, 12 + side) for i in range(Q)]
        wet = values[0] != SOLID
        values = relax_wet(stream_patch(values), wet)
        patches.append(stream_patch(values))
    own_columns = [jnp.where(low_side, patches[1][i], patches[0][i]) for i in range(Q)]
    seam = (lane < 2) | (lane >= 126)
    for row in range(8):
        wet = middle[0, row + 1] != SOLID
        values = stream_row(lambda i, at: middle[i, at], row + 1)
        for i in range(Q):
            value = jnp.where(seam, roll(own_columns[i], 0, -(8 * (row + 4) + 4)), values[i])
            turn[i, 8 * row : 8 * row + 8] = jnp.where(wet, value, 0.0)
    copies = []
    masses = []
    for slot in range(2):
        mass = None
        for k in range(2):
            layer = 2 * slot + k
            values = [turn[i, pl.ds(layer + 2, 8, stride=8)] for i in range(Q)]
            for i in range(Q):
                final[i, layer] = values[i]
            axis_sum = functools.reduce(jnp.add, values[1:7])
            edge_sum = functools.reduce(jnp.add, values[7:])
            density = values[0] * (1.0 / 3.0) + axis_sum * (1.0 / 18.0) + edge_sum * (1.0 / 36.0)
            mass = density if mass is None else mass + density
        masses.append(mass)
        layers = slice(2 * slot, 2 * slot + 2)
        copies.append(pltpu.make_async_copy(final.at[:, layers], out.at[:, layers], sems.at[slot]))
        copies[slot].start()
    count_copy.wait()
    for slot in range(2):
        count = jnp.maximum(wet_count[0, slot], 1).astype(F32)
        block_density[0, slot] = jnp.sum(masses[slot]) / count
    for copy in copies:
        copy.wait()


def exchange(to_low, to_high, axis, ring=False):
    count = lax.axis_size(axis)
    up = [(i, (i + 1) % count) for i in range(count if ring else count - 1)]
    down = [(target, source) for source, target in up]
    return lax.ppermute(to_high, axis, up), lax.ppermute(to_low, axis, down)


def call(kernel, outs, in_specs, out_specs=None, scratch=(), aliases=None, vmem=32):
    if out_specs is None:
        out_specs = [VMEM] * len(outs)
    return pl.pallas_call(
        kernel,
        out_shape=outs,
        in_specs=in_specs,
        out_specs=out_specs,
        scratch_shapes=list(scratch),
        input_output_aliases=aliases or {},
        compiler_params=pltpu.CompilerParams(vmem_limit_bytes=vmem * 1024 * 1024),
    )


def in_hbm(array):
    return pltpu.with_memory_space_constraint(array, pltpu.HBM)


def on_device(relative, fluid, block_fluid, new_owner):
    low, high, moved = call(
        split_slabs,
        [shape(Q + 1, 2, 8, 128), shape(Q + 1, 2, 8, 128), shape(2, 8, 128)],
        [HBM] * 3,
        scratch=[
            pltpu.VMEM((4, 8, 128), jnp.int32),
            pltpu.SMEM((1, 2), jnp.int32),
            pltpu.SemaphoreType.DMA((4,)),
        ],
    )(in_hbm(relative), in_hbm(fluid), in_hbm(new_owner.transpose(1, 2, 0).reshape(1, 2)))
    below, above = exchange(low, high, "gz", ring=True)
    own, y_low, y_high = call(
        first_relax,
        [shape(Q, 8, 8, 128), shape(3 * Q + 5, 8, 128), shape(3 * Q + 5, 8, 128)],
        [VMEM] * 5,
        scratch=[pltpu.VMEM((Q + 1, 64, 128), F32)],
    )(low, high, below, above, moved)
    below, above = exchange(y_low, y_high, "gy")
    main, edge, x_low, x_high = call(
        join_rows,
        [shape(Q, 16, 8, 128), shape(Q, 8, 128), shape(10, 8, 128), shape(10, 8, 128)],
        [VMEM] * 3,
    )(own, below, above)
    left, right = exchange(x_low, x_high, "gx")
    inner, inner_edge = call(
        two_steps,
        [shape(Q, 12, 8, 128), shape(Q, 8, 128)],
        [VMEM],
        scratch=[pltpu.VMEM((Q, 14, 8, 128), F32)],
    )(main)
    flat, z_low, z_high = call(
        patch_two_steps,
        [shape(FLAT_ROWS, 128), shape(NEAR + FAR, 8, 128), shape(NEAR + FAR, 8, 128)],
        [VMEM] * 5,
    )(inner, inner_edge, edge, left, right)
    below, above = exchange(z_low, z_high, "gz", ring=True)
    out, block_density, _ = call(
        last_two_steps,
        [shape(Q, 4, 8, 128), shape(1, 2), shape(FLAT_ROWS, 128)],
        [VMEM] * 3 + [HBM],
        [HBM, SMEM, VMEM],
        scratch=[
            pltpu.VMEM((Q, 10, 8, 128), F32),
            pltpu.VMEM((Q, 64, 128), F32),
            pltpu.VMEM((Q, 4, 8, 128), F32),
            pltpu.SMEM((1, 2), jnp.int32),
            pltpu.SemaphoreType.DMA((3,)),
        ],
        aliases={0: 2},
    )(flat, below, above, in_hbm(block_fluid.transpose(1, 2, 0).reshape(1, 2)))
    return out, block_density.reshape(1, 1, 2).transpose(2, 0, 1)


def solution(mesh):
    return jax.shard_map(
        on_device,
        mesh=mesh,
        in_specs=(
            P(None, "gz", "gy", "gx"),
            P("gz", "gy", "gx"),
            P("gz", "gy", "gx"),
            P("gz", "gy", "gx"),
        ),
        out_specs=(P(None, "gz", "gy", "gx"), P("gz", "gy", "gx")),
        check_vma=False,
    )
```

```python
import functools

import jax
import jax.numpy as jnp
from jax import lax
from jax.experimental import pallas as pl
from jax.experimental.pallas import tpu as pltpu
from jax.sharding import PartitionSpec as P


VELOCITIES = [
    (0, 0, 0),
    (1, 0, 0),
    (-1, 0, 0),
    (0, 1, 0),
    (0, -1, 0),
    (0, 0, 1),
    (0, 0, -1),
    (1, 1, 0),
    (-1, -1, 0),
    (1, -1, 0),
    (-1, 1, 0),
    (1, 0, 1),
    (-1, 0, -1),
    (1, 0, -1),
    (-1, 0, 1),
    (0, 1, 1),
    (0, -1, -1),
    (0, 1, -1),
    (0, -1, 1),
]
OPPOSITE = [0, 2, 1, 4, 3, 6, 5, 8, 7, 10, 9, 12, 11, 14, 13, 16, 15, 18, 17]
Q = 19
UP_Y = [i for i in range(Q) if VELOCITIES[i][1] == 1]
DOWN_Y = [i for i in range(Q) if VELOCITIES[i][1] == -1]
SOLID = 3.0e38
Z_ORDER = sorted(range(Q), key=lambda i: {1: 0, -1: 1, 0: 2}[VELOCITIES[i][0]])
SLOT = [Z_ORDER.index(i) for i in range(Q)]
PER_SLOT = 14
NEAR = 34
FAR = 9
FLAT_ROWS = 8 * 8 * NEAR
F32 = jnp.float32
UNROLL = 2
VMEM = pl.BlockSpec(memory_space=pltpu.VMEM)
SMEM = pl.BlockSpec(memory_space=pltpu.SMEM)
HBM = pl.BlockSpec(memory_space=pltpu.HBM)


def shape(*dims):
    return jax.ShapeDtypeStruct(dims, F32)


def lanes():
    return lax.broadcasted_iota(jnp.int32, (8, 128), 1)


def sublanes():
    return lax.broadcasted_iota(jnp.int32, (8, 128), 0)


def roll(value, sublane_shift, lane_shift):
    if sublane_shift % 8:
        value = pltpu.roll(value, sublane_shift % 8, 0)
    if lane_shift % 128:
        value = pltpu.roll(value, lane_shift % 128, 1)
    return value


def relax(g):
    sums = [g[k] + g[k + 1] for k in range(1, Q, 2)]
    diffs = [g[k] - g[k + 1] for k in range(1, Q, 2)]
    axis_sum = sums[0] + sums[1] + sums[2]
    edge_sum = (sums[3] + sums[4]) + (sums[5] + sums[6]) + (sums[7] + sums[8])
    density = 12.0 * g[0] + 2.0 * axis_sum + edge_sum
    moment_z = 2.0 * diffs[0] + ((diffs[3] + diffs[4]) + (diffs[5] + diffs[6]))
    moment_y = 2.0 * diffs[1] + ((diffs[3] - diffs[4]) + (diffs[7] + diffs[8]))
    moment_x = 2.0 * diffs[2] + ((diffs[5] - diffs[6]) + (diffs[7] - diffs[8]))
    inverse = 1.0 / density
    speed = [moment_z * inverse, moment_y * inverse, moment_x * inverse]
    square = speed[0] * speed[0] + speed[1] * speed[1] + speed[2] * speed[2]
    scaled = density * (1.5 / 36.0)
    base = scaled * (1.0 - 1.5 * square)
    linear = [(4.5 / 36.0) * m for m in (moment_z, moment_y, moment_x)]
    speed = [1.5 * s for s in speed]
    out = [base - 0.5 * g[0]]
    for pair in range(9):
        velocity = VELOCITIES[1 + 2 * pair]
        along = None
        twice = None
        for axis in range(3):
            if velocity[axis] == 0:
                continue
            if along is None:
                along, twice = linear[axis], speed[axis]
            elif velocity[axis] > 0:
                along, twice = along + linear[axis], twice + speed[axis]
            else:
                along, twice = along - linear[axis], twice - speed[axis]
        even = base + along * twice - 0.25 * sums[pair]
        odd = along - 0.25 * diffs[pair]
        out += [even + odd, even - odd]
    return out


def relax_wet(g, wet):
    return [jnp.where(wet, value, SOLID) for value in relax(g)]


def stream_row(tile, at):
    own = [tile(i, at) for i in range(Q)]
    out = [own[0]]
    for i in range(1, Q):
        step_z, step_y, step_x = VELOCITIES[i]
        source = own[i] if step_y == 0 else tile(i, at - step_y)
        source = roll(source, step_z, step_x)
        out.append(jnp.where(source == SOLID, own[OPPOSITE[i]], source))
    return out


def relax_row(tile, at):
    wet = tile(0, at) != SOLID
    return relax_wet(stream_row(tile, at), wet)


def stream_patch(values):
    out = [values[0]]
    for i in range(1, Q):
        step_z, step_y, step_x = VELOCITIES[i]
        source = roll(values[i], step_z, 8 * step_y + step_x)
        out.append(jnp.where(source == SOLID, values[OPPOSITE[i]], source))
    return out


def over_rows(first, last, body):
    def step(row, carry):
        body(row)
        return carry

    lax.fori_loop(first, last, step, 0, unroll=UNROLL)


def gather_columns(values, rows):
    lane_row = lanes() // 8
    tile = jnp.full((8, 128), SOLID, F32)
    for row, value in zip(rows, values):
        tile = jnp.where(lane_row == row, roll(value, 0, 8 * row + 4), tile)
    return tile


def split_slabs(relative, fluid, new_owner, low, high, moved, kinds, owner, sems):
    copies = [
        pltpu.make_async_copy(fluid, kinds, sems.at[0]),
        pltpu.make_async_copy(relative.at[:, 2:4], high.at[0:Q], sems.at[1]),
        pltpu.make_async_copy(relative.at[:, 0:2], low.at[0:Q], sems.at[2]),
        pltpu.make_async_copy(new_owner, owner, sems.at[3]),
    ]
    for copy in copies:
        copy.start()
    copies[3].wait()
    place = lax.axis_index("gz")
    moved[0] = jnp.full((8, 128), jnp.where((owner[0, 0] == place - 1) & (place > 0), 1.0, 0.0), F32)
    inside = place < lax.axis_size("gz") - 1
    moved[1] = jnp.full((8, 128), jnp.where((owner[0, 1] == place + 1) & inside, 1.0, 0.0), F32)
    copies[0].wait()
    low[Q] = kinds[0:2].astype(F32)
    high[Q] = kinds[2:4].astype(F32)
    copies[1].wait()
    copies[2].wait()


def first_relax(low, high, below, above, moved, own, ahead, back, turn):
    place = lax.axis_index("gz")
    at_low = place == 0
    at_high = place == lax.axis_size("gz") - 1
    swap_low = moved[0] > 0.5
    swap_high = moved[1] > 0.5
    for k in range(2):
        turn[Q, 8 * k : 8 * k + 8] = jnp.where(at_low, 0.0, below[Q, k])
        turn[Q, 8 * (k + 2) : 8 * (k + 3)] = low[Q, k]
        turn[Q, 8 * (k + 4) : 8 * (k + 5)] = high[Q, k]
        turn[Q, 8 * (k + 6) : 8 * (k + 7)] = jnp.where(at_high, 0.0, above[Q, k])
    for i in range(Q):
        for k in range(2):
            mine, other = low[i, k], below[i, k]
            turn[i, 8 * k : 8 * k + 8] = jnp.where(swap_low, mine, other)
            turn[i, 8 * (k + 2) : 8 * (k + 3)] = jnp.where(swap_low, other, mine)
            mine, other = high[i, k], above[i, k]
            turn[i, 8 * (k + 4) : 8 * (k + 5)] = jnp.where(swap_high, other, mine)
            turn[i, 8 * (k + 6) : 8 * (k + 7)] = jnp.where(swap_high, mine, other)
    for row in range(8):
        wet = turn[Q, pl.ds(row, 8, stride=8)] > 0.5
        values = relax_wet([turn[i, pl.ds(row, 8, stride=8)] for i in range(Q)], wet)
        for i in range(Q):
            own[i, row] = values[i]
    up = place % 2 == 0
    for message, high_rows in ((ahead, up), (back, jnp.logical_not(up))):
        first = jnp.where(high_rows, 5, 0)
        far = jnp.where(high_rows, 4, 3)
        for i in range(Q):
            for k in range(3):
                message[3 * i + k] = own[i, first + k]
        for k in range(5):
            message[3 * Q + k] = own[jnp.where(high_rows, UP_Y[k], DOWN_Y[k]), far]


def join_rows(own, ahead, back, main, edge, x_ahead, x_back):
    place = lax.axis_index("gy")
    up = lax.axis_index("gz") % 2 == 0
    outside_low = place == 0
    outside_high = place == lax.axis_size("gy") - 1
    for i in range(Q):
        main[i, 0] = jnp.full((8, 128), SOLID, F32)
        main[i, 15] = jnp.full((8, 128), SOLID, F32)
    for message, low_rows in ((ahead, up), (back, jnp.logical_not(up))):
        outside = jnp.where(low_rows, outside_low, outside_high)
        first = jnp.where(low_rows, 1, 12)
        far = jnp.where(low_rows, 0, 15)
        for i in range(Q):
            for k in range(3):
                main[i, first + k] = jnp.where(outside, SOLID, message[3 * i + k])
        for k in range(5):
            value = jnp.where(outside, SOLID, message[3 * Q + k])
            main[jnp.where(low_rows, UP_Y[k], DOWN_Y[k]), far] = value
    edges = []
    for i in range(Q):
        rows = [own[i, k] for k in range(8)]
        for k in range(8):
            main[i, 4 + k] = rows[k]
        rows = [main[i, k] for k in range(4)] + rows + [main[i, k] for k in range(12, 16)]
        edges.append(gather_columns(rows, range(16)))
        edge[i] = edges[i]
    low_side = lanes() % 8 < 4
    for i in range(10):
        if i + 10 < Q:
            to_low = jnp.where(low_side, roll(edges[i + 10], 0, -4), edges[i])
            to_high = jnp.where(low_side, edges[i], roll(edges[i + 10], 0, 4))
            x_ahead[i] = jnp.where(up, to_high, to_low)
            x_back[i] = jnp.where(up, to_low, to_high)
        else:
            x_ahead[i] = edges[i]
            x_back[i] = edges[i]


def two_steps(main, out, edge, middle):
    def first(row):
        values = relax_row(lambda i, at: main[i, at], row)
        for i in range(Q):
            middle[i, row - 1] = values[i]

    def second(row):
        values = relax_row(lambda i, at: middle[i, at], row - 1)
        for i in range(Q):
            out[i, row - 2] = values[i]

    over_rows(1, 15, first)
    over_rows(2, 14, second)
    for i in range(Q):
        edge[i] = gather_columns([out[i, k] for k in range(12)], range(2, 14))


def patch_two_steps(inner, inner_edge, edge, ahead, back, flat, below, above):
    up = lax.axis_index("gz") % 2 == 0
    place = lax.axis_index("gx")
    at_low = place == 0
    at_high = place == lax.axis_size("gx") - 1
    column = lanes() % 8
    low_side = column < 4
    sides = []
    for side in range(2):
        values = []
        for i in range(Q):
            message = jnp.where(up == (side == 0), ahead[i % 10], back[i % 10])
            if i >= 10:
                message = roll(message, 0, (-4, 4)[side])
            message = jnp.where((at_low, at_high)[side], SOLID, message)
            if side == 0:
                values.append(jnp.where(low_side, message, edge[i]))
            else:
                values.append(jnp.where(low_side, edge[i], message))
        for step in range(2):
            wet = values[0] != SOLID
            values = relax_wet(stream_patch(values), wet)
        sides.append(values)
    lane = lanes()
    seam = (lane < 2) | (lane >= 126)
    for i in range(Q):
        own_columns = jnp.where(low_side, sides[1][i], sides[0][i])
        first = PER_SLOT * SLOT[i]
        for row in range(12):
            value = jnp.where(seam, roll(own_columns, 0, -(8 * (row + 2) + 4)), inner[i, row])
            flat[8 * (first + row) : 8 * (first + row) + 8] = value
        fresh = inner_edge[i]
        for side in range(2):
            stale = (column < 6) if side == 0 else (column >= 2)
            at = 8 * (first + 12 + side)
            flat[at : at + 8] = jnp.where(stale, sides[side][i], fresh)
    flat[8 * PER_SLOT * Q :] = jnp.full((FLAT_ROWS - 8 * PER_SLOT * Q, 128), SOLID, F32)
    for group in range(NEAR):
        above[group] = flat[pl.ds(64 * group + 5, 8, stride=8)]
        below[group] = flat[pl.ds(64 * group + 2, 8, stride=8)]
    for group in range(FAR):
        above[NEAR + group] = flat[pl.ds(64 * group + 4, 8, stride=8)]
        below[NEAR + group] = flat[pl.ds(8 * 5 * PER_SLOT + 64 * group + 3, 8, stride=8)]


def last_two_steps(
    flat_in, below, above, block_fluid, out, block_density, flat, middle, turn, final, wet_count, sems
):
    count_copy = pltpu.make_async_copy(block_fluid, wet_count, sems.at[2])
    count_copy.start()
    place = lax.axis_index("gz")
    at_low = place == 0
    at_high = place == lax.axis_size("gz") - 1
    lane = lanes()
    low_side = lane % 8 < 4
    for group in range(NEAR):
        flat[pl.ds(64 * group + 1, 8, stride=8)] = jnp.where(at_low, SOLID, below[group])
        flat[pl.ds(64 * group + 6, 8, stride=8)] = jnp.where(at_high, SOLID, above[group])
    for group in range(FAR):
        flat[pl.ds(64 * group, 8, stride=8)] = jnp.where(at_low, SOLID, below[NEAR + group])
        flat[pl.ds(8 * 5 * PER_SLOT + 64 * group + 7, 8, stride=8)] = jnp.where(
            at_high, SOLID, above[NEAR + group]
        )

    def joined(i, at):
        return flat[pl.ds(pl.multiple_of(8 * (PER_SLOT * SLOT[i] + at), 8), 8)]

    def third(row):
        values = relax_row(joined, row - 2)
        for i in range(Q):
            middle[i, row - 3] = values[i]

    over_rows(3, 13, third)
    patches = []
    for side in range(2):
        values = [joined(i, 12 + side) for i in range(Q)]
        wet = values[0] != SOLID
        values = relax_wet(stream_patch(values), wet)
        patches.append(stream_patch(values))
    own_columns = [jnp.where(low_side, patches[1][i], patches[0][i]) for i in range(Q)]
    seam = (lane < 2) | (lane >= 126)
    for row in range(8):
        wet = middle[0, row + 1] != SOLID
        values = stream_row(lambda i, at: middle[i, at], row + 1)
        for i in range(Q):
            value = jnp.where(seam, roll(own_columns[i], 0, -(8 * (row + 4) + 4)), values[i])
            turn[i, 8 * row : 8 * row + 8] = jnp.where(wet, value, 0.0)
    copies = []
    masses = []
    for slot in range(2):
        mass = None
        for k in range(2):
            layer = 2 * slot + k
            values = [turn[i, pl.ds(layer + 2, 8, stride=8)] for i in range(Q)]
            for i in range(Q):
                final[i, layer] = values[i]
            axis_sum = functools.reduce(jnp.add, values[1:7])
            edge_sum = functools.reduce(jnp.add, values[7:])
            density = values[0] * (1.0 / 3.0) + axis_sum * (1.0 / 18.0) + edge_sum * (1.0 / 36.0)
            mass = density if mass is None else mass + density
        masses.append(mass)
        layers = slice(2 * slot, 2 * slot + 2)
        copies.append(pltpu.make_async_copy(final.at[:, layers], out.at[:, layers], sems.at[slot]))
        copies[slot].start()
    count_copy.wait()
    for slot in range(2):
        count = jnp.maximum(wet_count[0, slot], 1).astype(F32)
        block_density[0, slot] = jnp.sum(masses[slot]) / count
    for copy in copies:
        copy.wait()


def ring_exchange(to_low, to_high, axis):
    count = lax.axis_size(axis)
    up = [(i, (i + 1) % count) for i in range(count)]
    down = [(target, source) for source, target in up]
    return lax.ppermute(to_high, axis, up), lax.ppermute(to_low, axis, down)


def loop_exchange(ahead, back, axis):
    count = lax.axis_size(axis)
    layers = lax.axis_size("gz")
    pairs = []
    for i in range(count):
        for layer in range(layers):
            if layer % 2 == 0:
                target = (i + 1, layer) if i < count - 1 else (i, layer + 1)
            else:
                target = (i - 1, layer) if i > 0 else (i, layer - 1)
            pairs.append((i * layers + layer, target[0] * layers + target[1]))
    inverse = [(target, source) for source, target in pairs]
    axes = (axis, "gz")
    return lax.ppermute(ahead, axes, pairs), lax.ppermute(back, axes, inverse)


def call(kernel, outs, in_specs, out_specs=None, scratch=(), aliases=None, vmem=32):
    if out_specs is None:
        out_specs = [VMEM] * len(outs)
    return pl.pallas_call(
        kernel,
        out_shape=outs,
        in_specs=in_specs,
        out_specs=out_specs,
        scratch_shapes=list(scratch),
        input_output_aliases=aliases or {},
        compiler_params=pltpu.CompilerParams(vmem_limit_bytes=vmem * 1024 * 1024),
    )


def in_hbm(array):
    return pltpu.with_memory_space_constraint(array, pltpu.HBM)


def on_device(relative, fluid, block_fluid, new_owner):
    low, high, moved = call(
        split_slabs,
        [shape(Q + 1, 2, 8, 128), shape(Q + 1, 2, 8, 128), shape(2, 8, 128)],
        [HBM] * 3,
        scratch=[
            pltpu.VMEM((4, 8, 128), jnp.int32),
            pltpu.SMEM((1, 2), jnp.int32),
            pltpu.SemaphoreType.DMA((4,)),
        ],
    )(in_hbm(relative), in_hbm(fluid), in_hbm(new_owner.transpose(1, 2, 0).reshape(1, 2)))
    below, above = ring_exchange(low, high, "gz")
    own, ahead, back = call(
        first_relax,
        [shape(Q, 8, 8, 128), shape(3 * Q + 5, 8, 128), shape(3 * Q + 5, 8, 128)],
        [VMEM] * 5,
        scratch=[pltpu.VMEM((Q + 1, 64, 128), F32)],
    )(low, high, below, above, moved)
    ahead, back = loop_exchange(ahead, back, "gy")
    main, edge, x_ahead, x_back = call(
        join_rows,
        [shape(Q, 16, 8, 128), shape(Q, 8, 128), shape(10, 8, 128), shape(10, 8, 128)],
        [VMEM] * 3,
    )(own, ahead, back)
    x_ahead, x_back = loop_exchange(x_ahead, x_back, "gx")
    inner, inner_edge = call(
        two_steps,
        [shape(Q, 12, 8, 128), shape(Q, 8, 128)],
        [VMEM],
        scratch=[pltpu.VMEM((Q, 14, 8, 128), F32)],
    )(main)
    flat, z_low, z_high = call(
        patch_two_steps,
        [shape(FLAT_ROWS, 128), shape(NEAR + FAR, 8, 128), shape(NEAR + FAR, 8, 128)],
        [VMEM] * 5,
    )(inner, inner_edge, edge, x_ahead, x_back)
    below, above = ring_exchange(z_low, z_high, "gz")
    out, block_density, _ = call(
        last_two_steps,
        [shape(Q, 4, 8, 128), shape(1, 2), shape(FLAT_ROWS, 128)],
        [VMEM] * 3 + [HBM],
        [HBM, SMEM, VMEM],
        scratch=[
            pltpu.VMEM((Q, 10, 8, 128), F32),
            pltpu.VMEM((Q, 64, 128), F32),
            pltpu.VMEM((Q, 4, 8, 128), F32),
            pltpu.SMEM((1, 2), jnp.int32),
            pltpu.SemaphoreType.DMA((3,)),
        ],
        aliases={0: 2},
    )(flat, below, above, in_hbm(block_fluid.transpose(1, 2, 0).reshape(1, 2)))
    return out, block_density.reshape(1, 1, 2).transpose(2, 0, 1)


def solution(mesh):
    return jax.shard_map(
        on_device,
        mesh=mesh,
        in_specs=(
            P(None, "gz", "gy", "gx"),
            P("gz", "gy", "gx"),
            P("gz", "gy", "gx"),
            P("gz", "gy", "gx"),
        ),
        out_specs=(P(None, "gz", "gy", "gx"), P("gz", "gy", "gx")),
        check_vma=False,
    )
```

```python
import functools

import jax
import jax.numpy as jnp
from jax import lax
from jax.experimental import pallas as pl
from jax.experimental.pallas import tpu as pltpu
from jax.sharding import PartitionSpec as P


VELOCITIES = [
    (0, 0, 0),
    (1, 0, 0),
    (-1, 0, 0),
    (0, 1, 0),
    (0, -1, 0),
    (0, 0, 1),
    (0, 0, -1),
    (1, 1, 0),
    (-1, -1, 0),
    (1, -1, 0),
    (-1, 1, 0),
    (1, 0, 1),
    (-1, 0, -1),
    (1, 0, -1),
    (-1, 0, 1),
    (0, 1, 1),
    (0, -1, -1),
    (0, 1, -1),
    (0, -1, 1),
]
OPPOSITE = [0, 2, 1, 4, 3, 6, 5, 8, 7, 10, 9, 12, 11, 14, 13, 16, 15, 18, 17]
Q = 19
SOLID = 3.0e38
Z_ORDER = sorted(range(Q), key=lambda i: {1: 0, -1: 1, 0: 2}[VELOCITIES[i][0]])
SLOT = [Z_ORDER.index(i) for i in range(Q)]
UP_Y = [i for i in Z_ORDER if VELOCITIES[i][1] == 1]
DOWN_Y = [i for i in Z_ORDER if VELOCITIES[i][1] == -1]
Y_FIRST = [3 * s + min(s // 5, 2) for s in SLOT]
Y_FAR = [15, 31, 59, 60, 61]
Y_TILES = 52
PER_SLOT = 14
NEAR = 34
FAR = 9
FLAT_ROWS = 8 * 8 * NEAR
F32 = jnp.float32
VMEM = pl.BlockSpec(memory_space=pltpu.VMEM)
SMEM = pl.BlockSpec(memory_space=pltpu.SMEM)
HBM = pl.BlockSpec(memory_space=pltpu.HBM)


def shape(*dims):
    return jax.ShapeDtypeStruct(dims, F32)


def lanes():
    return lax.broadcasted_iota(jnp.int32, (8, 128), 1)


def sublanes():
    return lax.broadcasted_iota(jnp.int32, (8, 128), 0)


def roll(value, sublane_shift, lane_shift):
    if sublane_shift % 8:
        value = pltpu.roll(value, sublane_shift % 8, 0)
    if lane_shift % 128:
        value = pltpu.roll(value, lane_shift % 128, 1)
    return value


def relax(g):
    sums = [g[k] + g[k + 1] for k in range(1, Q, 2)]
    diffs = [g[k] - g[k + 1] for k in range(1, Q, 2)]
    axis_sum = sums[0] + sums[1] + sums[2]
    edge_sum = (sums[3] + sums[4]) + (sums[5] + sums[6]) + (sums[7] + sums[8])
    density = 12.0 * g[0] + 2.0 * axis_sum + edge_sum
    moment_z = 2.0 * diffs[0] + ((diffs[3] + diffs[4]) + (diffs[5] + diffs[6]))
    moment_y = 2.0 * diffs[1] + ((diffs[3] - diffs[4]) + (diffs[7] + diffs[8]))
    moment_x = 2.0 * diffs[2] + ((diffs[5] - diffs[6]) + (diffs[7] - diffs[8]))
    inverse = 1.0 / density
    speed = [moment_z * inverse, moment_y * inverse, moment_x * inverse]
    square = speed[0] * speed[0] + speed[1] * speed[1] + speed[2] * speed[2]
    scaled = density * (1.5 / 36.0)
    base = scaled * (1.0 - 1.5 * square)
    linear = [(4.5 / 36.0) * m for m in (moment_z, moment_y, moment_x)]
    speed = [1.5 * s for s in speed]
    out = [base - 0.5 * g[0]]
    for pair in range(9):
        velocity = VELOCITIES[1 + 2 * pair]
        along = None
        twice = None
        for axis in range(3):
            if velocity[axis] == 0:
                continue
            if along is None:
                along, twice = linear[axis], speed[axis]
            elif velocity[axis] > 0:
                along, twice = along + linear[axis], twice + speed[axis]
            else:
                along, twice = along - linear[axis], twice - speed[axis]
        even = base + along * twice - 0.25 * sums[pair]
        odd = along - 0.25 * diffs[pair]
        out += [even + odd, even - odd]
    return out


def relax_wet(g, wet):
    return [jnp.where(wet, value, SOLID) for value in relax(g)]


def stream_row(tile, at):
    own = [tile(i, at) for i in range(Q)]
    out = [own[0]]
    for i in range(1, Q):
        step_z, step_y, step_x = VELOCITIES[i]
        source = own[i] if step_y == 0 else tile(i, at - step_y)
        source = roll(source, step_z, step_x)
        out.append(jnp.where(source == SOLID, own[OPPOSITE[i]], source))
    return out


def relax_row(tile, at):
    wet = tile(0, at) != SOLID
    return relax_wet(stream_row(tile, at), wet)


def stream_patch(values):
    out = [values[0]]
    for i in range(1, Q):
        step_z, step_y, step_x = VELOCITIES[i]
        source = roll(values[i], step_z, 8 * step_y + step_x)
        out.append(jnp.where(source == SOLID, values[OPPOSITE[i]], source))
    return out


def gather_columns(values, rows):
    lane_row = lanes() // 8
    tile = jnp.full((8, 128), SOLID, F32)
    for row, value in zip(rows, values):
        tile = jnp.where(lane_row == row, roll(value, 0, 8 * row + 4), tile)
    return tile


def split_slabs(relative, fluid, new_owner, low, high, moved, kinds, owner, sems):
    copies = [
        pltpu.make_async_copy(fluid, kinds, sems.at[0]),
        pltpu.make_async_copy(relative.at[:, 2:4], high.at[0:Q], sems.at[1]),
        pltpu.make_async_copy(relative.at[:, 0:2], low.at[0:Q], sems.at[2]),
        pltpu.make_async_copy(new_owner, owner, sems.at[3]),
    ]
    for copy in copies:
        copy.start()
    copies[3].wait()
    place = lax.axis_index("gz")
    moved[0] = jnp.full((8, 128), jnp.where((owner[0, 0] == place - 1) & (place > 0), 1.0, 0.0), F32)
    inside = place < lax.axis_size("gz") - 1
    moved[1] = jnp.full((8, 128), jnp.where((owner[0, 1] == place + 1) & inside, 1.0, 0.0), F32)
    copies[0].wait()
    low[Q] = kinds[0:2].astype(F32)
    high[Q] = kinds[2:4].astype(F32)
    copies[1].wait()
    copies[2].wait()


def first_relax(high, low, above, below, moved, own, ahead, back, turn, stage):
    place = lax.axis_index("gz")
    at_low = place == 0
    at_high = place == lax.axis_size("gz") - 1
    swap_low = moved[0] > 0.5
    swap_high = moved[1] > 0.5
    for k in range(2):
        turn[Q, 8 * k : 8 * k + 8] = jnp.where(at_low, 0.0, below[Q, k])
        turn[Q, 8 * (k + 2) : 8 * (k + 3)] = low[Q, k]
        turn[Q, 8 * (k + 4) : 8 * (k + 5)] = high[Q, k]
        turn[Q, 8 * (k + 6) : 8 * (k + 7)] = jnp.where(at_high, 0.0, above[Q, k])
    for i in range(Q):
        for k in range(2):
            mine, other = low[i, k], below[i, k]
            turn[i, 8 * k : 8 * k + 8] = jnp.where(swap_low, mine, other)
            turn[i, 8 * (k + 2) : 8 * (k + 3)] = jnp.where(swap_low, other, mine)
            mine, other = high[i, k], above[i, k]
            turn[i, 8 * (k + 4) : 8 * (k + 5)] = jnp.where(swap_high, other, mine)
            turn[i, 8 * (k + 6) : 8 * (k + 7)] = jnp.where(swap_high, mine, other)
    for row in range(8):
        wet = turn[Q, pl.ds(row, 8, stride=8)] > 0.5
        values = relax_wet([turn[i, pl.ds(row, 8, stride=8)] for i in range(Q)], wet)
        for i in range(Q):
            own[i, row] = values[i]
    up = place % 2 == 0
    for side, (message, high_rows) in enumerate(((ahead, up), (back, jnp.logical_not(up)))):
        first = jnp.where(high_rows, 5, 0)
        far = jnp.where(high_rows, 4, 3)
        for i in range(Q):
            for k in range(3):
                at = 8 * (Y_FIRST[i] + k)
                stage[side, at : at + 8] = own[i, first + k]
        for k in range(5):
            at = 8 * Y_FAR[k]
            stage[side, at : at + 8] = own[jnp.where(high_rows, UP_Y[k], DOWN_Y[k]), far]
        stage[side, 8 * 62 :] = jnp.full((16, 128), SOLID, F32)
        for group in range(8):
            for layer in range(1, 7):
                message[6 * group + layer - 1] = stage[side, pl.ds(64 * group + layer, 8, stride=8)]
        for group in range(2):
            message[48 + group] = stage[side, pl.ds(64 * group, 8, stride=8)]
            message[50 + group] = stage[side, pl.ds(64 * (group + 2) + 7, 8, stride=8)]


def join_rows(own, ahead, back, main, edge, x_ahead, x_back, stage):
    place = lax.axis_index("gy")
    up = lax.axis_index("gz") % 2 == 0
    outside_low = place == 0
    outside_high = place == lax.axis_size("gy") - 1
    for i in range(Q):
        main[i, 0] = jnp.full((8, 128), SOLID, F32)
        main[i, 15] = jnp.full((8, 128), SOLID, F32)
    for side, (message, low_rows) in enumerate(((ahead, up), (back, jnp.logical_not(up)))):
        outside = jnp.where(low_rows, outside_low, outside_high)
        first = jnp.where(low_rows, 1, 12)
        far = jnp.where(low_rows, 0, 15)
        stage[side] = jnp.full((512, 128), SOLID, F32)
        for group in range(8):
            for layer in range(1, 7):
                stage[side, pl.ds(64 * group + layer, 8, stride=8)] = message[6 * group + layer - 1]
        for group in range(2):
            stage[side, pl.ds(64 * group, 8, stride=8)] = message[48 + group]
            stage[side, pl.ds(64 * (group + 2) + 7, 8, stride=8)] = message[50 + group]
        for i in range(Q):
            for k in range(3):
                at = 8 * (Y_FIRST[i] + k)
                main[i, first + k] = jnp.where(outside, SOLID, stage[side, at : at + 8])
        for k in range(5):
            at = 8 * Y_FAR[k]
            value = jnp.where(outside, SOLID, stage[side, at : at + 8])
            main[jnp.where(low_rows, UP_Y[k], DOWN_Y[k]), far] = value
    edges = []
    for i in range(Q):
        rows = [own[i, k] for k in range(8)]
        for k in range(8):
            main[i, 4 + k] = rows[k]
        rows = [main[i, k] for k in range(4)] + rows + [main[i, k] for k in range(12, 16)]
        edges.append(gather_columns(rows, range(16)))
        edge[i] = edges[i]
    low_side = lanes() % 8 < 4
    for i in range(10):
        if i + 10 < Q:
            to_low = jnp.where(low_side, roll(edges[i + 10], 0, -4), edges[i])
            to_high = jnp.where(low_side, edges[i], roll(edges[i + 10], 0, 4))
            x_ahead[i] = jnp.where(up, to_high, to_low)
            x_back[i] = jnp.where(up, to_low, to_high)
        else:
            x_ahead[i] = edges[i]
            x_back[i] = edges[i]


def two_steps(main, out, edge, middle):
    def first(row):
        values = relax_row(lambda i, at: main[i, at], row)
        for i in range(Q):
            middle[i, row - 1] = values[i]

    def second(row):
        values = relax_row(lambda i, at: middle[i, at], row - 1)
        for i in range(Q):
            out[i, row - 2] = values[i]

    for row in range(1, 15):
        first(row)
    for row in range(2, 14):
        second(row)
    for i in range(Q):
        edge[i] = gather_columns([out[i, k] for k in range(12)], range(2, 14))


def patch_two_steps(inner, inner_edge, edge, ahead, back, flat, below, above):
    up = lax.axis_index("gz") % 2 == 0
    place = lax.axis_index("gx")
    at_low = place == 0
    at_high = place == lax.axis_size("gx") - 1
    column = lanes() % 8
    low_side = column < 4
    sides = []
    for side in range(2):
        values = []
        for i in range(Q):
            message = jnp.where(up == (side == 0), ahead[i % 10], back[i % 10])
            if i >= 10:
                message = roll(message, 0, (-4, 4)[side])
            message = jnp.where((at_low, at_high)[side], SOLID, message)
            if side == 0:
                values.append(jnp.where(low_side, message, edge[i]))
            else:
                values.append(jnp.where(low_side, edge[i], message))
        for step in range(2):
            wet = values[0] != SOLID
            values = relax_wet(stream_patch(values), wet)
        sides.append(values)
    lane = lanes()
    seam = (lane < 2) | (lane >= 126)
    for i in range(Q):
        own_columns = jnp.where(low_side, sides[1][i], sides[0][i])
        first = PER_SLOT * SLOT[i]
        for row in range(12):
            value = jnp.where(seam, roll(own_columns, 0, -(8 * (row + 2) + 4)), inner[i, row])
            flat[8 * (first + row) : 8 * (first + row) + 8] = value
        fresh = inner_edge[i]
        for side in range(2):
            stale = (column < 6) if side == 0 else (column >= 2)
            at = 8 * (first + 12 + side)
            flat[at : at + 8] = jnp.where(stale, sides[side][i], fresh)
    flat[8 * PER_SLOT * Q :] = jnp.full((FLAT_ROWS - 8 * PER_SLOT * Q, 128), SOLID, F32)
    for group in range(NEAR):
        above[group] = flat[pl.ds(64 * group + 5, 8, stride=8)]
        below[group] = flat[pl.ds(64 * group + 2, 8, stride=8)]
    for group in range(FAR):
        above[NEAR + group] = flat[pl.ds(64 * group + 4, 8, stride=8)]
        below[NEAR + group] = flat[pl.ds(8 * 5 * PER_SLOT + 64 * group + 3, 8, stride=8)]


def last_two_steps(
    flat_in, below, above, block_fluid, out, block_density, flat, middle, turn, final, wet_count, sems
):
    count_copy = pltpu.make_async_copy(block_fluid, wet_count, sems.at[2])
    count_copy.start()
    place = lax.axis_index("gz")
    at_low = place == 0
    at_high = place == lax.axis_size("gz") - 1
    lane = lanes()
    low_side = lane % 8 < 4
    for group in range(NEAR):
        flat[pl.ds(64 * group + 1, 8, stride=8)] = jnp.where(at_low, SOLID, below[group])
        flat[pl.ds(64 * group + 6, 8, stride=8)] = jnp.where(at_high, SOLID, above[group])
    for group in range(FAR):
        flat[pl.ds(64 * group, 8, stride=8)] = jnp.where(at_low, SOLID, below[NEAR + group])
        flat[pl.ds(8 * 5 * PER_SLOT + 64 * group + 7, 8, stride=8)] = jnp.where(
            at_high, SOLID, above[NEAR + group]
        )

    def joined(i, at):
        return flat[pl.ds(8 * (PER_SLOT * SLOT[i] + at), 8)]

    def third(row):
        values = relax_row(joined, row - 2)
        for i in range(Q):
            middle[i, row - 3] = values[i]

    for row in range(3, 13):
        third(row)
    patches = []
    for side in range(2):
        values = [joined(i, 12 + side) for i in range(Q)]
        wet = values[0] != SOLID
        values = relax_wet(stream_patch(values), wet)
        patches.append(stream_patch(values))
    own_columns = [jnp.where(low_side, patches[1][i], patches[0][i]) for i in range(Q)]
    seam = (lane < 2) | (lane >= 126)
    for row in range(8):
        wet = middle[0, row + 1] != SOLID
        values = stream_row(lambda i, at: middle[i, at], row + 1)
        for i in range(Q):
            value = jnp.where(seam, roll(own_columns[i], 0, -(8 * (row + 4) + 4)), values[i])
            turn[i, 8 * row : 8 * row + 8] = jnp.where(wet, value, 0.0)
    copies = []
    masses = []
    for slot in range(2):
        mass = None
        for k in range(2):
            layer = 2 * slot + k
            values = [turn[i, pl.ds(layer + 2, 8, stride=8)] for i in range(Q)]
            for i in range(Q):
                final[i, layer] = values[i]
            axis_sum = functools.reduce(jnp.add, values[1:7])
            edge_sum = functools.reduce(jnp.add, values[7:])
            density = values[0] * (1.0 / 3.0) + axis_sum * (1.0 / 18.0) + edge_sum * (1.0 / 36.0)
            mass = density if mass is None else mass + density
        masses.append(mass)
        layers = slice(2 * slot, 2 * slot + 2)
        copies.append(pltpu.make_async_copy(final.at[:, layers], out.at[:, layers], sems.at[slot]))
        copies[slot].start()
    count_copy.wait()
    for slot in range(2):
        count = jnp.maximum(wet_count[0, slot], 1).astype(F32)
        block_density[0, slot] = jnp.sum(masses[slot]) / count
    for copy in copies:
        copy.wait()


def ring_exchange(to_low, to_high, axis):
    count = lax.axis_size(axis)
    up = [(i, (i + 1) % count) for i in range(count)]
    down = [(target, source) for source, target in up]
    return lax.ppermute(to_high, axis, up), lax.ppermute(to_low, axis, down)


def loop_exchange(ahead, back, axis):
    count = lax.axis_size(axis)
    layers = lax.axis_size("gz")
    pairs = []
    for i in range(count):
        for layer in range(layers):
            if layer % 2 == 0:
                target = (i + 1, layer) if i < count - 1 else (i, layer + 1)
            else:
                target = (i - 1, layer) if i > 0 else (i, layer - 1)
            pairs.append((i * layers + layer, target[0] * layers + target[1]))
    inverse = [(target, source) for source, target in pairs]
    axes = (axis, "gz")
    return lax.ppermute(ahead, axes, pairs), lax.ppermute(back, axes, inverse)


def call(kernel, outs, in_specs, out_specs=None, scratch=(), aliases=None, vmem=32):
    if out_specs is None:
        out_specs = [VMEM] * len(outs)
    return pl.pallas_call(
        kernel,
        out_shape=outs,
        in_specs=in_specs,
        out_specs=out_specs,
        scratch_shapes=list(scratch),
        input_output_aliases=aliases or {},
        compiler_params=pltpu.CompilerParams(vmem_limit_bytes=vmem * 1024 * 1024),
    )


def in_hbm(array):
    return pltpu.with_memory_space_constraint(array, pltpu.HBM)


def on_device(relative, fluid, block_fluid, new_owner):
    low, high, moved = call(
        split_slabs,
        [shape(Q + 1, 2, 8, 128), shape(Q + 1, 2, 8, 128), shape(2, 8, 128)],
        [HBM] * 3,
        scratch=[
            pltpu.VMEM((4, 8, 128), jnp.int32),
            pltpu.SMEM((1, 2), jnp.int32),
            pltpu.SemaphoreType.DMA((4,)),
        ],
    )(in_hbm(relative), in_hbm(fluid), in_hbm(new_owner.transpose(1, 2, 0).reshape(1, 2)))
    below, above = ring_exchange(low, high, "gz")
    own, ahead, back = call(
        first_relax,
        [shape(Q, 8, 8, 128), shape(Y_TILES, 8, 128), shape(Y_TILES, 8, 128)],
        [VMEM] * 5,
        scratch=[pltpu.VMEM((Q + 1, 64, 128), F32), pltpu.VMEM((2, 512, 128), F32)],
    )(high, low, above, below, moved)
    ahead, back = loop_exchange(ahead, back, "gy")
    main, edge, x_ahead, x_back = call(
        join_rows,
        [shape(Q, 16, 8, 128), shape(Q, 8, 128), shape(10, 8, 128), shape(10, 8, 128)],
        [VMEM] * 3,
        scratch=[pltpu.VMEM((2, 512, 128), F32)],
    )(own, ahead, back)
    x_ahead, x_back = loop_exchange(x_ahead, x_back, "gx")
    inner, inner_edge = call(
        two_steps,
        [shape(Q, 12, 8, 128), shape(Q, 8, 128)],
        [VMEM],
        scratch=[pltpu.VMEM((Q, 14, 8, 128), F32)],
    )(main)
    flat, z_low, z_high = call(
        patch_two_steps,
        [shape(FLAT_ROWS, 128), shape(NEAR + FAR, 8, 128), shape(NEAR + FAR, 8, 128)],
        [VMEM] * 5,
    )(inner, inner_edge, edge, x_ahead, x_back)
    below, above = ring_exchange(z_low, z_high, "gz")
    out, block_density, _ = call(
        last_two_steps,
        [shape(Q, 4, 8, 128), shape(1, 2), shape(FLAT_ROWS, 128)],
        [VMEM] * 3 + [HBM],
        [HBM, SMEM, VMEM],
        scratch=[
            pltpu.VMEM((Q, 10, 8, 128), F32),
            pltpu.VMEM((Q, 64, 128), F32),
            pltpu.VMEM((Q, 4, 8, 128), F32),
            pltpu.SMEM((1, 2), jnp.int32),
            pltpu.SemaphoreType.DMA((3,)),
        ],
        aliases={0: 2},
    )(flat, below, above, in_hbm(block_fluid.transpose(1, 2, 0).reshape(1, 2)))
    return out, block_density.reshape(1, 1, 2).transpose(2, 0, 1)


def solution(mesh):
    return jax.shard_map(
        on_device,
        mesh=mesh,
        in_specs=(
            P(None, "gz", "gy", "gx"),
            P("gz", "gy", "gx"),
            P("gz", "gy", "gx"),
            P("gz", "gy", "gx"),
        ),
        out_specs=(P(None, "gz", "gy", "gx"), P("gz", "gy", "gx")),
        check_vma=False,
    )
```

```python
import functools

import jax
import jax.numpy as jnp
from jax import lax
from jax.experimental import pallas as pl
from jax.experimental.pallas import tpu as pltpu
from jax.sharding import PartitionSpec as P


VELOCITIES = [
    (0, 0, 0),
    (1, 0, 0),
    (-1, 0, 0),
    (0, 1, 0),
    (0, -1, 0),
    (0, 0, 1),
    (0, 0, -1),
    (1, 1, 0),
    (-1, -1, 0),
    (1, -1, 0),
    (-1, 1, 0),
    (1, 0, 1),
    (-1, 0, -1),
    (1, 0, -1),
    (-1, 0, 1),
    (0, 1, 1),
    (0, -1, -1),
    (0, 1, -1),
    (0, -1, 1),
]
OPPOSITE = [0, 2, 1, 4, 3, 6, 5, 8, 7, 10, 9, 12, 11, 14, 13, 16, 15, 18, 17]
Q = 19
SOLID = 3.0e38
Z_ORDER = sorted(range(Q), key=lambda i: {1: 0, -1: 1, 0: 2}[VELOCITIES[i][0]])
SLOT = [Z_ORDER.index(i) for i in range(Q)]
UP_Y = [i for i in Z_ORDER if VELOCITIES[i][1] == 1]
DOWN_Y = [i for i in Z_ORDER if VELOCITIES[i][1] == -1]
Y_FIRST = [3 * s + min(s // 5, 2) for s in SLOT]
Y_FAR = [15, 31, 59, 60, 61]
Y_TILES = 52
PER_SLOT = 14
NEAR = 34
FAR = 9
FLAT_ROWS = 8 * 8 * NEAR
F32 = jnp.float32
VMEM = pl.BlockSpec(memory_space=pltpu.VMEM)
SMEM = pl.BlockSpec(memory_space=pltpu.SMEM)
HBM = pl.BlockSpec(memory_space=pltpu.HBM)


def shape(*dims):
    return jax.ShapeDtypeStruct(dims, F32)


def lanes():
    return lax.broadcasted_iota(jnp.int32, (8, 128), 1)


def sublanes():
    return lax.broadcasted_iota(jnp.int32, (8, 128), 0)


def roll(value, sublane_shift, lane_shift):
    if sublane_shift % 8:
        value = pltpu.roll(value, sublane_shift % 8, 0)
    if lane_shift % 128:
        value = pltpu.roll(value, lane_shift % 128, 1)
    return value


def relax(g):
    sums = [g[k] + g[k + 1] for k in range(1, Q, 2)]
    diffs = [g[k] - g[k + 1] for k in range(1, Q, 2)]
    axis_sum = sums[0] + sums[1] + sums[2]
    edge_sum = (sums[3] + sums[4]) + (sums[5] + sums[6]) + (sums[7] + sums[8])
    density = 12.0 * g[0] + 2.0 * axis_sum + edge_sum
    moment_z = 2.0 * diffs[0] + ((diffs[3] + diffs[4]) + (diffs[5] + diffs[6]))
    moment_y = 2.0 * diffs[1] + ((diffs[3] - diffs[4]) + (diffs[7] + diffs[8]))
    moment_x = 2.0 * diffs[2] + ((diffs[5] - diffs[6]) + (diffs[7] - diffs[8]))
    inverse = 1.0 / density
    speed = [moment_z * inverse, moment_y * inverse, moment_x * inverse]
    square = speed[0] * speed[0] + speed[1] * speed[1] + speed[2] * speed[2]
    scaled = density * (1.5 / 36.0)
    base = scaled * (1.0 - 1.5 * square)
    linear = [(4.5 / 36.0) * m for m in (moment_z, moment_y, moment_x)]
    speed = [1.5 * s for s in speed]
    out = [base - 0.5 * g[0]]
    for pair in range(9):
        velocity = VELOCITIES[1 + 2 * pair]
        along = None
        twice = None
        for axis in range(3):
            if velocity[axis] == 0:
                continue
            if along is None:
                along, twice = linear[axis], speed[axis]
            elif velocity[axis] > 0:
                along, twice = along + linear[axis], twice + speed[axis]
            else:
                along, twice = along - linear[axis], twice - speed[axis]
        even = base + along * twice - 0.25 * sums[pair]
        odd = along - 0.25 * diffs[pair]
        out += [even + odd, even - odd]
    return out


def relax_wet(g, wet):
    return [jnp.where(wet, value, SOLID) for value in relax(g)]


def stream_row(tile, at):
    own = [tile(i, at) for i in range(Q)]
    out = [own[0]]
    for i in range(1, Q):
        step_z, step_y, step_x = VELOCITIES[i]
        source = own[i] if step_y == 0 else tile(i, at - step_y)
        source = roll(source, step_z, step_x)
        out.append(jnp.where(source == SOLID, own[OPPOSITE[i]], source))
    return out


def relax_row(tile, at):
    wet = tile(0, at) != SOLID
    return relax_wet(stream_row(tile, at), wet)


def stream_patch(values):
    out = [values[0]]
    for i in range(1, Q):
        step_z, step_y, step_x = VELOCITIES[i]
        source = roll(values[i], step_z, 8 * step_y + step_x)
        out.append(jnp.where(source == SOLID, values[OPPOSITE[i]], source))
    return out


def gather_columns(values, rows):
    lane_row = lanes() // 8
    tile = jnp.full((8, 128), SOLID, F32)
    for row, value in zip(rows, values):
        tile = jnp.where(lane_row == row, roll(value, 0, 8 * row + 4), tile)
    return tile


def split_slabs(relative, fluid, new_owner, far, near, moved, kinds, owner, sems):
    place = lax.axis_index("gz")
    far_first = 2 * lax.rem(place, 2)
    near_first = 2 - far_first
    copies = [
        pltpu.make_async_copy(fluid, kinds, sems.at[0]),
        pltpu.make_async_copy(relative.at[:, pl.ds(far_first, 2)], far.at[0:Q], sems.at[1]),
        pltpu.make_async_copy(relative.at[:, pl.ds(near_first, 2)], near.at[0:Q], sems.at[2]),
        pltpu.make_async_copy(new_owner, owner, sems.at[3]),
    ]
    for copy in copies:
        copy.start()
    copies[3].wait()
    moved[0] = jnp.full((8, 128), jnp.where((owner[0, 0] == place - 1) & (place > 0), 1.0, 0.0), F32)
    inside = place < lax.axis_size("gz") - 1
    moved[1] = jnp.full((8, 128), jnp.where((owner[0, 1] == place + 1) & inside, 1.0, 0.0), F32)
    copies[0].wait()
    far[Q] = kinds[pl.ds(far_first, 2)].astype(F32)
    near[Q] = kinds[pl.ds(near_first, 2)].astype(F32)
    copies[1].wait()
    copies[2].wait()


def first_relax(far, near, got_far, got_near, moved, own, ahead, back, turn, stage):
    place = lax.axis_index("gz")
    at_low = place == 0
    at_high = place == lax.axis_size("gz") - 1
    even = lax.rem(place, 2) == 0
    swap_low = moved[0] > 0.5
    swap_high = moved[1] > 0.5

    def slabs(i, k):
        low = jnp.where(even, far[i, k], near[i, k])
        high = jnp.where(even, near[i, k], far[i, k])
        below = jnp.where(even, got_far[i, k], got_near[i, k])
        above = jnp.where(even, got_near[i, k], got_far[i, k])
        return low, high, below, above

    for k in range(2):
        low, high, below, above = slabs(Q, k)
        turn[Q, 8 * k : 8 * k + 8] = jnp.where(at_low, 0.0, below)
        turn[Q, 8 * (k + 2) : 8 * (k + 3)] = low
        turn[Q, 8 * (k + 4) : 8 * (k + 5)] = high
        turn[Q, 8 * (k + 6) : 8 * (k + 7)] = jnp.where(at_high, 0.0, above)
    for i in range(Q):
        for k in range(2):
            low, high, below, above = slabs(i, k)
            turn[i, 8 * k : 8 * k + 8] = jnp.where(swap_low, low, below)
            turn[i, 8 * (k + 2) : 8 * (k + 3)] = jnp.where(swap_low, below, low)
            turn[i, 8 * (k + 4) : 8 * (k + 5)] = jnp.where(swap_high, above, high)
            turn[i, 8 * (k + 6) : 8 * (k + 7)] = jnp.where(swap_high, high, above)
    for row in range(8):
        wet = turn[Q, pl.ds(row, 8, stride=8)] > 0.5
        values = relax_wet([turn[i, pl.ds(row, 8, stride=8)] for i in range(Q)], wet)
        for i in range(Q):
            own[i, row] = values[i]
    up = even
    for side, (message, high_rows) in enumerate(((ahead, up), (back, jnp.logical_not(up)))):
        first = jnp.where(high_rows, 5, 0)
        far = jnp.where(high_rows, 4, 3)
        for i in range(Q):
            for k in range(3):
                at = 8 * (Y_FIRST[i] + k)
                stage[side, at : at + 8] = own[i, first + k]
        for k in range(5):
            at = 8 * Y_FAR[k]
            stage[side, at : at + 8] = own[jnp.where(high_rows, UP_Y[k], DOWN_Y[k]), far]
        stage[side, 8 * 62 :] = jnp.full((16, 128), SOLID, F32)
        for group in range(8):
            for layer in range(1, 7):
                message[6 * group + layer - 1] = stage[side, pl.ds(64 * group + layer, 8, stride=8)]
        for group in range(2):
            message[48 + group] = stage[side, pl.ds(64 * group, 8, stride=8)]
            message[50 + group] = stage[side, pl.ds(64 * (group + 2) + 7, 8, stride=8)]


def join_rows(own, ahead, back, main, edge, x_ahead, x_back, stage):
    place = lax.axis_index("gy")
    up = lax.axis_index("gz") % 2 == 0
    outside_low = place == 0
    outside_high = place == lax.axis_size("gy") - 1
    for i in range(Q):
        main[i, 0] = jnp.full((8, 128), SOLID, F32)
        main[i, 15] = jnp.full((8, 128), SOLID, F32)
    for side, (message, low_rows) in enumerate(((ahead, up), (back, jnp.logical_not(up)))):
        outside = jnp.where(low_rows, outside_low, outside_high)
        first = jnp.where(low_rows, 1, 12)
        far = jnp.where(low_rows, 0, 15)
        stage[side] = jnp.full((512, 128), SOLID, F32)
        for group in range(8):
            for layer in range(1, 7):
                stage[side, pl.ds(64 * group + layer, 8, stride=8)] = message[6 * group + layer - 1]
        for group in range(2):
            stage[side, pl.ds(64 * group, 8, stride=8)] = message[48 + group]
            stage[side, pl.ds(64 * (group + 2) + 7, 8, stride=8)] = message[50 + group]
        for i in range(Q):
            for k in range(3):
                at = 8 * (Y_FIRST[i] + k)
                main[i, first + k] = jnp.where(outside, SOLID, stage[side, at : at + 8])
        for k in range(5):
            at = 8 * Y_FAR[k]
            value = jnp.where(outside, SOLID, stage[side, at : at + 8])
            main[jnp.where(low_rows, UP_Y[k], DOWN_Y[k]), far] = value
    edges = []
    for i in range(Q):
        rows = [own[i, k] for k in range(8)]
        for k in range(8):
            main[i, 4 + k] = rows[k]
        rows = [main[i, k] for k in range(4)] + rows + [main[i, k] for k in range(12, 16)]
        edges.append(gather_columns(rows, range(16)))
        edge[i] = edges[i]
    low_side = lanes() % 8 < 4
    for i in range(10):
        if i + 10 < Q:
            to_low = jnp.where(low_side, roll(edges[i + 10], 0, -4), edges[i])
            to_high = jnp.where(low_side, edges[i], roll(edges[i + 10], 0, 4))
            x_ahead[i] = jnp.where(up, to_high, to_low)
            x_back[i] = jnp.where(up, to_low, to_high)
        else:
            x_ahead[i] = edges[i]
            x_back[i] = edges[i]


def two_steps(main, out, edge, middle):
    def first(row):
        values = relax_row(lambda i, at: main[i, at], row)
        for i in range(Q):
            middle[i, row - 1] = values[i]

    def second(row):
        values = relax_row(lambda i, at: middle[i, at], row - 1)
        for i in range(Q):
            out[i, row - 2] = values[i]

    for row in range(1, 15):
        first(row)
    for row in range(2, 14):
        second(row)
    for i in range(Q):
        edge[i] = gather_columns([out[i, k] for k in range(12)], range(2, 14))


def patch_two_steps(inner, inner_edge, edge, ahead, back, flat, far, near):
    up = lax.axis_index("gz") % 2 == 0
    place = lax.axis_index("gx")
    at_low = place == 0
    at_high = place == lax.axis_size("gx") - 1
    column = lanes() % 8
    low_side = column < 4
    sides = []
    for side in range(2):
        values = []
        for i in range(Q):
            message = jnp.where(up == (side == 0), ahead[i % 10], back[i % 10])
            if i >= 10:
                message = roll(message, 0, (-4, 4)[side])
            message = jnp.where((at_low, at_high)[side], SOLID, message)
            if side == 0:
                values.append(jnp.where(low_side, message, edge[i]))
            else:
                values.append(jnp.where(low_side, edge[i], message))
        for step in range(2):
            wet = values[0] != SOLID
            values = relax_wet(stream_patch(values), wet)
        sides.append(values)
    lane = lanes()
    seam = (lane < 2) | (lane >= 126)
    for i in range(Q):
        own_columns = jnp.where(low_side, sides[1][i], sides[0][i])
        first = PER_SLOT * SLOT[i]
        for row in range(12):
            value = jnp.where(seam, roll(own_columns, 0, -(8 * (row + 2) + 4)), inner[i, row])
            flat[8 * (first + row) : 8 * (first + row) + 8] = value
        fresh = inner_edge[i]
        for side in range(2):
            stale = (column < 6) if side == 0 else (column >= 2)
            at = 8 * (first + 12 + side)
            flat[at : at + 8] = jnp.where(stale, sides[side][i], fresh)
    flat[8 * PER_SLOT * Q :] = jnp.full((FLAT_ROWS - 8 * PER_SLOT * Q, 128), SOLID, F32)
    for group in range(NEAR + FAR):
        if group < NEAR:
            to_low = flat[pl.ds(64 * group + 2, 8, stride=8)]
            to_high = flat[pl.ds(64 * group + 5, 8, stride=8)]
        else:
            to_low = flat[pl.ds(8 * 5 * PER_SLOT + 64 * (group - NEAR) + 3, 8, stride=8)]
            to_high = flat[pl.ds(64 * (group - NEAR) + 4, 8, stride=8)]
        far[group] = jnp.where(up, to_low, to_high)
        near[group] = jnp.where(up, to_high, to_low)


def last_two_steps(
    flat_in, far, near, block_fluid, out, block_density, flat, middle, turn, final, wet_count, sems
):
    count_copy = pltpu.make_async_copy(block_fluid, wet_count, sems.at[2])
    count_copy.start()
    place = lax.axis_index("gz")
    at_low = place == 0
    at_high = place == lax.axis_size("gz") - 1
    lane = lanes()
    low_side = lane % 8 < 4
    even = lax.rem(place, 2) == 0
    for group in range(NEAR + FAR):
        below = jnp.where(at_low, SOLID, jnp.where(even, far[group], near[group]))
        above = jnp.where(at_high, SOLID, jnp.where(even, near[group], far[group]))
        if group < NEAR:
            flat[pl.ds(64 * group + 1, 8, stride=8)] = below
            flat[pl.ds(64 * group + 6, 8, stride=8)] = above
        else:
            flat[pl.ds(64 * (group - NEAR), 8, stride=8)] = below
            flat[pl.ds(8 * 5 * PER_SLOT + 64 * (group - NEAR) + 7, 8, stride=8)] = above

    def joined(i, at):
        return flat[pl.ds(8 * (PER_SLOT * SLOT[i] + at), 8)]

    def third(row):
        values = relax_row(joined, row - 2)
        for i in range(Q):
            middle[i, row - 3] = values[i]

    for row in range(3, 13):
        third(row)
    patches = []
    for side in range(2):
        values = [joined(i, 12 + side) for i in range(Q)]
        wet = values[0] != SOLID
        values = relax_wet(stream_patch(values), wet)
        patches.append(stream_patch(values))
    own_columns = [jnp.where(low_side, patches[1][i], patches[0][i]) for i in range(Q)]
    seam = (lane < 2) | (lane >= 126)
    for row in range(8):
        wet = middle[0, row + 1] != SOLID
        values = stream_row(lambda i, at: middle[i, at], row + 1)
        for i in range(Q):
            value = jnp.where(seam, roll(own_columns[i], 0, -(8 * (row + 4) + 4)), values[i])
            turn[i, 8 * row : 8 * row + 8] = jnp.where(wet, value, 0.0)
    copies = []
    masses = []
    for slot in range(2):
        mass = None
        for k in range(2):
            layer = 2 * slot + k
            values = [turn[i, pl.ds(layer + 2, 8, stride=8)] for i in range(Q)]
            for i in range(Q):
                final[i, layer] = values[i]
            axis_sum = functools.reduce(jnp.add, values[1:7])
            edge_sum = functools.reduce(jnp.add, values[7:])
            density = values[0] * (1.0 / 3.0) + axis_sum * (1.0 / 18.0) + edge_sum * (1.0 / 36.0)
            mass = density if mass is None else mass + density
        masses.append(mass)
        layers = slice(2 * slot, 2 * slot + 2)
        copies.append(pltpu.make_async_copy(final.at[:, layers], out.at[:, layers], sems.at[slot]))
        copies[slot].start()
    count_copy.wait()
    for slot in range(2):
        count = jnp.maximum(wet_count[0, slot], 1).astype(F32)
        block_density[0, slot] = jnp.sum(masses[slot]) / count
    for copy in copies:
        copy.wait()


def layer_exchange(far, near):
    count = lax.axis_size("gz")
    swap = [(i, i + 1 - 2 * (i % 2)) for i in range(count)]
    cycle = []
    for i in range(count):
        if i % 2 == 0:
            cycle.append((i, i + 2 if i + 2 < count else i + 1))
        else:
            cycle.append((i, i - 2 if i - 2 >= 0 else i - 1))
    far = lax.ppermute(far, "gz", swap)
    far, near = lax.optimization_barrier((far, near))
    far = lax.ppermute(far, "gz", cycle)
    near = lax.ppermute(near, "gz", swap)
    return far, near


def loop_exchange(ahead, back, axis):
    count = lax.axis_size(axis)
    layers = lax.axis_size("gz")
    pairs = []
    for i in range(count):
        for layer in range(layers):
            if layer % 2 == 0:
                target = (i + 1, layer) if i < count - 1 else (i, layer + 1)
            else:
                target = (i - 1, layer) if i > 0 else (i, layer - 1)
            pairs.append((i * layers + layer, target[0] * layers + target[1]))
    inverse = [(target, source) for source, target in pairs]
    axes = (axis, "gz")
    return lax.ppermute(ahead, axes, pairs), lax.ppermute(back, axes, inverse)


def call(kernel, outs, in_specs, out_specs=None, scratch=(), aliases=None, vmem=32):
    if out_specs is None:
        out_specs = [VMEM] * len(outs)
    return pl.pallas_call(
        kernel,
        out_shape=outs,
        in_specs=in_specs,
        out_specs=out_specs,
        scratch_shapes=list(scratch),
        input_output_aliases=aliases or {},
        compiler_params=pltpu.CompilerParams(vmem_limit_bytes=vmem * 1024 * 1024),
    )


def in_hbm(array):
    return pltpu.with_memory_space_constraint(array, pltpu.HBM)


def on_device(relative, fluid, block_fluid, new_owner):
    far, near, moved = call(
        split_slabs,
        [shape(Q + 1, 2, 8, 128), shape(Q + 1, 2, 8, 128), shape(2, 8, 128)],
        [HBM] * 3,
        scratch=[
            pltpu.VMEM((4, 8, 128), jnp.int32),
            pltpu.SMEM((1, 2), jnp.int32),
            pltpu.SemaphoreType.DMA((4,)),
        ],
    )(in_hbm(relative), in_hbm(fluid), in_hbm(new_owner.transpose(1, 2, 0).reshape(1, 2)))
    got_far, got_near = layer_exchange(far, near)
    own, ahead, back = call(
        first_relax,
        [shape(Q, 8, 8, 128), shape(Y_TILES, 8, 128), shape(Y_TILES, 8, 128)],
        [VMEM] * 5,
        scratch=[pltpu.VMEM((Q + 1, 64, 128), F32), pltpu.VMEM((2, 512, 128), F32)],
    )(far, near, got_far, got_near, moved)
    ahead, back = loop_exchange(ahead, back, "gy")
    main, edge, x_ahead, x_back = call(
        join_rows,
        [shape(Q, 16, 8, 128), shape(Q, 8, 128), shape(10, 8, 128), shape(10, 8, 128)],
        [VMEM] * 3,
        scratch=[pltpu.VMEM((2, 512, 128), F32)],
    )(own, ahead, back)
    x_ahead, x_back = loop_exchange(x_ahead, x_back, "gx")
    inner, inner_edge = call(
        two_steps,
        [shape(Q, 12, 8, 128), shape(Q, 8, 128)],
        [VMEM],
        scratch=[pltpu.VMEM((Q, 14, 8, 128), F32)],
    )(main)
    flat, far, near = call(
        patch_two_steps,
        [shape(FLAT_ROWS, 128), shape(NEAR + FAR, 8, 128), shape(NEAR + FAR, 8, 128)],
        [VMEM] * 5,
    )(inner, inner_edge, edge, x_ahead, x_back)
    far, near = layer_exchange(far, near)
    out, block_density, _ = call(
        last_two_steps,
        [shape(Q, 4, 8, 128), shape(1, 2), shape(FLAT_ROWS, 128)],
        [VMEM] * 3 + [HBM],
        [HBM, SMEM, VMEM],
        scratch=[
            pltpu.VMEM((Q, 10, 8, 128), F32),
            pltpu.VMEM((Q, 64, 128), F32),
            pltpu.VMEM((Q, 4, 8, 128), F32),
            pltpu.SMEM((1, 2), jnp.int32),
            pltpu.SemaphoreType.DMA((3,)),
        ],
        aliases={0: 2},
    )(flat, far, near, in_hbm(block_fluid.transpose(1, 2, 0).reshape(1, 2)))
    return out, block_density.reshape(1, 1, 2).transpose(2, 0, 1)


def solution(mesh):
    return jax.shard_map(
        on_device,
        mesh=mesh,
        in_specs=(
            P(None, "gz", "gy", "gx"),
            P("gz", "gy", "gx"),
            P("gz", "gy", "gx"),
            P("gz", "gy", "gx"),
        ),
        out_specs=(P(None, "gz", "gy", "gx"), P("gz", "gy", "gx")),
        check_vma=False,
    )
```

```python
import functools

import jax
import jax.numpy as jnp
from jax import lax
from jax.experimental import pallas as pl
from jax.experimental.pallas import tpu as pltpu
from jax.sharding import PartitionSpec as P


VELOCITIES = [
    (0, 0, 0),
    (1, 0, 0),
    (-1, 0, 0),
    (0, 1, 0),
    (0, -1, 0),
    (0, 0, 1),
    (0, 0, -1),
    (1, 1, 0),
    (-1, -1, 0),
    (1, -1, 0),
    (-1, 1, 0),
    (1, 0, 1),
    (-1, 0, -1),
    (1, 0, -1),
    (-1, 0, 1),
    (0, 1, 1),
    (0, -1, -1),
    (0, 1, -1),
    (0, -1, 1),
]
OPPOSITE = [0, 2, 1, 4, 3, 6, 5, 8, 7, 10, 9, 12, 11, 14, 13, 16, 15, 18, 17]
Q = 19
SOLID = 3.0e38
Z_ORDER = sorted(range(Q), key=lambda i: {1: 0, -1: 1, 0: 2}[VELOCITIES[i][0]])
SLOT = [Z_ORDER.index(i) for i in range(Q)]
UP_Y = [i for i in Z_ORDER if VELOCITIES[i][1] == 1]
DOWN_Y = [i for i in Z_ORDER if VELOCITIES[i][1] == -1]
Y_FIRST = [3 * s + min(s // 5, 2) for s in SLOT]
Y_FAR = [15, 31, 59, 60, 61]
Y_TILES = 52
MAIN = (12, 29, 8)
PATCH = (4, 10, 3)
F32 = jnp.float32
VMEM = pl.BlockSpec(memory_space=pltpu.VMEM)
SMEM = pl.BlockSpec(memory_space=pltpu.SMEM)
HBM = pl.BlockSpec(memory_space=pltpu.HBM)


def shape(*dims):
    return jax.ShapeDtypeStruct(dims, F32)


def lanes():
    return lax.broadcasted_iota(jnp.int32, (8, 128), 1)


def sublanes():
    return lax.broadcasted_iota(jnp.int32, (8, 128), 0)


def roll(value, sublane_shift, lane_shift):
    if sublane_shift % 8:
        value = pltpu.roll(value, sublane_shift % 8, 0)
    if lane_shift % 128:
        value = pltpu.roll(value, lane_shift % 128, 1)
    return value


def relax(g):
    sums = [g[k] + g[k + 1] for k in range(1, Q, 2)]
    diffs = [g[k] - g[k + 1] for k in range(1, Q, 2)]
    axis_sum = sums[0] + sums[1] + sums[2]
    edge_sum = (sums[3] + sums[4]) + (sums[5] + sums[6]) + (sums[7] + sums[8])
    density = 12.0 * g[0] + 2.0 * axis_sum + edge_sum
    moment_z = 2.0 * diffs[0] + ((diffs[3] + diffs[4]) + (diffs[5] + diffs[6]))
    moment_y = 2.0 * diffs[1] + ((diffs[3] - diffs[4]) + (diffs[7] + diffs[8]))
    moment_x = 2.0 * diffs[2] + ((diffs[5] - diffs[6]) + (diffs[7] - diffs[8]))
    inverse = 1.0 / density
    speed = [moment_z * inverse, moment_y * inverse, moment_x * inverse]
    square = speed[0] * speed[0] + speed[1] * speed[1] + speed[2] * speed[2]
    scaled = density * (1.5 / 36.0)
    base = scaled * (1.0 - 1.5 * square)
    linear = [(4.5 / 36.0) * m for m in (moment_z, moment_y, moment_x)]
    speed = [1.5 * s for s in speed]
    out = [base - 0.5 * g[0]]
    for pair in range(9):
        velocity = VELOCITIES[1 + 2 * pair]
        along = None
        twice = None
        for axis in range(3):
            if velocity[axis] == 0:
                continue
            if along is None:
                along, twice = linear[axis], speed[axis]
            elif velocity[axis] > 0:
                along, twice = along + linear[axis], twice + speed[axis]
            else:
                along, twice = along - linear[axis], twice - speed[axis]
        even = base + along * twice - 0.25 * sums[pair]
        odd = along - 0.25 * diffs[pair]
        out += [even + odd, even - odd]
    return out


def relax_wet(g, wet):
    return [jnp.where(wet, value, SOLID) for value in relax(g)]


def stream_row(tile, at):
    own = [tile(i, at) for i in range(Q)]
    out = [own[0]]
    for i in range(1, Q):
        step_z, step_y, step_x = VELOCITIES[i]
        source = own[i] if step_y == 0 else tile(i, at - step_y)
        source = roll(source, step_z, step_x)
        out.append(jnp.where(source == SOLID, own[OPPOSITE[i]], source))
    return out


def relax_row(tile, at):
    wet = tile(0, at) != SOLID
    return relax_wet(stream_row(tile, at), wet)


def stream_patch(values):
    lane = lanes()
    out = [values[0]]
    for i in range(1, Q):
        step_z, step_y, step_x = VELOCITIES[i]
        low, high = (roll(value, step_z, 16 * step_y + step_x) for value in values[i])
        if step_y == 1:
            high = jnp.where(lane < 16, low, high)
        elif step_y == -1:
            low = jnp.where(lane >= 112, high, low)
        bounce = values[OPPOSITE[i]]
        out.append(
            (jnp.where(low == SOLID, bounce[0], low), jnp.where(high == SOLID, bounce[1], high))
        )
    return out


def relax_patch(values):
    halves = []
    streamed = stream_patch(values)
    for half in range(2):
        wet = values[0][half] != SOLID
        halves.append(relax_wet([value[half] for value in streamed], wet))
    return list(zip(*halves))


def layers_to_send(flat, sizes, low, high):
    tiles, near, far = sizes
    for group in range(near):
        high[group] = flat[pl.ds(64 * group + 5, 8, stride=8)]
        low[group] = flat[pl.ds(64 * group + 2, 8, stride=8)]
    for group in range(far):
        high[near + group] = flat[pl.ds(64 * group + 4, 8, stride=8)]
        low[near + group] = flat[pl.ds(8 * 5 * tiles + 64 * group + 3, 8, stride=8)]


def layers_to_place(flat, sizes, below, above):
    tiles, near, far = sizes
    place = lax.axis_index("gz")
    at_low = place == 0
    at_high = place == lax.axis_size("gz") - 1
    for group in range(near):
        flat[pl.ds(64 * group + 1, 8, stride=8)] = jnp.where(at_low, SOLID, below[group])
        flat[pl.ds(64 * group + 6, 8, stride=8)] = jnp.where(at_high, SOLID, above[group])
    for group in range(far):
        flat[pl.ds(64 * group, 8, stride=8)] = jnp.where(at_low, SOLID, below[near + group])
        first = 8 * 5 * tiles + 64 * group + 7
        flat[pl.ds(first, 8, stride=8)] = jnp.where(at_high, SOLID, above[near + group])


def gather_columns(values):
    lane_row = lanes() // 16
    tile = roll(values[0], 0, 8)
    for row in range(1, 8):
        tile = jnp.where(lane_row == row, roll(values[row], 0, 16 * row + 8), tile)
    return tile


def split_slabs(relative, fluid, new_owner, low, high, moved, kinds, owner, sems):
    copies = [
        pltpu.make_async_copy(fluid, kinds, sems.at[0]),
        pltpu.make_async_copy(relative.at[:, 2:4], high.at[0:Q], sems.at[1]),
        pltpu.make_async_copy(relative.at[:, 0:2], low.at[0:Q], sems.at[2]),
        pltpu.make_async_copy(new_owner, owner, sems.at[3]),
    ]
    for copy in copies:
        copy.start()
    copies[3].wait()
    place = lax.axis_index("gz")
    moved[0] = jnp.full((8, 128), jnp.where((owner[0, 0] == place - 1) & (place > 0), 1.0, 0.0), F32)
    inside = place < lax.axis_size("gz") - 1
    moved[1] = jnp.full((8, 128), jnp.where((owner[0, 1] == place + 1) & inside, 1.0, 0.0), F32)
    copies[0].wait()
    low[Q] = kinds[0:2].astype(F32)
    high[Q] = kinds[2:4].astype(F32)
    copies[1].wait()
    copies[2].wait()


def first_relax(low, high, below, above, moved, own, ahead, back, turn, stage):
    place = lax.axis_index("gz")
    at_low = place == 0
    at_high = place == lax.axis_size("gz") - 1
    swap_low = moved[0] > 0.5
    swap_high = moved[1] > 0.5
    for k in range(2):
        turn[Q, 8 * k : 8 * k + 8] = jnp.where(at_low, 0.0, below[Q, k])
        turn[Q, 8 * (k + 2) : 8 * (k + 3)] = low[Q, k]
        turn[Q, 8 * (k + 4) : 8 * (k + 5)] = high[Q, k]
        turn[Q, 8 * (k + 6) : 8 * (k + 7)] = jnp.where(at_high, 0.0, above[Q, k])
    for i in range(Q):
        for k in range(2):
            mine, other = low[i, k], below[i, k]
            turn[i, 8 * k : 8 * k + 8] = jnp.where(swap_low, mine, other)
            turn[i, 8 * (k + 2) : 8 * (k + 3)] = jnp.where(swap_low, other, mine)
            mine, other = high[i, k], above[i, k]
            turn[i, 8 * (k + 4) : 8 * (k + 5)] = jnp.where(swap_high, other, mine)
            turn[i, 8 * (k + 6) : 8 * (k + 7)] = jnp.where(swap_high, mine, other)
    for row in range(8):
        wet = turn[Q, pl.ds(row, 8, stride=8)] > 0.5
        values = relax_wet([turn[i, pl.ds(row, 8, stride=8)] for i in range(Q)], wet)
        for i in range(Q):
            own[i, row] = values[i]
    up = place % 2 == 0
    for side, (message, high_rows) in enumerate(((ahead, up), (back, jnp.logical_not(up)))):
        first = jnp.where(high_rows, 5, 0)
        far = jnp.where(high_rows, 4, 3)
        for i in range(Q):
            for k in range(3):
                at = 8 * (Y_FIRST[i] + k)
                stage[side, at : at + 8] = own[i, first + k]
        for k in range(5):
            at = 8 * Y_FAR[k]
            stage[side, at : at + 8] = own[jnp.where(high_rows, UP_Y[k], DOWN_Y[k]), far]
        stage[side, 8 * 62 :] = jnp.full((16, 128), SOLID, F32)
        for group in range(8):
            for layer in range(1, 7):
                message[6 * group + layer - 1] = stage[side, pl.ds(64 * group + layer, 8, stride=8)]
        for group in range(2):
            message[48 + group] = stage[side, pl.ds(64 * group, 8, stride=8)]
            message[50 + group] = stage[side, pl.ds(64 * (group + 2) + 7, 8, stride=8)]


def join_rows(own, ahead, back, main, edge, x_ahead, x_back, stage):
    place = lax.axis_index("gy")
    up = lax.axis_index("gz") % 2 == 0
    outside_low = place == 0
    outside_high = place == lax.axis_size("gy") - 1
    for i in range(Q):
        main[i, 0] = jnp.full((8, 128), SOLID, F32)
        main[i, 15] = jnp.full((8, 128), SOLID, F32)
    for side, (message, low_rows) in enumerate(((ahead, up), (back, jnp.logical_not(up)))):
        outside = jnp.where(low_rows, outside_low, outside_high)
        first = jnp.where(low_rows, 1, 12)
        far = jnp.where(low_rows, 0, 15)
        stage[side] = jnp.full((512, 128), SOLID, F32)
        for group in range(8):
            for layer in range(1, 7):
                stage[side, pl.ds(64 * group + layer, 8, stride=8)] = message[6 * group + layer - 1]
        for group in range(2):
            stage[side, pl.ds(64 * group, 8, stride=8)] = message[48 + group]
            stage[side, pl.ds(64 * (group + 2) + 7, 8, stride=8)] = message[50 + group]
        for i in range(Q):
            for k in range(3):
                at = 8 * (Y_FIRST[i] + k)
                main[i, first + k] = jnp.where(outside, SOLID, stage[side, at : at + 8])
        for k in range(5):
            at = 8 * Y_FAR[k]
            value = jnp.where(outside, SOLID, stage[side, at : at + 8])
            main[jnp.where(low_rows, UP_Y[k], DOWN_Y[k]), far] = value
    edges = []
    for i in range(Q):
        rows = [own[i, k] for k in range(8)]
        for k in range(8):
            main[i, 4 + k] = rows[k]
        rows = [main[i, k] for k in range(4)] + rows + [main[i, k] for k in range(12, 16)]
        for half in range(2):
            edges.append(gather_columns(rows[8 * half : 8 * half + 8]))
            edge[i, half] = edges[-1]
    part = lanes() % 16 // 4
    for group in range(10):
        to_low = jnp.full((8, 128), SOLID, F32)
        to_high = to_low
        for k, tile in enumerate(edges[4 * group : 4 * group + 4]):
            to_low = jnp.where(part == k, roll(tile, 0, 4 * (k - 2)), to_low)
            to_high = jnp.where(part == k, roll(tile, 0, 4 * (k - 1)), to_high)
        x_ahead[group] = jnp.where(up, to_high, to_low)
        x_back[group] = jnp.where(up, to_low, to_high)


def two_steps(main, flat, z_low, z_high, middle):
    for row in range(1, 15):
        values = relax_row(lambda i, at: main[i, at], row)
        for i in range(Q):
            middle[i, row - 1] = values[i]
    for row in range(2, 14):
        values = relax_row(lambda i, at: middle[i, at], row - 1)
        for i in range(Q):
            at = 8 * (12 * SLOT[i] + row - 2)
            flat[at : at + 8] = values[i]
    flat[8 * 12 * Q :] = jnp.full((32, 128), SOLID, F32)
    layers_to_send(flat, MAIN, z_low, z_high)


def patch_two_steps(edge, ahead, back, flat, z_low, z_high):
    up = lax.axis_index("gz") % 2 == 0
    place = lax.axis_index("gx")
    outside = (place == 0, place == lax.axis_size("gx") - 1)
    own_part = (lanes() % 16 >= 8, lanes() % 16 < 8)
    for side in range(2):
        values = []
        for i in range(Q):
            tiles = []
            for half in range(2):
                group, k = divmod(2 * i + half, 4)
                message = jnp.where(up == (side == 0), ahead[group], back[group])
                message = roll(message, 0, -4 * (k - 1 - side))
                message = jnp.where(outside[side], SOLID, message)
                tiles.append(jnp.where(own_part[side], edge[i, half], message))
            values.append(tiles)
        values = relax_patch(relax_patch(values))
        for i in range(Q):
            for half in range(2):
                at = 8 * (4 * SLOT[i] + 2 * side + half)
                flat[at : at + 8] = values[i][half]
    flat[8 * 4 * Q :] = jnp.full((32, 128), SOLID, F32)
    layers_to_send(flat, PATCH, z_low, z_high)


def last_two_steps(flat_in, below, above, out, flat, middle):
    layers_to_place(flat, MAIN, below, above)

    def joined(i, at):
        return flat[pl.ds(8 * (12 * SLOT[i] + at), 8)]

    for row in range(3, 13):
        values = relax_row(joined, row - 2)
        for i in range(Q):
            middle[i, row - 3] = values[i]
    for row in range(8):
        wet = middle[0, row + 1] != SOLID
        values = stream_row(lambda i, at: middle[i, at], row + 1)
        for i in range(Q):
            out[i, row] = jnp.where(wet, values[i], 0.0)


def patch_last_two_steps(
    flat_in, below, above, inner, block_fluid, out, block_density, flat, turn, final, wet_count, sems
):
    count_copy = pltpu.make_async_copy(block_fluid, wet_count, sems.at[2])
    count_copy.start()
    layers_to_place(flat, PATCH, below, above)
    patches = []
    for side in range(2):
        values = []
        for i in range(Q):
            at = 8 * (4 * SLOT[i] + 2 * side)
            values.append((flat[at : at + 8], flat[at + 8 : at + 16]))
        values = relax_patch(values)
        wet = [value != SOLID for value in values[0]]
        values = stream_patch(values)
        patches.append([[jnp.where(wet[half], v[half], 0.0) for half in range(2)] for v in values])
    lane = lanes()
    seam = (lane < 4) | (lane >= 124)
    low_part = lane % 16 < 8
    for i in range(Q):
        columns = [jnp.where(low_part, patches[1][i][half], patches[0][i][half]) for half in range(2)]
        for row in range(8):
            half, at = divmod(row + 4, 8)
            value = jnp.where(seam, roll(columns[half], 0, -(16 * at + 8)), inner[i, row])
            turn[i, 8 * row : 8 * row + 8] = value
    copies = []
    masses = []
    for slot in range(2):
        mass = None
        for k in range(2):
            layer = 2 * slot + k
            values = [turn[i, pl.ds(layer + 2, 8, stride=8)] for i in range(Q)]
            for i in range(Q):
                final[i, layer] = values[i]
            axis_sum = functools.reduce(jnp.add, values[1:7])
            edge_sum = functools.reduce(jnp.add, values[7:])
            density = values[0] * (1.0 / 3.0) + axis_sum * (1.0 / 18.0) + edge_sum * (1.0 / 36.0)
            mass = density if mass is None else mass + density
        masses.append(mass)
        layers = slice(2 * slot, 2 * slot + 2)
        copies.append(pltpu.make_async_copy(final.at[:, layers], out.at[:, layers], sems.at[slot]))
        copies[slot].start()
    count_copy.wait()
    for slot in range(2):
        count = jnp.maximum(wet_count[0, slot], 1).astype(F32)
        block_density[0, slot] = jnp.sum(masses[slot]) / count
    for copy in copies:
        copy.wait()


def ring_exchange(to_low, to_high, axis):
    count = lax.axis_size(axis)
    up = [(i, (i + 1) % count) for i in range(count)]
    down = [(target, source) for source, target in up]
    return lax.ppermute(to_high, axis, up), lax.ppermute(to_low, axis, down)


def loop_exchange(ahead, back, axis):
    count = lax.axis_size(axis)
    layers = lax.axis_size("gz")
    pairs = []
    for i in range(count):
        for layer in range(layers):
            if layer % 2 == 0:
                target = (i + 1, layer) if i < count - 1 else (i, layer + 1)
            else:
                target = (i - 1, layer) if i > 0 else (i, layer - 1)
            pairs.append((i * layers + layer, target[0] * layers + target[1]))
    inverse = [(target, source) for source, target in pairs]
    axes = (axis, "gz")
    return lax.ppermute(ahead, axes, pairs), lax.ppermute(back, axes, inverse)


def call(kernel, outs, in_specs, out_specs=None, scratch=(), aliases=None):
    if out_specs is None:
        out_specs = [VMEM] * len(outs)
    return pl.pallas_call(
        kernel,
        out_shape=outs,
        in_specs=in_specs,
        out_specs=out_specs,
        scratch_shapes=list(scratch),
        input_output_aliases=aliases or {},
        compiler_params=pltpu.CompilerParams(vmem_limit_bytes=32 * 1024 * 1024),
    )


def in_hbm(array):
    return pltpu.with_memory_space_constraint(array, pltpu.HBM)


def on_device(relative, fluid, block_fluid, new_owner):
    low, high, moved = call(
        split_slabs,
        [shape(Q + 1, 2, 8, 128), shape(Q + 1, 2, 8, 128), shape(2, 8, 128)],
        [HBM] * 3,
        scratch=[
            pltpu.VMEM((4, 8, 128), jnp.int32),
            pltpu.SMEM((1, 2), jnp.int32),
            pltpu.SemaphoreType.DMA((4,)),
        ],
    )(in_hbm(relative), in_hbm(fluid), in_hbm(new_owner.transpose(1, 2, 0).reshape(1, 2)))
    below, above = ring_exchange(low, high, "gz")
    own, ahead, back = call(
        first_relax,
        [shape(Q, 8, 8, 128), shape(Y_TILES, 8, 128), shape(Y_TILES, 8, 128)],
        [VMEM] * 5,
        scratch=[pltpu.VMEM((Q + 1, 64, 128), F32), pltpu.VMEM((2, 512, 128), F32)],
    )(low, high, below, above, moved)
    ahead, back = loop_exchange(ahead, back, "gy")
    main, edge, x_ahead, x_back = call(
        join_rows,
        [shape(Q, 16, 8, 128), shape(Q, 2, 8, 128), shape(10, 8, 128), shape(10, 8, 128)],
        [VMEM] * 3,
        scratch=[pltpu.VMEM((2, 512, 128), F32)],
    )(own, ahead, back)
    x_ahead, x_back = loop_exchange(x_ahead, x_back, "gx")
    flat, z_low, z_high = call(
        two_steps,
        [shape(64 * MAIN[1], 128)] + [shape(sum(MAIN[1:]), 8, 128)] * 2,
        [VMEM],
        scratch=[pltpu.VMEM((Q, 14, 8, 128), F32)],
    )(main)
    below, above = ring_exchange(z_low, z_high, "gz")
    patch, z_low, z_high = call(
        patch_two_steps,
        [shape(64 * PATCH[1], 128)] + [shape(sum(PATCH[1:]), 8, 128)] * 2,
        [VMEM] * 3,
    )(edge, x_ahead, x_back)
    patch_below, patch_above = ring_exchange(z_low, z_high, "gz")
    inner, _ = call(
        last_two_steps,
        [shape(Q, 8, 8, 128), shape(64 * MAIN[1], 128)],
        [VMEM] * 3,
        scratch=[pltpu.VMEM((Q, 10, 8, 128), F32)],
        aliases={0: 1},
    )(flat, below, above)
    out, block_density, _ = call(
        patch_last_two_steps,
        [shape(Q, 4, 8, 128), shape(1, 2), shape(64 * PATCH[1], 128)],
        [VMEM] * 4 + [HBM],
        [HBM, SMEM, VMEM],
        scratch=[
            pltpu.VMEM((Q, 64, 128), F32),
            pltpu.VMEM((Q, 4, 8, 128), F32),
            pltpu.SMEM((1, 2), jnp.int32),
            pltpu.SemaphoreType.DMA((3,)),
        ],
        aliases={0: 2},
    )(patch, patch_below, patch_above, inner, in_hbm(block_fluid.transpose(1, 2, 0).reshape(1, 2)))
    return out, block_density.reshape(1, 1, 2).transpose(2, 0, 1)


def solution(mesh):
    return jax.shard_map(
        on_device,
        mesh=mesh,
        in_specs=(
            P(None, "gz", "gy", "gx"),
            P("gz", "gy", "gx"),
            P("gz", "gy", "gx"),
            P("gz", "gy", "gx"),
        ),
        out_specs=(P(None, "gz", "gy", "gx"), P("gz", "gy", "gx")),
        check_vma=False,
    )
```

```python
import functools

import jax
import jax.numpy as jnp
from jax import lax
from jax.experimental import pallas as pl
from jax.experimental.pallas import tpu as pltpu
from jax.sharding import PartitionSpec as P


VELOCITIES = [
    (0, 0, 0),
    (1, 0, 0),
    (-1, 0, 0),
    (0, 1, 0),
    (0, -1, 0),
    (0, 0, 1),
    (0, 0, -1),
    (1, 1, 0),
    (-1, -1, 0),
    (1, -1, 0),
    (-1, 1, 0),
    (1, 0, 1),
    (-1, 0, -1),
    (1, 0, -1),
    (-1, 0, 1),
    (0, 1, 1),
    (0, -1, -1),
    (0, 1, -1),
    (0, -1, 1),
]
OPPOSITE = [0, 2, 1, 4, 3, 6, 5, 8, 7, 10, 9, 12, 11, 14, 13, 16, 15, 18, 17]
Q = 19
SOLID = 3.0e38
Z_ORDER = sorted(range(Q), key=lambda i: {1: 0, -1: 1, 0: 2}[VELOCITIES[i][0]])
SLOT = [Z_ORDER.index(i) for i in range(Q)]
UP_Y = [i for i in Z_ORDER if VELOCITIES[i][1] == 1]
DOWN_Y = [i for i in Z_ORDER if VELOCITIES[i][1] == -1]
Y_FIRST = [3 * s + min(s // 5, 2) for s in SLOT]
Y_FAR = [15, 31, 59, 60, 61]
Y_TILES = 52
PER_SLOT = 14
NEAR = 34
FAR = 9
FLAT_ROWS = 8 * 8 * NEAR
F32 = jnp.float32
VMEM = pl.BlockSpec(memory_space=pltpu.VMEM)
SMEM = pl.BlockSpec(memory_space=pltpu.SMEM)
HBM = pl.BlockSpec(memory_space=pltpu.HBM)


def shape(*dims):
    return jax.ShapeDtypeStruct(dims, F32)


def lanes():
    return lax.broadcasted_iota(jnp.int32, (8, 128), 1)


def sublanes():
    return lax.broadcasted_iota(jnp.int32, (8, 128), 0)


def roll(value, sublane_shift, lane_shift):
    if sublane_shift % 8:
        value = pltpu.roll(value, sublane_shift % 8, 0)
    if lane_shift % 128:
        value = pltpu.roll(value, lane_shift % 128, 1)
    return value


def relax(g):
    sums = [g[k] + g[k + 1] for k in range(1, Q, 2)]
    diffs = [g[k] - g[k + 1] for k in range(1, Q, 2)]
    axis_sum = sums[0] + sums[1] + sums[2]
    edge_sum = (sums[3] + sums[4]) + (sums[5] + sums[6]) + (sums[7] + sums[8])
    density = 12.0 * g[0] + 2.0 * axis_sum + edge_sum
    moment_z = 2.0 * diffs[0] + ((diffs[3] + diffs[4]) + (diffs[5] + diffs[6]))
    moment_y = 2.0 * diffs[1] + ((diffs[3] - diffs[4]) + (diffs[7] + diffs[8]))
    moment_x = 2.0 * diffs[2] + ((diffs[5] - diffs[6]) + (diffs[7] - diffs[8]))
    inverse = 1.0 / density
    speed = [moment_z * inverse, moment_y * inverse, moment_x * inverse]
    square = speed[0] * speed[0] + speed[1] * speed[1] + speed[2] * speed[2]
    scaled = density * (1.5 / 36.0)
    base = scaled * (1.0 - 1.5 * square)
    linear = [(4.5 / 36.0) * m for m in (moment_z, moment_y, moment_x)]
    speed = [1.5 * s for s in speed]
    out = [base - 0.5 * g[0]]
    for pair in range(9):
        velocity = VELOCITIES[1 + 2 * pair]
        along = None
        twice = None
        for axis in range(3):
            if velocity[axis] == 0:
                continue
            if along is None:
                along, twice = linear[axis], speed[axis]
            elif velocity[axis] > 0:
                along, twice = along + linear[axis], twice + speed[axis]
            else:
                along, twice = along - linear[axis], twice - speed[axis]
        even = base + along * twice - 0.25 * sums[pair]
        odd = along - 0.25 * diffs[pair]
        out += [even + odd, even - odd]
    return out


def relax_wet(g, wet):
    return [jnp.where(wet, value, SOLID) for value in relax(g)]


def stream_row(tile, at):
    own = [tile(i, at) for i in range(Q)]
    out = [own[0]]
    for i in range(1, Q):
        step_z, step_y, step_x = VELOCITIES[i]
        source = own[i] if step_y == 0 else tile(i, at - step_y)
        source = roll(source, step_z, step_x)
        out.append(jnp.where(source == SOLID, own[OPPOSITE[i]], source))
    return out


def relax_row(tile, at):
    wet = tile(0, at) != SOLID
    return relax_wet(stream_row(tile, at), wet)


def stream_patch(values):
    out = [values[0]]
    for i in range(1, Q):
        step_z, step_y, step_x = VELOCITIES[i]
        source = roll(values[i], step_z, 8 * step_y + step_x)
        out.append(jnp.where(source == SOLID, values[OPPOSITE[i]], source))
    return out


def gather_columns(tile, values, rows):
    lane_row = lanes() // 8
    for row, value in zip(rows, values):
        tile = jnp.where(lane_row == row, roll(value, 0, 8 * row + 4), tile)
    return tile


def split_slabs(relative, fluid, new_owner, low, high, moved, kinds, owner, sems):
    copies = [
        pltpu.make_async_copy(fluid, kinds, sems.at[0]),
        pltpu.make_async_copy(relative.at[:, 2:4], high.at[0:Q], sems.at[1]),
        pltpu.make_async_copy(relative.at[:, 0:2], low.at[0:Q], sems.at[2]),
        pltpu.make_async_copy(new_owner, owner, sems.at[3]),
    ]
    for copy in copies:
        copy.start()
    copies[3].wait()
    place = lax.axis_index("gz")
    moved[0] = jnp.full((8, 128), jnp.where((owner[0, 0] == place - 1) & (place > 0), 1.0, 0.0), F32)
    inside = place < lax.axis_size("gz") - 1
    moved[1] = jnp.full((8, 128), jnp.where((owner[0, 1] == place + 1) & inside, 1.0, 0.0), F32)
    copies[0].wait()
    low[Q] = kinds[0:2].astype(F32)
    high[Q] = kinds[2:4].astype(F32)
    copies[1].wait()
    copies[2].wait()


def first_relax(high, low, above, below, moved, own, ahead, back, turn, stage):
    place = lax.axis_index("gz")
    at_low = place == 0
    at_high = place == lax.axis_size("gz") - 1
    swap_low = moved[0] > 0.5
    swap_high = moved[1] > 0.5
    for k in range(2):
        turn[Q, 8 * k : 8 * k + 8] = jnp.where(at_low, 0.0, below[Q, k])
        turn[Q, 8 * (k + 2) : 8 * (k + 3)] = low[Q, k]
        turn[Q, 8 * (k + 4) : 8 * (k + 5)] = high[Q, k]
        turn[Q, 8 * (k + 6) : 8 * (k + 7)] = jnp.where(at_high, 0.0, above[Q, k])
    for i in range(Q):
        for k in range(2):
            mine, other = low[i, k], below[i, k]
            turn[i, 8 * k : 8 * k + 8] = jnp.where(swap_low, mine, other)
            turn[i, 8 * (k + 2) : 8 * (k + 3)] = jnp.where(swap_low, other, mine)
            mine, other = high[i, k], above[i, k]
            turn[i, 8 * (k + 4) : 8 * (k + 5)] = jnp.where(swap_high, other, mine)
            turn[i, 8 * (k + 6) : 8 * (k + 7)] = jnp.where(swap_high, mine, other)
    for row in range(8):
        wet = turn[Q, pl.ds(row, 8, stride=8)] > 0.5
        values = relax_wet([turn[i, pl.ds(row, 8, stride=8)] for i in range(Q)], wet)
        for i in range(Q):
            own[i, row] = values[i]
    up = place % 2 == 0
    for side, (message, high_rows) in enumerate(((ahead, up), (back, jnp.logical_not(up)))):
        first = jnp.where(high_rows, 5, 0)
        far = jnp.where(high_rows, 4, 3)
        for i in range(Q):
            for k in range(3):
                at = 8 * (Y_FIRST[i] + k)
                stage[side, at : at + 8] = own[i, first + k]
        for k in range(5):
            at = 8 * Y_FAR[k]
            stage[side, at : at + 8] = own[jnp.where(high_rows, UP_Y[k], DOWN_Y[k]), far]
        stage[side, 8 * 62 :] = jnp.full((16, 128), SOLID, F32)
        for group in range(8):
            for layer in range(1, 7):
                message[6 * group + layer - 1] = stage[side, pl.ds(64 * group + layer, 8, stride=8)]
        for group in range(2):
            message[48 + group] = stage[side, pl.ds(64 * group, 8, stride=8)]
            message[50 + group] = stage[side, pl.ds(64 * (group + 2) + 7, 8, stride=8)]


def own_rows(own, main, edge):
    for i in range(Q):
        rows = [own[i, k] for k in range(8)]
        main[i, 0] = jnp.full((8, 128), SOLID, F32)
        main[i, 15] = jnp.full((8, 128), SOLID, F32)
        for k in range(8):
            main[i, 4 + k] = rows[k]
        edge[i] = gather_columns(jnp.full((8, 128), SOLID, F32), rows, range(4, 12))


def join_rows(main_in, edge_in, ahead, back, main, edge, x_ahead, x_back, stage):
    place = lax.axis_index("gy")
    up = lax.axis_index("gz") % 2 == 0
    outside_low = place == 0
    outside_high = place == lax.axis_size("gy") - 1
    for side, (message, low_rows) in enumerate(((ahead, up), (back, jnp.logical_not(up)))):
        outside = jnp.where(low_rows, outside_low, outside_high)
        first = jnp.where(low_rows, 1, 12)
        far = jnp.where(low_rows, 0, 15)
        stage[side] = jnp.full((512, 128), SOLID, F32)
        for group in range(8):
            for layer in range(1, 7):
                stage[side, pl.ds(64 * group + layer, 8, stride=8)] = message[6 * group + layer - 1]
        for group in range(2):
            stage[side, pl.ds(64 * group, 8, stride=8)] = message[48 + group]
            stage[side, pl.ds(64 * (group + 2) + 7, 8, stride=8)] = message[50 + group]
        for i in range(Q):
            for k in range(3):
                at = 8 * (Y_FIRST[i] + k)
                main[i, first + k] = jnp.where(outside, SOLID, stage[side, at : at + 8])
        for k in range(5):
            at = 8 * Y_FAR[k]
            value = jnp.where(outside, SOLID, stage[side, at : at + 8])
            main[jnp.where(low_rows, UP_Y[k], DOWN_Y[k]), far] = value
    edges = []
    for i in range(Q):
        beside = [*range(4), *range(12, 16)]
        edges.append(gather_columns(edge[i], [main[i, k] for k in beside], beside))
        edge[i] = edges[i]
    low_side = lanes() % 8 < 4
    for i in range(10):
        if i + 10 < Q:
            to_low = jnp.where(low_side, roll(edges[i + 10], 0, -4), edges[i])
            to_high = jnp.where(low_side, edges[i], roll(edges[i + 10], 0, 4))
            x_ahead[i] = jnp.where(up, to_high, to_low)
            x_back[i] = jnp.where(up, to_low, to_high)
        else:
            x_ahead[i] = edges[i]
            x_back[i] = edges[i]


def two_steps(main, out, edge, middle):
    def first(row):
        values = relax_row(lambda i, at: main[i, at], row)
        for i in range(Q):
            middle[i, row - 1] = values[i]

    def second(row):
        values = relax_row(lambda i, at: middle[i, at], row - 1)
        for i in range(Q):
            out[i, row - 2] = values[i]

    for row in range(1, 15):
        first(row)
    for row in range(2, 14):
        second(row)
    for i in range(Q):
        edge[i] = gather_columns(out[i, 0], [out[i, k] for k in range(12)], range(2, 14))


def patch_two_steps(inner, inner_edge, edge, ahead, back, flat, below, above):
    up = lax.axis_index("gz") % 2 == 0
    place = lax.axis_index("gx")
    at_low = place == 0
    at_high = place == lax.axis_size("gx") - 1
    column = lanes() % 8
    low_side = column < 4
    sides = []
    for side in range(2):
        values = []
        for i in range(Q):
            message = jnp.where(up == (side == 0), ahead[i % 10], back[i % 10])
            if i >= 10:
                message = roll(message, 0, (-4, 4)[side])
            message = jnp.where((at_low, at_high)[side], SOLID, message)
            if side == 0:
                values.append(jnp.where(low_side, message, edge[i]))
            else:
                values.append(jnp.where(low_side, edge[i], message))
        for step in range(2):
            wet = values[0] != SOLID
            values = relax_wet(stream_patch(values), wet)
        sides.append(values)
    lane = lanes()
    seam = (lane < 2) | (lane >= 126)
    for i in range(Q):
        own_columns = jnp.where(low_side, sides[1][i], sides[0][i])
        first = PER_SLOT * SLOT[i]
        for row in range(12):
            value = jnp.where(seam, roll(own_columns, 0, -(8 * (row + 2) + 4)), inner[i, row])
            flat[8 * (first + row) : 8 * (first + row) + 8] = value
        fresh = inner_edge[i]
        for side in range(2):
            stale = (column < 6) if side == 0 else (column >= 2)
            at = 8 * (first + 12 + side)
            flat[at : at + 8] = jnp.where(stale, sides[side][i], fresh)
    flat[8 * PER_SLOT * Q :] = jnp.full((FLAT_ROWS - 8 * PER_SLOT * Q, 128), SOLID, F32)
    for group in range(NEAR):
        above[group] = flat[pl.ds(64 * group + 5, 8, stride=8)]
        below[group] = flat[pl.ds(64 * group + 2, 8, stride=8)]
    for group in range(FAR):
        above[NEAR + group] = flat[pl.ds(64 * group + 4, 8, stride=8)]
        below[NEAR + group] = flat[pl.ds(8 * 5 * PER_SLOT + 64 * group + 3, 8, stride=8)]


def last_two_steps(
    flat_in, below, above, block_fluid, out, block_density, flat, middle, turn, final, wet_count, mean, sems
):
    count_copy = pltpu.make_async_copy(block_fluid, wet_count, sems.at[4])
    count_copy.start()
    place = lax.axis_index("gz")
    at_low = place == 0
    at_high = place == lax.axis_size("gz") - 1
    lane = lanes()
    low_side = lane % 8 < 4
    for group in range(NEAR):
        flat[pl.ds(64 * group + 1, 8, stride=8)] = jnp.where(at_low, SOLID, below[group])
        flat[pl.ds(64 * group + 6, 8, stride=8)] = jnp.where(at_high, SOLID, above[group])
    for group in range(FAR):
        flat[pl.ds(64 * group, 8, stride=8)] = jnp.where(at_low, SOLID, below[NEAR + group])
        flat[pl.ds(8 * 5 * PER_SLOT + 64 * group + 7, 8, stride=8)] = jnp.where(
            at_high, SOLID, above[NEAR + group]
        )

    def joined(i, at):
        return flat[pl.ds(8 * (PER_SLOT * SLOT[i] + at), 8)]

    def third(row):
        values = relax_row(joined, row - 2)
        for i in range(Q):
            middle[i, row - 3] = values[i]

    for row in range(3, 13):
        third(row)
    patches = []
    for side in range(2):
        values = [joined(i, 12 + side) for i in range(Q)]
        wet = values[0] != SOLID
        values = relax_wet(stream_patch(values), wet)
        patches.append(stream_patch(values))
    own_columns = [jnp.where(low_side, patches[1][i], patches[0][i]) for i in range(Q)]
    seam = (lane < 2) | (lane >= 126)
    for row in range(8):
        wet = middle[0, row + 1] != SOLID
        values = stream_row(lambda i, at: middle[i, at], row + 1)
        for i in range(Q):
            value = jnp.where(seam, roll(own_columns[i], 0, -(8 * (row + 4) + 4)), values[i])
            turn[i, 8 * row : 8 * row + 8] = jnp.where(wet, value, 0.0)
    copies = []
    masses = []
    for layer in range(4):
        values = [turn[i, pl.ds(layer + 2, 8, stride=8)] for i in range(Q)]
        for i in range(Q):
            final[i, layer] = values[i]
        copies.append(pltpu.make_async_copy(final.at[:, layer], out.at[:, layer], sems.at[layer]))
        copies[layer].start()
        axis_sum = functools.reduce(jnp.add, values[1:7])
        edge_sum = functools.reduce(jnp.add, values[7:])
        masses.append(values[0] * (1.0 / 3.0) + axis_sum * (1.0 / 18.0) + edge_sum * (1.0 / 36.0))
    count_copy.wait()
    for slot in range(2):
        count = jnp.maximum(wet_count[0, slot], 1).astype(F32)
        mean[0, slot] = jnp.sum(masses[2 * slot] + masses[2 * slot + 1]) / count
    copies.append(pltpu.make_async_copy(mean, block_density, sems.at[5]))
    copies[4].start()
    for copy in copies:
        copy.wait()


def ring_exchange(to_low, to_high, axis):
    count = lax.axis_size(axis)
    up = [(i, (i + 1) % count) for i in range(count)]
    down = [(target, source) for source, target in up]
    return lax.ppermute(to_high, axis, up), lax.ppermute(to_low, axis, down)


def loop_exchange(ahead, back, axis):
    count = lax.axis_size(axis)
    layers = lax.axis_size("gz")
    pairs = []
    for i in range(count):
        for layer in range(layers):
            if layer % 2 == 0:
                target = (i + 1, layer) if i < count - 1 else (i, layer + 1)
            else:
                target = (i - 1, layer) if i > 0 else (i, layer - 1)
            pairs.append((i * layers + layer, target[0] * layers + target[1]))
    inverse = [(target, source) for source, target in pairs]
    axes = (axis, "gz")
    return lax.ppermute(ahead, axes, pairs), lax.ppermute(back, axes, inverse)


def call(kernel, outs, in_specs, out_specs=None, scratch=(), aliases=None, vmem=32):
    if out_specs is None:
        out_specs = [VMEM] * len(outs)
    return pl.pallas_call(
        kernel,
        out_shape=outs,
        in_specs=in_specs,
        out_specs=out_specs,
        scratch_shapes=list(scratch),
        input_output_aliases=aliases or {},
        compiler_params=pltpu.CompilerParams(vmem_limit_bytes=vmem * 1024 * 1024),
    )


def in_hbm(array):
    return pltpu.with_memory_space_constraint(array, pltpu.HBM)


def on_device(relative, fluid, block_fluid, new_owner):
    low, high, moved = call(
        split_slabs,
        [shape(Q + 1, 2, 8, 128), shape(Q + 1, 2, 8, 128), shape(2, 8, 128)],
        [HBM] * 3,
        scratch=[
            pltpu.VMEM((4, 8, 128), jnp.int32),
            pltpu.SMEM((1, 2), jnp.int32),
            pltpu.SemaphoreType.DMA((4,)),
        ],
    )(in_hbm(relative), in_hbm(fluid), in_hbm(new_owner.transpose(1, 2, 0).reshape(1, 2)))
    below, above = ring_exchange(low, high, "gz")
    own, ahead, back = call(
        first_relax,
        [shape(Q, 8, 8, 128), shape(Y_TILES, 8, 128), shape(Y_TILES, 8, 128)],
        [VMEM] * 5,
        scratch=[pltpu.VMEM((Q + 1, 64, 128), F32), pltpu.VMEM((2, 512, 128), F32)],
    )(high, low, above, below, moved)
    ahead, back = loop_exchange(ahead, back, "gy")
    main, edge = call(own_rows, [shape(Q, 16, 8, 128), shape(Q, 8, 128)], [VMEM])(own)
    main, edge, x_ahead, x_back = call(
        join_rows,
        [shape(Q, 16, 8, 128), shape(Q, 8, 128), shape(10, 8, 128), shape(10, 8, 128)],
        [VMEM] * 4,
        scratch=[pltpu.VMEM((2, 512, 128), F32)],
        aliases={0: 0, 1: 1},
    )(main, edge, ahead, back)
    x_ahead, x_back = loop_exchange(x_ahead, x_back, "gx")
    inner, inner_edge = call(
        two_steps,
        [shape(Q, 12, 8, 128), shape(Q, 8, 128)],
        [VMEM],
        scratch=[pltpu.VMEM((Q, 14, 8, 128), F32)],
    )(main)
    flat, z_low, z_high = call(
        patch_two_steps,
        [shape(FLAT_ROWS, 128), shape(NEAR + FAR, 8, 128), shape(NEAR + FAR, 8, 128)],
        [VMEM] * 5,
    )(inner, inner_edge, edge, x_ahead, x_back)
    below, above = ring_exchange(z_low, z_high, "gz")
    out, block_density, _ = call(
        last_two_steps,
        [shape(Q, 4, 8, 128), shape(1, 2), shape(FLAT_ROWS, 128)],
        [VMEM] * 3 + [HBM],
        [HBM, HBM, VMEM],
        scratch=[
            pltpu.VMEM((Q, 10, 8, 128), F32),
            pltpu.VMEM((Q, 64, 128), F32),
            pltpu.VMEM((Q, 4, 8, 128), F32),
            pltpu.SMEM((1, 2), jnp.int32),
            pltpu.SMEM((1, 2), F32),
            pltpu.SemaphoreType.DMA((6,)),
        ],
        aliases={0: 2},
    )(flat, below, above, in_hbm(block_fluid.transpose(1, 2, 0).reshape(1, 2)))
    return out, block_density.reshape(1, 1, 2).transpose(2, 0, 1)


def solution(mesh):
    return jax.shard_map(
        on_device,
        mesh=mesh,
        in_specs=(
            P(None, "gz", "gy", "gx"),
            P("gz", "gy", "gx"),
            P("gz", "gy", "gx"),
            P("gz", "gy", "gx"),
        ),
        out_specs=(P(None, "gz", "gy", "gx"), P("gz", "gy", "gx")),
        check_vma=False,
    )
```

```python
import functools

import jax
import jax.numpy as jnp
from jax import lax
from jax.experimental import pallas as pl
from jax.experimental.pallas import tpu as pltpu
from jax.sharding import PartitionSpec as P


VELOCITIES = [
    (0, 0, 0),
    (1, 0, 0),
    (-1, 0, 0),
    (0, 1, 0),
    (0, -1, 0),
    (0, 0, 1),
    (0, 0, -1),
    (1, 1, 0),
    (-1, -1, 0),
    (1, -1, 0),
    (-1, 1, 0),
    (1, 0, 1),
    (-1, 0, -1),
    (1, 0, -1),
    (-1, 0, 1),
    (0, 1, 1),
    (0, -1, -1),
    (0, 1, -1),
    (0, -1, 1),
]
OPPOSITE = [0, 2, 1, 4, 3, 6, 5, 8, 7, 10, 9, 12, 11, 14, 13, 16, 15, 18, 17]
Q = 19
SOLID = 3.0e38
Z_ORDER = sorted(range(Q), key=lambda i: {1: 0, -1: 1, 0: 2}[VELOCITIES[i][0]])
SLOT = [Z_ORDER.index(i) for i in range(Q)]
UP_Y = [i for i in Z_ORDER if VELOCITIES[i][1] == 1]
DOWN_Y = [i for i in Z_ORDER if VELOCITIES[i][1] == -1]
Y_FIRST = [3 * s + min(s // 5, 2) for s in SLOT]
Y_FAR = [15, 31, 59, 60, 61]
Y_TILES = 52
PER_SLOT = 14
NEAR = 34
FAR = 9
FLAT_ROWS = 8 * 8 * NEAR
F32 = jnp.float32
VMEM = pl.BlockSpec(memory_space=pltpu.VMEM)
SMEM = pl.BlockSpec(memory_space=pltpu.SMEM)
HBM = pl.BlockSpec(memory_space=pltpu.HBM)


def shape(*dims):
    return jax.ShapeDtypeStruct(dims, F32)


def lanes():
    return lax.broadcasted_iota(jnp.int32, (8, 128), 1)


def sublanes():
    return lax.broadcasted_iota(jnp.int32, (8, 128), 0)


def roll(value, sublane_shift, lane_shift):
    if sublane_shift % 8:
        value = pltpu.roll(value, sublane_shift % 8, 0)
    if lane_shift % 128:
        value = pltpu.roll(value, lane_shift % 128, 1)
    return value


def relax(g):
    sums = [g[k] + g[k + 1] for k in range(1, Q, 2)]
    diffs = [g[k] - g[k + 1] for k in range(1, Q, 2)]
    axis_sum = sums[0] + sums[1] + sums[2]
    edge_sum = (sums[3] + sums[4]) + (sums[5] + sums[6]) + (sums[7] + sums[8])
    density = 12.0 * g[0] + 2.0 * axis_sum + edge_sum
    moment_z = 2.0 * diffs[0] + ((diffs[3] + diffs[4]) + (diffs[5] + diffs[6]))
    moment_y = 2.0 * diffs[1] + ((diffs[3] - diffs[4]) + (diffs[7] + diffs[8]))
    moment_x = 2.0 * diffs[2] + ((diffs[5] - diffs[6]) + (diffs[7] - diffs[8]))
    inverse = 1.0 / density
    speed = [moment_z * inverse, moment_y * inverse, moment_x * inverse]
    square = speed[0] * speed[0] + speed[1] * speed[1] + speed[2] * speed[2]
    scaled = density * (1.5 / 36.0)
    base = scaled * (1.0 - 1.5 * square)
    linear = [(4.5 / 36.0) * m for m in (moment_z, moment_y, moment_x)]
    speed = [1.5 * s for s in speed]
    out = [base - 0.5 * g[0]]
    for pair in range(9):
        velocity = VELOCITIES[1 + 2 * pair]
        along = None
        twice = None
        for axis in range(3):
            if velocity[axis] == 0:
                continue
            if along is None:
                along, twice = linear[axis], speed[axis]
            elif velocity[axis] > 0:
                along, twice = along + linear[axis], twice + speed[axis]
            else:
                along, twice = along - linear[axis], twice - speed[axis]
        even = base + along * twice - 0.25 * sums[pair]
        odd = along - 0.25 * diffs[pair]
        out += [even + odd, even - odd]
    return out


def relax_wet(g, wet):
    return [jnp.where(wet, value, SOLID) for value in relax(g)]


def stream_row(tile, at):
    own = [tile(i, at) for i in range(Q)]
    out = [own[0]]
    for i in range(1, Q):
        step_z, step_y, step_x = VELOCITIES[i]
        source = own[i] if step_y == 0 else tile(i, at - step_y)
        source = roll(source, step_z, step_x)
        out.append(jnp.where(source == SOLID, own[OPPOSITE[i]], source))
    return out


def relax_row(tile, at):
    wet = tile(0, at) != SOLID
    return relax_wet(stream_row(tile, at), wet)


def stream_patch(values):
    out = [values[0]]
    for i in range(1, Q):
        step_z, step_y, step_x = VELOCITIES[i]
        source = roll(values[i], step_z, 8 * step_y + step_x)
        out.append(jnp.where(source == SOLID, values[OPPOSITE[i]], source))
    return out


def gather_columns(tile, values, rows):
    lane_row = lanes() // 8
    for row, value in zip(rows, values):
        tile = jnp.where(lane_row == row, roll(value, 0, 8 * row + 4), tile)
    return tile


def split_slabs(relative, fluid, new_owner, low, high, moved, kinds, owner, sems):
    copies = [
        pltpu.make_async_copy(fluid, kinds, sems.at[0]),
        pltpu.make_async_copy(relative.at[:, 2:4], high.at[0:Q], sems.at[1]),
        pltpu.make_async_copy(relative.at[:, 0:2], low.at[0:Q], sems.at[2]),
        pltpu.make_async_copy(new_owner, owner, sems.at[3]),
    ]
    for copy in copies:
        copy.start()
    copies[3].wait()
    place = lax.axis_index("gz")
    moved[0] = jnp.full((8, 128), jnp.where((owner[0, 0] == place - 1) & (place > 0), 1.0, 0.0), F32)
    inside = place < lax.axis_size("gz") - 1
    moved[1] = jnp.full((8, 128), jnp.where((owner[0, 1] == place + 1) & inside, 1.0, 0.0), F32)
    copies[0].wait()
    low[Q] = kinds[0:2].astype(F32)
    high[Q] = kinds[2:4].astype(F32)
    copies[1].wait()
    copies[2].wait()


def first_relax(high, low, above, below, moved, own, ahead, back, turn, stage):
    place = lax.axis_index("gz")
    at_low = place == 0
    at_high = place == lax.axis_size("gz") - 1
    swap_low = moved[0] > 0.5
    swap_high = moved[1] > 0.5
    for k in range(2):
        turn[Q, 8 * k : 8 * k + 8] = jnp.where(at_low, 0.0, below[Q, k])
        turn[Q, 8 * (k + 2) : 8 * (k + 3)] = low[Q, k]
        turn[Q, 8 * (k + 4) : 8 * (k + 5)] = high[Q, k]
        turn[Q, 8 * (k + 6) : 8 * (k + 7)] = jnp.where(at_high, 0.0, above[Q, k])
    for i in range(Q):
        for k in range(2):
            mine, other = low[i, k], below[i, k]
            turn[i, 8 * k : 8 * k + 8] = jnp.where(swap_low, mine, other)
            turn[i, 8 * (k + 2) : 8 * (k + 3)] = jnp.where(swap_low, other, mine)
            mine, other = high[i, k], above[i, k]
            turn[i, 8 * (k + 4) : 8 * (k + 5)] = jnp.where(swap_high, other, mine)
            turn[i, 8 * (k + 6) : 8 * (k + 7)] = jnp.where(swap_high, mine, other)
    for row in range(8):
        wet = turn[Q, pl.ds(row, 8, stride=8)] > 0.5
        values = relax_wet([turn[i, pl.ds(row, 8, stride=8)] for i in range(Q)], wet)
        for i in range(Q):
            own[i, row] = values[i]
    up = place % 2 == 0
    for side, (message, high_rows) in enumerate(((ahead, up), (back, jnp.logical_not(up)))):
        first = jnp.where(high_rows, 5, 0)
        far = jnp.where(high_rows, 4, 3)
        for i in range(Q):
            for k in range(3):
                at = 8 * (Y_FIRST[i] + k)
                stage[side, at : at + 8] = own[i, first + k]
        for k in range(5):
            at = 8 * Y_FAR[k]
            stage[side, at : at + 8] = own[jnp.where(high_rows, UP_Y[k], DOWN_Y[k]), far]
        stage[side, 8 * 62 :] = jnp.full((16, 128), SOLID, F32)
        for group in range(8):
            for layer in range(1, 7):
                message[6 * group + layer - 1] = stage[side, pl.ds(64 * group + layer, 8, stride=8)]
        for group in range(2):
            message[48 + group] = stage[side, pl.ds(64 * group, 8, stride=8)]
            message[50 + group] = stage[side, pl.ds(64 * (group + 2) + 7, 8, stride=8)]


def own_rows(own, main, edge):
    for i in range(Q):
        rows = [own[i, k] for k in range(8)]
        main[i, 0] = jnp.full((8, 128), SOLID, F32)
        main[i, 15] = jnp.full((8, 128), SOLID, F32)
        for k in range(8):
            main[i, 4 + k] = rows[k]
        edge[i] = gather_columns(jnp.full((8, 128), SOLID, F32), rows, range(4, 12))


def join_rows(main_in, edge_in, ahead, back, main, edge, x_ahead, x_back, stage):
    place = lax.axis_index("gy")
    up = lax.axis_index("gz") % 2 == 0
    outside_low = place == 0
    outside_high = place == lax.axis_size("gy") - 1
    for side, (message, low_rows) in enumerate(((ahead, up), (back, jnp.logical_not(up)))):
        outside = jnp.where(low_rows, outside_low, outside_high)
        first = jnp.where(low_rows, 1, 12)
        far = jnp.where(low_rows, 0, 15)
        stage[side] = jnp.full((512, 128), SOLID, F32)
        for group in range(8):
            for layer in range(1, 7):
                stage[side, pl.ds(64 * group + layer, 8, stride=8)] = message[6 * group + layer - 1]
        for group in range(2):
            stage[side, pl.ds(64 * group, 8, stride=8)] = message[48 + group]
            stage[side, pl.ds(64 * (group + 2) + 7, 8, stride=8)] = message[50 + group]
        for i in range(Q):
            for k in range(3):
                at = 8 * (Y_FIRST[i] + k)
                main[i, first + k] = jnp.where(outside, SOLID, stage[side, at : at + 8])
        for k in range(5):
            at = 8 * Y_FAR[k]
            value = jnp.where(outside, SOLID, stage[side, at : at + 8])
            main[jnp.where(low_rows, UP_Y[k], DOWN_Y[k]), far] = value
    edges = []
    for i in range(Q):
        beside = [*range(4), *range(12, 16)]
        edges.append(gather_columns(edge[i], [main[i, k] for k in beside], beside))
        edge[i] = edges[i]
    low_side = lanes() % 8 < 4
    for i in range(10):
        if i + 10 < Q:
            to_low = jnp.where(low_side, roll(edges[i + 10], 0, -4), edges[i])
            to_high = jnp.where(low_side, edges[i], roll(edges[i + 10], 0, 4))
            x_ahead[i] = jnp.where(up, to_high, to_low)
            x_back[i] = jnp.where(up, to_low, to_high)
        else:
            x_ahead[i] = edges[i]
            x_back[i] = edges[i]


def two_steps(main, out, edge, middle):
    def first(row):
        values = relax_row(lambda i, at: main[i, at], row)
        for i in range(Q):
            middle[i, row - 1] = values[i]

    def second(row):
        values = relax_row(lambda i, at: middle[i, at], row - 1)
        for i in range(Q):
            out[i, row - 2] = values[i]

    for row in range(1, 15):
        first(row)
    for row in range(2, 14):
        second(row)
    for i in range(Q):
        edge[i] = gather_columns(out[i, 0], [out[i, k] for k in range(12)], range(2, 14))


def patch_two_steps(inner, inner_edge, edge, ahead, back, flat, below, above):
    up = lax.axis_index("gz") % 2 == 0
    place = lax.axis_index("gx")
    at_low = place == 0
    at_high = place == lax.axis_size("gx") - 1
    column = lanes() % 8
    low_side = column < 4
    sides = []
    for side in range(2):
        values = []
        for i in range(Q):
            message = jnp.where(up == (side == 0), ahead[i % 10], back[i % 10])
            if i >= 10:
                message = roll(message, 0, (-4, 4)[side])
            message = jnp.where((at_low, at_high)[side], SOLID, message)
            if side == 0:
                values.append(jnp.where(low_side, message, edge[i]))
            else:
                values.append(jnp.where(low_side, edge[i], message))
        sides.append(values)
    for step in range(2):
        for side in range(2):
            wet = sides[side][0] != SOLID
            sides[side] = relax_wet(stream_patch(sides[side]), wet)
    lane = lanes()
    seam = (lane < 2) | (lane >= 126)
    for i in range(Q):
        own_columns = jnp.where(low_side, sides[1][i], sides[0][i])
        first = PER_SLOT * SLOT[i]
        for row in range(12):
            value = jnp.where(seam, roll(own_columns, 0, -(8 * (row + 2) + 4)), inner[i, row])
            flat[8 * (first + row) : 8 * (first + row) + 8] = value
        fresh = inner_edge[i]
        for side in range(2):
            stale = (column < 6) if side == 0 else (column >= 2)
            at = 8 * (first + 12 + side)
            flat[at : at + 8] = jnp.where(stale, sides[side][i], fresh)
    flat[8 * PER_SLOT * Q :] = jnp.full((FLAT_ROWS - 8 * PER_SLOT * Q, 128), SOLID, F32)
    for group in range(NEAR):
        above[group] = flat[pl.ds(64 * group + 5, 8, stride=8)]
        below[group] = flat[pl.ds(64 * group + 2, 8, stride=8)]
    for group in range(FAR):
        above[NEAR + group] = flat[pl.ds(64 * group + 4, 8, stride=8)]
        below[NEAR + group] = flat[pl.ds(8 * 5 * PER_SLOT + 64 * group + 3, 8, stride=8)]


def last_two_steps(
    flat_in, below, above, block_fluid, out, block_density, flat, middle, turn, patch, columns, final, wet_count, mean, sems
):
    count_copy = pltpu.make_async_copy(block_fluid, wet_count, sems.at[4])
    count_copy.start()
    place = lax.axis_index("gz")
    at_low = place == 0
    at_high = place == lax.axis_size("gz") - 1
    lane = lanes()
    low_side = lane % 8 < 4
    for group in range(NEAR):
        flat[pl.ds(64 * group + 1, 8, stride=8)] = jnp.where(at_low, SOLID, below[group])
        flat[pl.ds(64 * group + 6, 8, stride=8)] = jnp.where(at_high, SOLID, above[group])
    for group in range(FAR):
        flat[pl.ds(64 * group, 8, stride=8)] = jnp.where(at_low, SOLID, below[NEAR + group])
        flat[pl.ds(8 * 5 * PER_SLOT + 64 * group + 7, 8, stride=8)] = jnp.where(
            at_high, SOLID, above[NEAR + group]
        )

    def joined(i, at):
        return flat[pl.ds(8 * (PER_SLOT * SLOT[i] + at), 8)]

    def third(row):
        values = relax_row(joined, row - 2)
        for i in range(Q):
            middle[i, row - 3] = values[i]

    for side in range(2):
        values = [joined(i, 12 + side) for i in range(Q)]
        wet = values[0] != SOLID
        values = relax_wet(stream_patch(values), wet)
        for i in range(Q):
            patch[side, i] = values[i]
    for row in range(3, 13):
        third(row)
    streamed = [stream_patch([patch[side, i] for i in range(Q)]) for side in range(2)]
    for i in range(Q):
        columns[i] = jnp.where(low_side, streamed[1][i], streamed[0][i])
    seam = (lane < 2) | (lane >= 126)
    mass = jnp.zeros((8, 128), F32)
    for row in range(8):
        wet = middle[0, row + 1] != SOLID
        values = stream_row(lambda i, at: middle[i, at], row + 1)
        for i in range(Q):
            value = jnp.where(seam, roll(columns[i], 0, -(8 * (row + 4) + 4)), values[i])
            values[i] = jnp.where(wet, value, 0.0)
            turn[i, 8 * row : 8 * row + 8] = values[i]
        axis_sum = functools.reduce(jnp.add, values[1:7])
        edge_sum = functools.reduce(jnp.add, values[7:])
        mass += values[0] * (1.0 / 3.0) + axis_sum * (1.0 / 18.0) + edge_sum * (1.0 / 36.0)
    mass = jnp.sum(mass, axis=1, keepdims=True)
    layer = lax.broadcasted_iota(jnp.int32, (8, 1), 0) // 2
    totals = [jnp.sum(jnp.where(layer == slot + 1, mass, 0.0), axis=0, keepdims=True) for slot in range(2)]
    slot = lax.broadcasted_iota(jnp.int32, (1, 2), 1)
    totals = jnp.where(slot == 0, totals[0], totals[1])
    copies = []
    for layer in range(4):
        for i in range(Q):
            final[i, layer] = turn[i, pl.ds(layer + 2, 8, stride=8)]
        copies.append(pltpu.make_async_copy(final.at[:, layer], out.at[:, layer], sems.at[layer]))
        copies[-1].start()
    count_copy.wait()
    mean[...] = totals / jnp.maximum(wet_count[...], 1).astype(F32)
    copies.append(pltpu.make_async_copy(mean, block_density, sems.at[5]))
    copies[-1].start()
    for copy in copies:
        copy.wait()


def ring_exchange(to_low, to_high, axis):
    count = lax.axis_size(axis)
    up = [(i, (i + 1) % count) for i in range(count)]
    down = [(target, source) for source, target in up]
    return lax.ppermute(to_high, axis, up), lax.ppermute(to_low, axis, down)


def loop_exchange(ahead, back, axis):
    count = lax.axis_size(axis)
    layers = lax.axis_size("gz")
    pairs = []
    for i in range(count):
        for layer in range(layers):
            if layer % 2 == 0:
                target = (i + 1, layer) if i < count - 1 else (i, layer + 1)
            else:
                target = (i - 1, layer) if i > 0 else (i, layer - 1)
            pairs.append((i * layers + layer, target[0] * layers + target[1]))
    inverse = [(target, source) for source, target in pairs]
    axes = (axis, "gz")
    return lax.ppermute(ahead, axes, pairs), lax.ppermute(back, axes, inverse)


def call(kernel, outs, in_specs, out_specs=None, scratch=(), aliases=None, vmem=32):
    if out_specs is None:
        out_specs = [VMEM] * len(outs)
    return pl.pallas_call(
        kernel,
        out_shape=outs,
        in_specs=in_specs,
        out_specs=out_specs,
        scratch_shapes=list(scratch),
        input_output_aliases=aliases or {},
        compiler_params=pltpu.CompilerParams(vmem_limit_bytes=vmem * 1024 * 1024),
    )


def in_hbm(array):
    return pltpu.with_memory_space_constraint(array, pltpu.HBM)


def on_device(relative, fluid, block_fluid, new_owner):
    low, high, moved = call(
        split_slabs,
        [shape(Q + 1, 2, 8, 128), shape(Q + 1, 2, 8, 128), shape(2, 8, 128)],
        [HBM] * 3,
        scratch=[
            pltpu.VMEM((4, 8, 128), jnp.int32),
            pltpu.SMEM((1, 2), jnp.int32),
            pltpu.SemaphoreType.DMA((4,)),
        ],
    )(in_hbm(relative), in_hbm(fluid), in_hbm(new_owner.transpose(1, 2, 0).reshape(1, 2)))
    below, above = ring_exchange(low, high, "gz")
    own, ahead, back = call(
        first_relax,
        [shape(Q, 8, 8, 128), shape(Y_TILES, 8, 128), shape(Y_TILES, 8, 128)],
        [VMEM] * 5,
        scratch=[pltpu.VMEM((Q + 1, 64, 128), F32), pltpu.VMEM((2, 512, 128), F32)],
    )(high, low, above, below, moved)
    ahead, back = loop_exchange(ahead, back, "gy")
    main, edge = call(own_rows, [shape(Q, 16, 8, 128), shape(Q, 8, 128)], [VMEM])(own)
    main, edge, x_ahead, x_back = call(
        join_rows,
        [shape(Q, 16, 8, 128), shape(Q, 8, 128), shape(10, 8, 128), shape(10, 8, 128)],
        [VMEM] * 4,
        scratch=[pltpu.VMEM((2, 512, 128), F32)],
        aliases={0: 0, 1: 1},
    )(main, edge, ahead, back)
    x_ahead, x_back = loop_exchange(x_ahead, x_back, "gx")
    inner, inner_edge = call(
        two_steps,
        [shape(Q, 12, 8, 128), shape(Q, 8, 128)],
        [VMEM],
        scratch=[pltpu.VMEM((Q, 14, 8, 128), F32)],
    )(main)
    flat, z_low, z_high = call(
        patch_two_steps,
        [shape(FLAT_ROWS, 128), shape(NEAR + FAR, 8, 128), shape(NEAR + FAR, 8, 128)],
        [VMEM] * 5,
    )(inner, inner_edge, edge, x_ahead, x_back)
    below, above = ring_exchange(z_low, z_high, "gz")
    out, block_density, _ = call(
        last_two_steps,
        [shape(Q, 4, 8, 128), shape(1, 2), shape(FLAT_ROWS, 128)],
        [VMEM] * 3 + [HBM],
        [HBM, HBM, VMEM],
        scratch=[
            pltpu.VMEM((Q, 10, 8, 128), F32),
            pltpu.VMEM((Q, 64, 128), F32),
            pltpu.VMEM((2, Q, 8, 128), F32),
            pltpu.VMEM((Q, 8, 128), F32),
            pltpu.VMEM((Q, 4, 8, 128), F32),
            pltpu.VMEM((1, 2), jnp.int32),
            pltpu.VMEM((1, 2), F32),
            pltpu.SemaphoreType.DMA((6,)),
        ],
        aliases={0: 2},
    )(flat, below, above, in_hbm(block_fluid.transpose(1, 2, 0).reshape(1, 2)))
    return out, block_density.reshape(1, 1, 2).transpose(2, 0, 1)


def solution(mesh):
    return jax.shard_map(
        on_device,
        mesh=mesh,
        in_specs=(
            P(None, "gz", "gy", "gx"),
            P("gz", "gy", "gx"),
            P("gz", "gy", "gx"),
            P("gz", "gy", "gx"),
        ),
        out_specs=(P(None, "gz", "gy", "gx"), P("gz", "gy", "gx")),
        check_vma=False,
    )
```

```python
import functools

import jax
import jax.numpy as jnp
from jax import lax
from jax.experimental import pallas as pl
from jax.experimental.pallas import tpu as pltpu
from jax.sharding import PartitionSpec as P


VELOCITIES = [
    (0, 0, 0),
    (1, 0, 0),
    (-1, 0, 0),
    (0, 1, 0),
    (0, -1, 0),
    (0, 0, 1),
    (0, 0, -1),
    (1, 1, 0),
    (-1, -1, 0),
    (1, -1, 0),
    (-1, 1, 0),
    (1, 0, 1),
    (-1, 0, -1),
    (1, 0, -1),
    (-1, 0, 1),
    (0, 1, 1),
    (0, -1, -1),
    (0, 1, -1),
    (0, -1, 1),
]
OPPOSITE = [0, 2, 1, 4, 3, 6, 5, 8, 7, 10, 9, 12, 11, 14, 13, 16, 15, 18, 17]
Q = 19
SOLID = 3.0e38
Z_ORDER = sorted(range(Q), key=lambda i: {1: 0, -1: 1, 0: 2}[VELOCITIES[i][0]])
SLOT = [Z_ORDER.index(i) for i in range(Q)]
UP_Y = [i for i in Z_ORDER if VELOCITIES[i][1] == 1]
DOWN_Y = [i for i in Z_ORDER if VELOCITIES[i][1] == -1]
Y_FIRST = [3 * s + min(s // 5, 2) for s in SLOT]
Y_FAR = [15, 31, 59, 60, 61]
Y_TILES = 52
PER_SLOT = 14
NEAR = 34
FAR = 9
FLAT_ROWS = 8 * 8 * NEAR
F32 = jnp.float32
VMEM = pl.BlockSpec(memory_space=pltpu.VMEM)
SMEM = pl.BlockSpec(memory_space=pltpu.SMEM)
HBM = pl.BlockSpec(memory_space=pltpu.HBM)


def shape(*dims):
    return jax.ShapeDtypeStruct(dims, F32)


def lanes():
    return lax.broadcasted_iota(jnp.int32, (8, 128), 1)


def sublanes():
    return lax.broadcasted_iota(jnp.int32, (8, 128), 0)


def roll(value, sublane_shift, lane_shift):
    if sublane_shift % 8:
        value = pltpu.roll(value, sublane_shift % 8, 0)
    if lane_shift % 128:
        value = pltpu.roll(value, lane_shift % 128, 1)
    return value


def relax(g):
    sums = [g[k] + g[k + 1] for k in range(1, Q, 2)]
    diffs = [g[k] - g[k + 1] for k in range(1, Q, 2)]
    axis_sum = sums[0] + sums[1] + sums[2]
    edge_sum = (sums[3] + sums[4]) + (sums[5] + sums[6]) + (sums[7] + sums[8])
    density = 12.0 * g[0] + 2.0 * axis_sum + edge_sum
    moment_z = 2.0 * diffs[0] + ((diffs[3] + diffs[4]) + (diffs[5] + diffs[6]))
    moment_y = 2.0 * diffs[1] + ((diffs[3] - diffs[4]) + (diffs[7] + diffs[8]))
    moment_x = 2.0 * diffs[2] + ((diffs[5] - diffs[6]) + (diffs[7] - diffs[8]))
    inverse = 1.0 / density
    speed = [moment_z * inverse, moment_y * inverse, moment_x * inverse]
    square = speed[0] * speed[0] + speed[1] * speed[1] + speed[2] * speed[2]
    scaled = density * (1.5 / 36.0)
    base = scaled * (1.0 - 1.5 * square)
    linear = [(4.5 / 36.0) * m for m in (moment_z, moment_y, moment_x)]
    speed = [1.5 * s for s in speed]
    out = [base - 0.5 * g[0]]
    for pair in range(9):
        velocity = VELOCITIES[1 + 2 * pair]
        along = None
        twice = None
        for axis in range(3):
            if velocity[axis] == 0:
                continue
            if along is None:
                along, twice = linear[axis], speed[axis]
            elif velocity[axis] > 0:
                along, twice = along + linear[axis], twice + speed[axis]
            else:
                along, twice = along - linear[axis], twice - speed[axis]
        even = base + along * twice - 0.25 * sums[pair]
        odd = along - 0.25 * diffs[pair]
        out += [even + odd, even - odd]
    return out


def relax_wet(g, wet):
    return [jnp.where(wet, value, SOLID) for value in relax(g)]


def stream_row(tile, at):
    own = [tile(i, at) for i in range(Q)]
    out = [own[0]]
    for i in range(1, Q):
        step_z, step_y, step_x = VELOCITIES[i]
        source = own[i] if step_y == 0 else tile(i, at - step_y)
        source = roll(source, step_z, step_x)
        out.append(jnp.where(source == SOLID, own[OPPOSITE[i]], source))
    return out


def relax_row(tile, at):
    wet = tile(0, at) != SOLID
    return relax_wet(stream_row(tile, at), wet)


def stream_patch(values):
    out = [values[0]]
    for i in range(1, Q):
        step_z, step_y, step_x = VELOCITIES[i]
        source = roll(values[i], step_z, 8 * step_y + step_x)
        out.append(jnp.where(source == SOLID, values[OPPOSITE[i]], source))
    return out


def gather_columns(tile, values, rows):
    lane_row = lanes() // 8
    for row, value in zip(rows, values):
        tile = jnp.where(lane_row == row, roll(value, 0, 8 * row + 4), tile)
    return tile


def split_slabs(relative, fluid, new_owner, low, high, moved, kinds, owner, sems):
    copies = [
        pltpu.make_async_copy(fluid, kinds, sems.at[0]),
        pltpu.make_async_copy(relative.at[:, 2:4], high.at[0:Q], sems.at[1]),
        pltpu.make_async_copy(relative.at[:, 0:2], low.at[0:Q], sems.at[2]),
        pltpu.make_async_copy(new_owner, owner, sems.at[3]),
    ]
    for copy in copies:
        copy.start()
    copies[3].wait()
    place = lax.axis_index("gz")
    moved[0] = jnp.full((8, 128), jnp.where((owner[0, 0] == place - 1) & (place > 0), 1.0, 0.0), F32)
    inside = place < lax.axis_size("gz") - 1
    moved[1] = jnp.full((8, 128), jnp.where((owner[0, 1] == place + 1) & inside, 1.0, 0.0), F32)
    copies[0].wait()
    low[Q] = kinds[0:2].astype(F32)
    high[Q] = kinds[2:4].astype(F32)
    copies[1].wait()
    copies[2].wait()


def first_relax(high, low, above, below, moved, own, ahead, back, turn, stage):
    place = lax.axis_index("gz")
    at_low = place == 0
    at_high = place == lax.axis_size("gz") - 1
    swap_low = moved[0] > 0.5
    swap_high = moved[1] > 0.5
    for k in range(2):
        turn[Q, 8 * k : 8 * k + 8] = jnp.where(at_low, 0.0, below[Q, k])
        turn[Q, 8 * (k + 2) : 8 * (k + 3)] = low[Q, k]
        turn[Q, 8 * (k + 4) : 8 * (k + 5)] = high[Q, k]
        turn[Q, 8 * (k + 6) : 8 * (k + 7)] = jnp.where(at_high, 0.0, above[Q, k])
    for i in range(Q):
        for k in range(2):
            mine, other = low[i, k], below[i, k]
            turn[i, 8 * k : 8 * k + 8] = jnp.where(swap_low, mine, other)
            turn[i, 8 * (k + 2) : 8 * (k + 3)] = jnp.where(swap_low, other, mine)
            mine, other = high[i, k], above[i, k]
            turn[i, 8 * (k + 4) : 8 * (k + 5)] = jnp.where(swap_high, other, mine)
            turn[i, 8 * (k + 6) : 8 * (k + 7)] = jnp.where(swap_high, mine, other)
    for row in range(8):
        wet = turn[Q, pl.ds(row, 8, stride=8)] > 0.5
        values = relax_wet([turn[i, pl.ds(row, 8, stride=8)] for i in range(Q)], wet)
        for i in range(Q):
            own[i, row] = values[i]
    up = place % 2 == 0
    for side, (message, high_rows) in enumerate(((ahead, up), (back, jnp.logical_not(up)))):
        first = jnp.where(high_rows, 5, 0)
        far = jnp.where(high_rows, 4, 3)
        for i in range(Q):
            for k in range(3):
                at = 8 * (Y_FIRST[i] + k)
                stage[side, at : at + 8] = own[i, first + k]
        for k in range(5):
            at = 8 * Y_FAR[k]
            stage[side, at : at + 8] = own[jnp.where(high_rows, UP_Y[k], DOWN_Y[k]), far]
        stage[side, 8 * 62 :] = jnp.full((16, 128), SOLID, F32)
        for group in range(8):
            for layer in range(1, 7):
                message[6 * group + layer - 1] = stage[side, pl.ds(64 * group + layer, 8, stride=8)]
        for group in range(2):
            message[48 + group] = stage[side, pl.ds(64 * group, 8, stride=8)]
            message[50 + group] = stage[side, pl.ds(64 * (group + 2) + 7, 8, stride=8)]


def own_rows(own, main, edge):
    for i in range(Q):
        rows = [own[i, k] for k in range(8)]
        main[i, 0] = jnp.full((8, 128), SOLID, F32)
        main[i, 15] = jnp.full((8, 128), SOLID, F32)
        for k in range(8):
            main[i, 4 + k] = rows[k]
        edge[i] = gather_columns(jnp.full((8, 128), SOLID, F32), rows, range(4, 12))


def join_rows(main_in, edge_in, ahead, back, main, edge, x_ahead, x_back, stage):
    place = lax.axis_index("gy")
    up = lax.axis_index("gz") % 2 == 0
    outside_low = place == 0
    outside_high = place == lax.axis_size("gy") - 1
    for side, (message, low_rows) in enumerate(((ahead, up), (back, jnp.logical_not(up)))):
        outside = jnp.where(low_rows, outside_low, outside_high)
        first = jnp.where(low_rows, 1, 12)
        far = jnp.where(low_rows, 0, 15)
        stage[side] = jnp.full((512, 128), SOLID, F32)
        for group in range(8):
            for layer in range(1, 7):
                stage[side, pl.ds(64 * group + layer, 8, stride=8)] = message[6 * group + layer - 1]
        for group in range(2):
            stage[side, pl.ds(64 * group, 8, stride=8)] = message[48 + group]
            stage[side, pl.ds(64 * (group + 2) + 7, 8, stride=8)] = message[50 + group]
        for i in range(Q):
            for k in range(3):
                at = 8 * (Y_FIRST[i] + k)
                main[i, first + k] = jnp.where(outside, SOLID, stage[side, at : at + 8])
        for k in range(5):
            at = 8 * Y_FAR[k]
            value = jnp.where(outside, SOLID, stage[side, at : at + 8])
            main[jnp.where(low_rows, UP_Y[k], DOWN_Y[k]), far] = value
    edges = []
    for i in range(Q):
        beside = [*range(4), *range(12, 16)]
        edges.append(gather_columns(edge[i], [main[i, k] for k in beside], beside))
        edge[i] = edges[i]
    low_side = lanes() % 8 < 4
    for i in range(10):
        if i + 10 < Q:
            to_low = jnp.where(low_side, roll(edges[i + 10], 0, -4), edges[i])
            to_high = jnp.where(low_side, edges[i], roll(edges[i + 10], 0, 4))
            x_ahead[i] = jnp.where(up, to_high, to_low)
            x_back[i] = jnp.where(up, to_low, to_high)
        else:
            x_ahead[i] = edges[i]
            x_back[i] = edges[i]


def two_steps(main, out, edge, middle):
    def first(row):
        values = relax_row(lambda i, at: main[i, at], row)
        for i in range(Q):
            middle[i, row - 1] = values[i]

    def second(row):
        values = relax_row(lambda i, at: middle[i, at], row - 1)
        for i in range(Q):
            out[i, row - 2] = values[i]

    for row in range(1, 15):
        first(row)
    for row in range(2, 14):
        second(row)
    for i in range(Q):
        edge[i] = gather_columns(out[i, 0], [out[i, k] for k in range(12)], range(2, 14))


def side_two_steps(edge, message, at_low_end):
    place = lax.axis_index("gx")
    outside = place == jnp.where(at_low_end, 0, lax.axis_size("gx") - 1)
    low_side = lanes() % 8 < 4
    values = []
    for i in range(Q):
        beside = message[i % 10]
        if i >= 10:
            beside = jnp.where(at_low_end, roll(beside, 0, -4), roll(beside, 0, 4))
        beside = jnp.where(outside, SOLID, beside)
        low = jnp.where(at_low_end, beside, edge[i])
        high = jnp.where(at_low_end, edge[i], beside)
        values.append(jnp.where(low_side, low, high))
    for step in range(2):
        wet = values[0] != SOLID
        values = relax_wet(stream_patch(values), wet)
    return values


def first_side(edge, ahead, side):
    values = side_two_steps(edge, ahead, lax.rem(lax.axis_index("gz"), 2) == 0)
    for i in range(Q):
        side[i] = values[i]


def patch_two_steps(inner, inner_edge, edge, side_ahead, back, flat, z_low, z_high):
    up = lax.rem(lax.axis_index("gz"), 2) == 0
    column = lanes() % 8
    low_side = column < 4
    other = side_two_steps(edge, back, jnp.logical_not(up))
    sides = [
        [jnp.where(up, side_ahead[i], other[i]) for i in range(Q)],
        [jnp.where(up, other[i], side_ahead[i]) for i in range(Q)],
    ]
    lane = lanes()
    seam = (lane < 2) | (lane >= 126)
    for i in range(Q):
        own_columns = jnp.where(low_side, sides[1][i], sides[0][i])
        first = PER_SLOT * SLOT[i]
        for row in range(12):
            value = jnp.where(seam, roll(own_columns, 0, -(8 * (row + 2) + 4)), inner[i, row])
            flat[8 * (first + row) : 8 * (first + row) + 8] = value
        fresh = inner_edge[i]
        for side in range(2):
            stale = (column < 6) if side == 0 else (column >= 2)
            at = 8 * (first + 12 + side)
            flat[at : at + 8] = jnp.where(stale, sides[side][i], fresh)
    flat[8 * PER_SLOT * Q :] = jnp.full((FLAT_ROWS - 8 * PER_SLOT * Q, 128), SOLID, F32)
    for group in range(NEAR):
        z_high[group] = flat[pl.ds(64 * group + 5, 8, stride=8)]
        z_low[group] = flat[pl.ds(64 * group + 2, 8, stride=8)]
    for group in range(FAR):
        z_high[NEAR + group] = flat[pl.ds(64 * group + 4, 8, stride=8)]
        z_low[NEAR + group] = flat[pl.ds(8 * 5 * PER_SLOT + 64 * group + 3, 8, stride=8)]


def last_two_steps(
    flat_in, below, above, block_fluid, out, block_density, flat, middle, turn, patch, columns, final, wet_count, mean, sems
):
    count_copy = pltpu.make_async_copy(block_fluid, wet_count, sems.at[4])
    count_copy.start()
    place = lax.axis_index("gz")
    at_low = place == 0
    at_high = place == lax.axis_size("gz") - 1
    lane = lanes()
    low_side = lane % 8 < 4
    for group in range(NEAR):
        flat[pl.ds(64 * group + 1, 8, stride=8)] = jnp.where(at_low, SOLID, below[group])
        flat[pl.ds(64 * group + 6, 8, stride=8)] = jnp.where(at_high, SOLID, above[group])
    for group in range(FAR):
        flat[pl.ds(64 * group, 8, stride=8)] = jnp.where(at_low, SOLID, below[NEAR + group])
        flat[pl.ds(8 * 5 * PER_SLOT + 64 * group + 7, 8, stride=8)] = jnp.where(
            at_high, SOLID, above[NEAR + group]
        )

    def joined(i, at):
        return flat[pl.ds(8 * (PER_SLOT * SLOT[i] + at), 8)]

    def third(row):
        values = relax_row(joined, row - 2)
        for i in range(Q):
            middle[i, row - 3] = values[i]

    for side in range(2):
        values = [joined(i, 12 + side) for i in range(Q)]
        wet = values[0] != SOLID
        values = relax_wet(stream_patch(values), wet)
        for i in range(Q):
            patch[side, i] = values[i]
    for row in range(3, 13):
        third(row)
    streamed = [stream_patch([patch[side, i] for i in range(Q)]) for side in range(2)]
    for i in range(Q):
        columns[i] = jnp.where(low_side, streamed[1][i], streamed[0][i])
    seam = (lane < 2) | (lane >= 126)
    mass = jnp.zeros((8, 128), F32)
    for row in range(8):
        wet = middle[0, row + 1] != SOLID
        values = stream_row(lambda i, at: middle[i, at], row + 1)
        for i in range(Q):
            value = jnp.where(seam, roll(columns[i], 0, -(8 * (row + 4) + 4)), values[i])
            values[i] = jnp.where(wet, value, 0.0)
            turn[i, 8 * row : 8 * row + 8] = values[i]
        axis_sum = functools.reduce(jnp.add, values[1:7])
        edge_sum = functools.reduce(jnp.add, values[7:])
        mass += values[0] * (1.0 / 3.0) + axis_sum * (1.0 / 18.0) + edge_sum * (1.0 / 36.0)
    mass = jnp.sum(mass, axis=1, keepdims=True)
    layer = lax.broadcasted_iota(jnp.int32, (8, 1), 0) // 2
    totals = [jnp.sum(jnp.where(layer == slot + 1, mass, 0.0), axis=0, keepdims=True) for slot in range(2)]
    slot = lax.broadcasted_iota(jnp.int32, (1, 2), 1)
    totals = jnp.where(slot == 0, totals[0], totals[1])
    copies = []
    for layer in range(4):
        for i in range(Q):
            final[i, layer] = turn[i, pl.ds(layer + 2, 8, stride=8)]
        copies.append(pltpu.make_async_copy(final.at[:, layer], out.at[:, layer], sems.at[layer]))
        copies[-1].start()
    count_copy.wait()
    mean[...] = totals / jnp.maximum(wet_count[...], 1).astype(F32)
    copies.append(pltpu.make_async_copy(mean, block_density, sems.at[5]))
    copies[-1].start()
    for copy in copies:
        copy.wait()


def ring_exchange(to_low, to_high, axis):
    count = lax.axis_size(axis)
    up = [(i, (i + 1) % count) for i in range(count)]
    down = [(target, source) for source, target in up]
    return lax.ppermute(to_high, axis, up), lax.ppermute(to_low, axis, down)


def loop_exchange(ahead, back, axis):
    count = lax.axis_size(axis)
    layers = lax.axis_size("gz")
    pairs = []
    for i in range(count):
        for layer in range(layers):
            if layer % 2 == 0:
                target = (i + 1, layer) if i < count - 1 else (i, layer + 1)
            else:
                target = (i - 1, layer) if i > 0 else (i, layer - 1)
            pairs.append((i * layers + layer, target[0] * layers + target[1]))
    inverse = [(target, source) for source, target in pairs]
    axes = (axis, "gz")
    return lax.ppermute(ahead, axes, pairs), lax.ppermute(back, axes, inverse)


def call(kernel, outs, in_specs, out_specs=None, scratch=(), aliases=None, vmem=32):
    if out_specs is None:
        out_specs = [VMEM] * len(outs)
    return pl.pallas_call(
        kernel,
        out_shape=outs,
        in_specs=in_specs,
        out_specs=out_specs,
        scratch_shapes=list(scratch),
        input_output_aliases=aliases or {},
        compiler_params=pltpu.CompilerParams(vmem_limit_bytes=vmem * 1024 * 1024),
    )


def in_hbm(array):
    return pltpu.with_memory_space_constraint(array, pltpu.HBM)


def on_device(relative, fluid, block_fluid, new_owner):
    low, high, moved = call(
        split_slabs,
        [shape(Q + 1, 2, 8, 128), shape(Q + 1, 2, 8, 128), shape(2, 8, 128)],
        [HBM] * 3,
        scratch=[
            pltpu.VMEM((4, 8, 128), jnp.int32),
            pltpu.SMEM((1, 2), jnp.int32),
            pltpu.SemaphoreType.DMA((4,)),
        ],
    )(in_hbm(relative), in_hbm(fluid), in_hbm(new_owner.transpose(1, 2, 0).reshape(1, 2)))
    below, above = ring_exchange(low, high, "gz")
    own, ahead, back = call(
        first_relax,
        [shape(Q, 8, 8, 128), shape(Y_TILES, 8, 128), shape(Y_TILES, 8, 128)],
        [VMEM] * 5,
        scratch=[pltpu.VMEM((Q + 1, 64, 128), F32), pltpu.VMEM((2, 512, 128), F32)],
    )(high, low, above, below, moved)
    ahead, back = loop_exchange(ahead, back, "gy")
    main, edge = call(own_rows, [shape(Q, 16, 8, 128), shape(Q, 8, 128)], [VMEM])(own)
    main, edge, x_ahead, x_back = call(
        join_rows,
        [shape(Q, 16, 8, 128), shape(Q, 8, 128), shape(10, 8, 128), shape(10, 8, 128)],
        [VMEM] * 4,
        scratch=[pltpu.VMEM((2, 512, 128), F32)],
        aliases={0: 0, 1: 1},
    )(main, edge, ahead, back)
    x_ahead, x_back = loop_exchange(x_ahead, x_back, "gx")
    inner, inner_edge = call(
        two_steps,
        [shape(Q, 12, 8, 128), shape(Q, 8, 128)],
        [VMEM],
        scratch=[pltpu.VMEM((Q, 14, 8, 128), F32)],
    )(main)
    side = call(first_side, [shape(Q, 8, 128)], [VMEM] * 2)(edge, x_ahead)[0]
    flat, z_low, z_high = call(
        patch_two_steps,
        [shape(FLAT_ROWS, 128), shape(NEAR + FAR, 8, 128), shape(NEAR + FAR, 8, 128)],
        [VMEM] * 5,
    )(inner, inner_edge, edge, side, x_back)
    below, above = ring_exchange(z_low, z_high, "gz")
    out, block_density, _ = call(
        last_two_steps,
        [shape(Q, 4, 8, 128), shape(1, 2), shape(FLAT_ROWS, 128)],
        [VMEM] * 3 + [HBM],
        [HBM, HBM, VMEM],
        scratch=[
            pltpu.VMEM((Q, 10, 8, 128), F32),
            pltpu.VMEM((Q, 64, 128), F32),
            pltpu.VMEM((2, Q, 8, 128), F32),
            pltpu.VMEM((Q, 8, 128), F32),
            pltpu.VMEM((Q, 4, 8, 128), F32),
            pltpu.VMEM((1, 2), jnp.int32),
            pltpu.VMEM((1, 2), F32),
            pltpu.SemaphoreType.DMA((6,)),
        ],
        aliases={0: 2},
    )(flat, below, above, in_hbm(block_fluid.transpose(1, 2, 0).reshape(1, 2)))
    return out, block_density.reshape(1, 1, 2).transpose(2, 0, 1)


def solution(mesh):
    return jax.shard_map(
        on_device,
        mesh=mesh,
        in_specs=(
            P(None, "gz", "gy", "gx"),
            P("gz", "gy", "gx"),
            P("gz", "gy", "gx"),
            P("gz", "gy", "gx"),
        ),
        out_specs=(P(None, "gz", "gy", "gx"), P("gz", "gy", "gx")),
        check_vma=False,
    )
```

```python
import functools

import jax
import jax.numpy as jnp
from jax import lax
from jax.experimental import pallas as pl
from jax.experimental.pallas import tpu as pltpu
from jax.sharding import PartitionSpec as P


VELOCITIES = [
    (0, 0, 0),
    (1, 0, 0),
    (-1, 0, 0),
    (0, 1, 0),
    (0, -1, 0),
    (0, 0, 1),
    (0, 0, -1),
    (1, 1, 0),
    (-1, -1, 0),
    (1, -1, 0),
    (-1, 1, 0),
    (1, 0, 1),
    (-1, 0, -1),
    (1, 0, -1),
    (-1, 0, 1),
    (0, 1, 1),
    (0, -1, -1),
    (0, 1, -1),
    (0, -1, 1),
]
OPPOSITE = [0, 2, 1, 4, 3, 6, 5, 8, 7, 10, 9, 12, 11, 14, 13, 16, 15, 18, 17]
Q = 19
SOLID = 3.0e38
Z_ORDER = sorted(range(Q), key=lambda i: {1: 0, -1: 1, 0: 2}[VELOCITIES[i][0]])
SLOT = [Z_ORDER.index(i) for i in range(Q)]
UP_Y = [i for i in Z_ORDER if VELOCITIES[i][1] == 1]
DOWN_Y = [i for i in Z_ORDER if VELOCITIES[i][1] == -1]
Y_FIRST = [3 * s + min(s // 5, 2) for s in SLOT]
Y_FAR = [15, 31, 59, 60, 61]
Y_TILES = 52
PER_SLOT = 14
NEAR = 34
FAR = 9
FLAT_ROWS = 8 * 8 * NEAR
F32 = jnp.float32
VMEM = pl.BlockSpec(memory_space=pltpu.VMEM)
SMEM = pl.BlockSpec(memory_space=pltpu.SMEM)
HBM = pl.BlockSpec(memory_space=pltpu.HBM)


def shape(*dims):
    return jax.ShapeDtypeStruct(dims, F32)


def lanes():
    return lax.broadcasted_iota(jnp.int32, (8, 128), 1)


def sublanes():
    return lax.broadcasted_iota(jnp.int32, (8, 128), 0)


def roll(value, sublane_shift, lane_shift):
    if sublane_shift % 8:
        value = pltpu.roll(value, sublane_shift % 8, 0)
    if lane_shift % 128:
        value = pltpu.roll(value, lane_shift % 128, 1)
    return value


def relax(g):
    sums = [g[k] + g[k + 1] for k in range(1, Q, 2)]
    diffs = [g[k] - g[k + 1] for k in range(1, Q, 2)]
    axis_sum = sums[0] + sums[1] + sums[2]
    edge_sum = (sums[3] + sums[4]) + (sums[5] + sums[6]) + (sums[7] + sums[8])
    density = 12.0 * g[0] + 2.0 * axis_sum + edge_sum
    moment_z = 2.0 * diffs[0] + ((diffs[3] + diffs[4]) + (diffs[5] + diffs[6]))
    moment_y = 2.0 * diffs[1] + ((diffs[3] - diffs[4]) + (diffs[7] + diffs[8]))
    moment_x = 2.0 * diffs[2] + ((diffs[5] - diffs[6]) + (diffs[7] - diffs[8]))
    inverse = 1.0 / density
    speed = [moment_z * inverse, moment_y * inverse, moment_x * inverse]
    square = speed[0] * speed[0] + speed[1] * speed[1] + speed[2] * speed[2]
    scaled = density * (1.5 / 36.0)
    base = scaled * (1.0 - 1.5 * square)
    linear = [(4.5 / 36.0) * m for m in (moment_z, moment_y, moment_x)]
    speed = [1.5 * s for s in speed]
    out = [base - 0.5 * g[0]]
    for pair in range(9):
        velocity = VELOCITIES[1 + 2 * pair]
        along = None
        twice = None
        for axis in range(3):
            if velocity[axis] == 0:
                continue
            if along is None:
                along, twice = linear[axis], speed[axis]
            elif velocity[axis] > 0:
                along, twice = along + linear[axis], twice + speed[axis]
            else:
                along, twice = along - linear[axis], twice - speed[axis]
        even = base + along * twice - 0.25 * sums[pair]
        odd = along - 0.25 * diffs[pair]
        out += [even + odd, even - odd]
    return out


def relax_wet(g, wet):
    return [jnp.where(wet, value, SOLID) for value in relax(g)]


def stream_row(tile, at):
    own = [tile(i, at) for i in range(Q)]
    out = [own[0]]
    for i in range(1, Q):
        step_z, step_y, step_x = VELOCITIES[i]
        source = own[i] if step_y == 0 else tile(i, at - step_y)
        source = roll(source, step_z, step_x)
        out.append(jnp.where(source == SOLID, own[OPPOSITE[i]], source))
    return out


def relax_row(tile, at):
    wet = tile(0, at) != SOLID
    return relax_wet(stream_row(tile, at), wet)


def stream_patch(values):
    out = [values[0]]
    for i in range(1, Q):
        step_z, step_y, step_x = VELOCITIES[i]
        source = roll(values[i], step_z, 8 * step_y + step_x)
        out.append(jnp.where(source == SOLID, values[OPPOSITE[i]], source))
    return out


def gather_columns(tile, values, rows):
    lane_row = lanes() // 8
    for row, value in zip(rows, values):
        tile = jnp.where(lane_row == row, roll(value, 0, 8 * row + 4), tile)
    return tile


def split_slabs(relative, fluid, new_owner, low, high, moved, kinds, owner, sems):
    copies = [
        pltpu.make_async_copy(fluid, kinds, sems.at[0]),
        pltpu.make_async_copy(relative.at[:, 2:4], high.at[0:Q], sems.at[1]),
        pltpu.make_async_copy(relative.at[:, 0:2], low.at[0:Q], sems.at[2]),
        pltpu.make_async_copy(new_owner, owner, sems.at[3]),
    ]
    for copy in copies:
        copy.start()
    copies[3].wait()
    place = lax.axis_index("gz")
    moved[0] = jnp.full((8, 128), jnp.where((owner[0, 0] == place - 1) & (place > 0), 1.0, 0.0), F32)
    inside = place < lax.axis_size("gz") - 1
    moved[1] = jnp.full((8, 128), jnp.where((owner[0, 1] == place + 1) & inside, 1.0, 0.0), F32)
    copies[0].wait()
    low[Q] = kinds[0:2].astype(F32)
    high[Q] = kinds[2:4].astype(F32)
    copies[1].wait()
    copies[2].wait()


def first_relax(high, low, above, below, moved, own, ahead, back, turn, stage):
    place = lax.axis_index("gz")
    at_low = place == 0
    at_high = place == lax.axis_size("gz") - 1
    swap_low = moved[0] > 0.5
    swap_high = moved[1] > 0.5
    for k in range(2):
        turn[Q, 8 * k : 8 * k + 8] = jnp.where(at_low, 0.0, below[Q, k])
        turn[Q, 8 * (k + 2) : 8 * (k + 3)] = low[Q, k]
        turn[Q, 8 * (k + 4) : 8 * (k + 5)] = high[Q, k]
        turn[Q, 8 * (k + 6) : 8 * (k + 7)] = jnp.where(at_high, 0.0, above[Q, k])
    for i in range(Q):
        for k in range(2):
            mine, other = low[i, k], below[i, k]
            turn[i, 8 * k : 8 * k + 8] = jnp.where(swap_low, mine, other)
            turn[i, 8 * (k + 2) : 8 * (k + 3)] = jnp.where(swap_low, other, mine)
            mine, other = high[i, k], above[i, k]
            turn[i, 8 * (k + 4) : 8 * (k + 5)] = jnp.where(swap_high, other, mine)
            turn[i, 8 * (k + 6) : 8 * (k + 7)] = jnp.where(swap_high, mine, other)
    for row in range(8):
        wet = turn[Q, pl.ds(row, 8, stride=8)] > 0.5
        values = relax_wet([turn[i, pl.ds(row, 8, stride=8)] for i in range(Q)], wet)
        for i in range(Q):
            own[i, row] = values[i]
    up = place % 2 == 0
    for side, (message, high_rows) in enumerate(((ahead, up), (back, jnp.logical_not(up)))):
        first = jnp.where(high_rows, 5, 0)
        far = jnp.where(high_rows, 4, 3)
        for i in range(Q):
            for k in range(3):
                at = 8 * (Y_FIRST[i] + k)
                stage[side, at : at + 8] = own[i, first + k]
        for k in range(5):
            at = 8 * Y_FAR[k]
            stage[side, at : at + 8] = own[jnp.where(high_rows, UP_Y[k], DOWN_Y[k]), far]
        stage[side, 8 * 62 :] = jnp.full((16, 128), SOLID, F32)
        for group in range(8):
            for layer in range(1, 7):
                message[6 * group + layer - 1] = stage[side, pl.ds(64 * group + layer, 8, stride=8)]
        for group in range(2):
            message[48 + group] = stage[side, pl.ds(64 * group, 8, stride=8)]
            message[50 + group] = stage[side, pl.ds(64 * (group + 2) + 7, 8, stride=8)]


def own_rows(own, main, edge):
    for i in range(Q):
        rows = [own[i, k] for k in range(8)]
        main[i, 0] = jnp.full((8, 128), SOLID, F32)
        main[i, 15] = jnp.full((8, 128), SOLID, F32)
        for k in range(8):
            main[i, 4 + k] = rows[k]
        edge[i] = gather_columns(jnp.full((8, 128), SOLID, F32), rows, range(4, 12))


def join_rows(main_in, edge_in, ahead, back, main, edge, x_ahead, x_back, stage):
    place = lax.axis_index("gy")
    up = lax.axis_index("gz") % 2 == 0
    outside_low = place == 0
    outside_high = place == lax.axis_size("gy") - 1
    for side, (message, low_rows) in enumerate(((ahead, up), (back, jnp.logical_not(up)))):
        outside = jnp.where(low_rows, outside_low, outside_high)
        first = jnp.where(low_rows, 1, 12)
        far = jnp.where(low_rows, 0, 15)
        stage[side] = jnp.full((512, 128), SOLID, F32)
        for group in range(8):
            for layer in range(1, 7):
                stage[side, pl.ds(64 * group + layer, 8, stride=8)] = message[6 * group + layer - 1]
        for group in range(2):
            stage[side, pl.ds(64 * group, 8, stride=8)] = message[48 + group]
            stage[side, pl.ds(64 * (group + 2) + 7, 8, stride=8)] = message[50 + group]
        for i in range(Q):
            for k in range(3):
                at = 8 * (Y_FIRST[i] + k)
                main[i, first + k] = jnp.where(outside, SOLID, stage[side, at : at + 8])
        for k in range(5):
            at = 8 * Y_FAR[k]
            value = jnp.where(outside, SOLID, stage[side, at : at + 8])
            main[jnp.where(low_rows, UP_Y[k], DOWN_Y[k]), far] = value
    edges = []
    for i in range(Q):
        beside = [*range(4), *range(12, 16)]
        edges.append(gather_columns(edge[i], [main[i, k] for k in beside], beside))
        edge[i] = edges[i]
    low_side = lanes() % 8 < 4
    for i in range(10):
        if i + 10 < Q:
            to_low = jnp.where(low_side, roll(edges[i + 10], 0, -4), edges[i])
            to_high = jnp.where(low_side, edges[i], roll(edges[i + 10], 0, 4))
            x_ahead[i] = jnp.where(up, to_high, to_low)
            x_back[i] = jnp.where(up, to_low, to_high)
        else:
            x_ahead[i] = edges[i]
            x_back[i] = edges[i]


def two_steps(main, flat, edge, middle):
    def first(row):
        values = relax_row(lambda i, at: main[i, at], row)
        for i in range(Q):
            middle[i, row - 1] = values[i]

    def second(row):
        values = relax_row(lambda i, at: middle[i, at], row - 1)
        for i in range(Q):
            at = 8 * (PER_SLOT * SLOT[i] + row - 2)
            flat[at : at + 8] = values[i]

    for row in range(1, 15):
        first(row)
    for row in range(2, 14):
        second(row)
    for i in range(Q):
        at = 8 * PER_SLOT * SLOT[i]
        rows = [flat[at + 8 * k : at + 8 * k + 8] for k in range(12)]
        edge[i] = gather_columns(rows[0], rows, range(2, 14))
    flat[8 * PER_SLOT * Q :] = jnp.full((FLAT_ROWS - 8 * PER_SLOT * Q, 128), SOLID, F32)


def side_two_steps(edge, message, at_low_end):
    place = lax.axis_index("gx")
    outside = place == jnp.where(at_low_end, 0, lax.axis_size("gx") - 1)
    low_side = lanes() % 8 < 4
    values = []
    for i in range(Q):
        beside = message[i % 10]
        if i >= 10:
            beside = jnp.where(at_low_end, roll(beside, 0, -4), roll(beside, 0, 4))
        beside = jnp.where(outside, SOLID, beside)
        low = jnp.where(at_low_end, beside, edge[i])
        high = jnp.where(at_low_end, edge[i], beside)
        values.append(jnp.where(low_side, low, high))
    for step in range(2):
        wet = values[0] != SOLID
        values = relax_wet(stream_patch(values), wet)
    return values


def first_side(edge, ahead, side):
    values = side_two_steps(edge, ahead, lax.rem(lax.axis_index("gz"), 2) == 0)
    for i in range(Q):
        side[i] = values[i]


def patch_two_steps(flat_in, inner_edge, edge, side_ahead, back, flat, z_low, z_high):
    up = lax.rem(lax.axis_index("gz"), 2) == 0
    column = lanes() % 8
    low_side = column < 4
    other = side_two_steps(edge, back, jnp.logical_not(up))
    sides = [
        [jnp.where(up, side_ahead[i], other[i]) for i in range(Q)],
        [jnp.where(up, other[i], side_ahead[i]) for i in range(Q)],
    ]
    lane = lanes()
    seam = (lane < 2) | (lane >= 126)
    for i in range(Q):
        own_columns = jnp.where(low_side, sides[1][i], sides[0][i])
        first = PER_SLOT * SLOT[i]
        for row in range(12):
            value = roll(own_columns, 0, -(8 * (row + 2) + 4))
            pltpu.store(flat.at[8 * (first + row) : 8 * (first + row) + 8], value, mask=seam)
        fresh = inner_edge[i]
        for side in range(2):
            stale = (column < 6) if side == 0 else (column >= 2)
            at = 8 * (first + 12 + side)
            flat[at : at + 8] = jnp.where(stale, sides[side][i], fresh)
    for group in range(NEAR):
        z_high[group] = flat[pl.ds(64 * group + 5, 8, stride=8)]
        z_low[group] = flat[pl.ds(64 * group + 2, 8, stride=8)]
    for group in range(FAR):
        z_high[NEAR + group] = flat[pl.ds(64 * group + 4, 8, stride=8)]
        z_low[NEAR + group] = flat[pl.ds(8 * 5 * PER_SLOT + 64 * group + 3, 8, stride=8)]


def last_two_steps(
    flat_in, below, above, block_fluid, out, block_density, flat, middle, turn, patch, columns, final, wet_count, mean, sems
):
    count_copy = pltpu.make_async_copy(block_fluid, wet_count, sems.at[4])
    count_copy.start()
    place = lax.axis_index("gz")
    at_low = place == 0
    at_high = place == lax.axis_size("gz") - 1
    lane = lanes()
    low_side = lane % 8 < 4
    for group in range(NEAR):
        flat[pl.ds(64 * group + 1, 8, stride=8)] = jnp.where(at_low, SOLID, below[group])
        flat[pl.ds(64 * group + 6, 8, stride=8)] = jnp.where(at_high, SOLID, above[group])
    for group in range(FAR):
        flat[pl.ds(64 * group, 8, stride=8)] = jnp.where(at_low, SOLID, below[NEAR + group])
        flat[pl.ds(8 * 5 * PER_SLOT + 64 * group + 7, 8, stride=8)] = jnp.where(
            at_high, SOLID, above[NEAR + group]
        )

    def joined(i, at):
        return flat[pl.ds(8 * (PER_SLOT * SLOT[i] + at), 8)]

    def third(row):
        values = relax_row(joined, row - 2)
        for i in range(Q):
            middle[i, row - 3] = values[i]

    for side in range(2):
        values = [joined(i, 12 + side) for i in range(Q)]
        wet = values[0] != SOLID
        values = relax_wet(stream_patch(values), wet)
        for i in range(Q):
            patch[side, i] = values[i]
    for row in range(3, 13):
        third(row)
    streamed = [stream_patch([patch[side, i] for i in range(Q)]) for side in range(2)]
    for i in range(Q):
        columns[i] = jnp.where(low_side, streamed[1][i], streamed[0][i])
    seam = (lane < 2) | (lane >= 126)
    mass = jnp.zeros((8, 128), F32)
    for row in range(8):
        wet = middle[0, row + 1] != SOLID
        values = stream_row(lambda i, at: middle[i, at], row + 1)
        for i in range(Q):
            value = jnp.where(seam, roll(columns[i], 0, -(8 * (row + 4) + 4)), values[i])
            values[i] = jnp.where(wet, value, 0.0)
            turn[i, 8 * row : 8 * row + 8] = values[i]
        axis_sum = functools.reduce(jnp.add, values[1:7])
        edge_sum = functools.reduce(jnp.add, values[7:])
        mass += values[0] * (1.0 / 3.0) + axis_sum * (1.0 / 18.0) + edge_sum * (1.0 / 36.0)
    mass = jnp.sum(mass, axis=1, keepdims=True)
    layer = lax.broadcasted_iota(jnp.int32, (8, 1), 0) // 2
    totals = [jnp.sum(jnp.where(layer == slot + 1, mass, 0.0), axis=0, keepdims=True) for slot in range(2)]
    slot = lax.broadcasted_iota(jnp.int32, (1, 2), 1)
    totals = jnp.where(slot == 0, totals[0], totals[1])
    copies = []
    for layer in range(4):
        for i in range(Q):
            final[i, layer] = turn[i, pl.ds(layer + 2, 8, stride=8)]
        copies.append(pltpu.make_async_copy(final.at[:, layer], out.at[:, layer], sems.at[layer]))
        copies[-1].start()
    count_copy.wait()
    mean[...] = totals / jnp.maximum(wet_count[...], 1).astype(F32)
    copies.append(pltpu.make_async_copy(mean, block_density, sems.at[5]))
    copies[-1].start()
    for copy in copies:
        copy.wait()


def ring_exchange(to_low, to_high, axis):
    count = lax.axis_size(axis)
    up = [(i, (i + 1) % count) for i in range(count)]
    down = [(target, source) for source, target in up]
    return lax.ppermute(to_high, axis, up), lax.ppermute(to_low, axis, down)


def loop_exchange(ahead, back, axis):
    count = lax.axis_size(axis)
    layers = lax.axis_size("gz")
    pairs = []
    for i in range(count):
        for layer in range(layers):
            if layer % 2 == 0:
                target = (i + 1, layer) if i < count - 1 else (i, layer + 1)
            else:
                target = (i - 1, layer) if i > 0 else (i, layer - 1)
            pairs.append((i * layers + layer, target[0] * layers + target[1]))
    inverse = [(target, source) for source, target in pairs]
    axes = (axis, "gz")
    return lax.ppermute(ahead, axes, pairs), lax.ppermute(back, axes, inverse)


def call(kernel, outs, in_specs, out_specs=None, scratch=(), aliases=None, vmem=32):
    if out_specs is None:
        out_specs = [VMEM] * len(outs)
    return pl.pallas_call(
        kernel,
        out_shape=outs,
        in_specs=in_specs,
        out_specs=out_specs,
        scratch_shapes=list(scratch),
        input_output_aliases=aliases or {},
        compiler_params=pltpu.CompilerParams(vmem_limit_bytes=vmem * 1024 * 1024),
    )


def in_hbm(array):
    return pltpu.with_memory_space_constraint(array, pltpu.HBM)


def on_device(relative, fluid, block_fluid, new_owner):
    low, high, moved = call(
        split_slabs,
        [shape(Q + 1, 2, 8, 128), shape(Q + 1, 2, 8, 128), shape(2, 8, 128)],
        [HBM] * 3,
        scratch=[
            pltpu.VMEM((4, 8, 128), jnp.int32),
            pltpu.SMEM((1, 2), jnp.int32),
            pltpu.SemaphoreType.DMA((4,)),
        ],
    )(in_hbm(relative), in_hbm(fluid), in_hbm(new_owner.transpose(1, 2, 0).reshape(1, 2)))
    below, above = ring_exchange(low, high, "gz")
    own, ahead, back = call(
        first_relax,
        [shape(Q, 8, 8, 128), shape(Y_TILES, 8, 128), shape(Y_TILES, 8, 128)],
        [VMEM] * 5,
        scratch=[pltpu.VMEM((Q + 1, 64, 128), F32), pltpu.VMEM((2, 512, 128), F32)],
    )(high, low, above, below, moved)
    ahead, back = loop_exchange(ahead, back, "gy")
    main, edge = call(own_rows, [shape(Q, 16, 8, 128), shape(Q, 8, 128)], [VMEM])(own)
    main, edge, x_ahead, x_back = call(
        join_rows,
        [shape(Q, 16, 8, 128), shape(Q, 8, 128), shape(10, 8, 128), shape(10, 8, 128)],
        [VMEM] * 4,
        scratch=[pltpu.VMEM((2, 512, 128), F32)],
        aliases={0: 0, 1: 1},
    )(main, edge, ahead, back)
    x_ahead, x_back = loop_exchange(x_ahead, x_back, "gx")
    flat, inner_edge = call(
        two_steps,
        [shape(FLAT_ROWS, 128), shape(Q, 8, 128)],
        [VMEM],
        scratch=[pltpu.VMEM((Q, 14, 8, 128), F32)],
    )(main)
    side = call(first_side, [shape(Q, 8, 128)], [VMEM] * 2)(edge, x_ahead)[0]
    flat, z_low, z_high = call(
        patch_two_steps,
        [shape(FLAT_ROWS, 128), shape(NEAR + FAR, 8, 128), shape(NEAR + FAR, 8, 128)],
        [VMEM] * 5,
        aliases={0: 0},
    )(flat, inner_edge, edge, side, x_back)
    below, above = ring_exchange(z_low, z_high, "gz")
    out, block_density, _ = call(
        last_two_steps,
        [shape(Q, 4, 8, 128), shape(1, 2), shape(FLAT_ROWS, 128)],
        [VMEM] * 3 + [HBM],
        [HBM, HBM, VMEM],
        scratch=[
            pltpu.VMEM((Q, 10, 8, 128), F32),
            pltpu.VMEM((Q, 64, 128), F32),
            pltpu.VMEM((2, Q, 8, 128), F32),
            pltpu.VMEM((Q, 8, 128), F32),
            pltpu.VMEM((Q, 4, 8, 128), F32),
            pltpu.VMEM((1, 2), jnp.int32),
            pltpu.VMEM((1, 2), F32),
            pltpu.SemaphoreType.DMA((6,)),
        ],
        aliases={0: 2},
    )(flat, below, above, in_hbm(block_fluid.transpose(1, 2, 0).reshape(1, 2)))
    return out, block_density.reshape(1, 1, 2).transpose(2, 0, 1)


def solution(mesh):
    return jax.shard_map(
        on_device,
        mesh=mesh,
        in_specs=(
            P(None, "gz", "gy", "gx"),
            P("gz", "gy", "gx"),
            P("gz", "gy", "gx"),
            P("gz", "gy", "gx"),
        ),
        out_specs=(P(None, "gz", "gy", "gx"), P("gz", "gy", "gx")),
        check_vma=False,
    )
```
